256 devices in a mesh: dp: 16 (over x_lo, y, core), mp: 16 (over z, x_hi).
Axes of the slice: x: 4 (x_hi: 2, x_lo: 2; x = x_hi * 2 + x_lo), y: 4, z: 8, core: 2. Of those that a mesh axis runs over, the one named last changes fastest.
Arguments:
- image_feats: bfloat16 [8192, 1152], P('dp'), may hold values from -10 to 10
- text_feats: bfloat16 [8192, 1152], P(('dp', 'mp')), may hold values from -10 to 10
- w_in: bfloat16 [1152, 4096], P(None, 'mp'), may hold values from -0.1875 to 0.1875
- w_out: bfloat16 [4096, 1152], P('mp'), may hold values from -0.09375 to 0.09375
- image_bucket: int32 [8192], P('dp'), may hold values from 0 to 7
- text_bucket: int32 [8192], P(('dp', 'mp')), may hold values from 0 to 7
- positive: int32 [8192], P('dp'), may hold values from 0 to 8191, each once
- reward_table: float32 [8, 8], replicated, may hold values from 0.05 to 80
Outputs:
- pair_loss: float32 [], replicated
- grad_text: float32 [8192, 1152], P(('dp', 'mp'))
- grad_image: float32 [8192, 1152], P(('dp', 'mp'))
- grad_w_in: float32 [1152, 4096], P(None, 'mp')
- grad_w_out: float32 [4096, 1152], P('mp')
The draws below stay inside these ranges and needn't reach their ends.
Inputs may be any that keep to these rules, and one draw needn't show every extreme that they name: `positive`: every caption is the match of exactly one image.
All inputs are finite; a program needn't handle non-finite values.
Results may differ from the reference program's by a relative error of at most 0.0029.
Values may be sent and summed in bfloat16 or wider, within the bound.
A program may use at most 64 MiB of HBM per device.

```python
import jax
import jax.numpy as jnp
from jax import lax

D = 1152
FF = 4096
NB = 8
B_DEV = 512
TOTAL = 8192
N_DP = 16


cluster_count = 64


def cluster_centers(key):
    return jnp.clip(jax.random.normal(key, (cluster_count, D), jnp.float32), -3.0, 3.0)


def cluster_rows(key, centers, amp_low, amp_high, noise_rows):
    labels = jax.random.randint(jax.random.fold_in(key, 1), (TOTAL,), 0, cluster_count)
    amplitude = jax.random.uniform(jax.random.fold_in(key, 2), (TOTAL, 1), jnp.float32, amp_low, amp_high)
    return (amplitude * centers[labels] + noise_rows).astype(jnp.bfloat16)


def noise_field(key):
    return jnp.clip(jax.random.normal(jax.random.fold_in(key, 3), (TOTAL, D), jnp.float32), -4.0, 4.0)


def draw_image_feats(key, part):
    centers = cluster_centers(key)
    key = jax.random.fold_in(key, 11)
    return cluster_rows(key, centers, 1.5, 1.5, noise_field(key))


def draw_text_feats(key, part):
    centers = cluster_centers(key)
    key = jax.random.fold_in(key, 23)
    return cluster_rows(key, centers, 1.5, 1.5, noise_field(key))


def jitter_levels(key, levels):
    jitter = jax.random.randint(key, (TOTAL,), -1, 2)
    return jnp.clip(levels + jitter, 0, NB - 1).astype(jnp.int32)


def draw_image_bucket(key, part):
    key = jax.random.fold_in(key, 37)
    rows = jnp.arange(TOTAL, dtype=jnp.int32)
    return jitter_levels(key, rows * NB // TOTAL)


def draw_text_bucket(key, part):
    key = jax.random.fold_in(key, 41)
    rows = jnp.arange(TOTAL, dtype=jnp.int32)
    return jitter_levels(key, rows % B_DEV * NB // B_DEV)


def growth_table(key, rate, offset):
    levels = jnp.arange(NB, dtype=jnp.float32)
    spread = jax.random.uniform(key, (NB, NB), jnp.float32, jnp.log(0.7), jnp.log(1.4))
    return jnp.exp(rate * (levels[:, None] + levels[None, :]) - offset + spread)


def draw_reward_table(key, part):
    key = jax.random.fold_in(key, 53)
    return growth_table(key, 0.3, 1.9)


def level_of(own_key, dims, cuts, low, largest):
    level, own = 1.0, jax.random.fold_in(own_key, 6)
    for position, blocks in cuts:
        steps = jnp.exp(jax.random.uniform(jax.random.fold_in(own, position), (blocks,), jnp.float32, low / len(cuts), largest / len(cuts)))
        level = level * jnp.repeat(steps, dims[position] // blocks).reshape([-1 if axis == position else 1 for axis in range(len(dims))])
    return level


def gaussian(stream_key, shape, width, limit, shards=(), held_as=jnp.bfloat16):
    loudness = level_of(stream_key, shape, shards, -0.22, 0.18) if shards else 1.0
    drawn = jax.random.normal(stream_key, shape, jnp.float32) * width * loudness
    return jnp.minimum(jnp.maximum(drawn, -limit), limit).astype(held_as)


def setup_inputs(seed: int = 0) -> dict:
    seeds = jax.random.split(jax.random.key(seed), 9)
    image_feats = draw_image_feats(jax.random.fold_in(seeds[8], 71), 0)
    text_feats = draw_text_feats(jax.random.fold_in(seeds[8], 71), 0)
    w_in = gaussian(seeds[2], (D, FF), D ** -0.5, 0.1875, ((1, 16),))
    w_out = gaussian(seeds[3], (FF, D), FF ** -0.5, 0.09375, ((0, 16),))
    image_bucket = draw_image_bucket(jax.random.fold_in(seeds[8], 71), 0)
    text_bucket = draw_text_bucket(jax.random.fold_in(seeds[8], 71), 0)
    positive = jax.random.permutation(seeds[6], TOTAL).astype(jnp.int32)
    reward_table = draw_reward_table(jax.random.fold_in(seeds[8], 71), 0)
    return {"image_feats": image_feats, "text_feats": text_feats, "w_in": w_in, "w_out": w_out, "image_bucket": image_bucket, "text_bucket": text_bucket, "positive": positive, "reward_table": reward_table}


logit_scale = 4.0
logit_bias = -2.0
norm_eps = 1e-06
root_coef = 0.7978845608028654
cubic_coef = 0.044715

def gelu_tanh(values):
    return 0.5 * values * (1.0 + jnp.tanh(root_coef * (values + cubic_coef * values * values * values)))

def gelu_slope(values):
    tangent = jnp.tanh(root_coef * (values + cubic_coef * values * values * values))
    return 0.5 * (1.0 + tangent) + 0.5 * values * (1.0 - tangent * tangent) * root_coef * (1.0 + 3.0 * cubic_coef * values * values)

def row_norm(values):
    return jnp.sqrt(lax.optimization_barrier(jnp.sum(values * values, axis=-1, keepdims=True)) + norm_eps)

def reference(image_feats, text_feats, w_in, w_out, image_bucket, text_bucket, positive, reward_table):
    hidden_pre = jnp.dot(image_feats, w_in, preferred_element_type=jnp.float32)
    activation = gelu_tanh(hidden_pre).astype(jnp.bfloat16)
    branch = jnp.dot(activation, w_out, preferred_element_type=jnp.float32)
    features = image_feats.astype(jnp.float32) + branch
    image_norm = row_norm(features)
    image_unit = features / image_norm
    image_emb = image_unit.astype(jnp.bfloat16)
    text_wide = text_feats.astype(jnp.float32)
    text_emb = (text_wide / row_norm(text_wide)).astype(jnp.bfloat16)
    text_index = jnp.arange(TOTAL, dtype=jnp.int32)

    def block_pass(state_now, pieces):
        loss_sum, text_grad = state_now
        image_rows, bucket_rows, positive_rows = pieces
        logits = logit_scale * jnp.dot(image_rows, text_emb.T, preferred_element_type=jnp.float32) + logit_bias
        signed = jnp.where(positive_rows[:, None] == text_index[None, :], 1.0, -1.0)
        weight = reward_table[bucket_rows[:, None], text_bucket[None, :]]
        margin = signed * logits
        loss_sum = loss_sum + jnp.sum(weight * jax.nn.softplus(-margin))
        coefficient = (-logit_scale * weight * signed * jax.nn.sigmoid(-margin)).astype(jnp.bfloat16)
        image_grad = jnp.dot(coefficient, text_emb, preferred_element_type=jnp.float32)
        text_grad = text_grad + jnp.dot(coefficient.T, image_rows, preferred_element_type=jnp.float32)
        return ((loss_sum, text_grad), image_grad)
    start_state = (jnp.zeros((), jnp.float32), jnp.zeros((TOTAL, D), jnp.float32))
    pieces = (image_emb.reshape(N_DP, B_DEV, D), image_bucket.reshape(N_DP, B_DEV), positive.reshape(N_DP, B_DEV))
    (loss_sum, grad_text), image_grads = lax.scan(block_pass, start_state, pieces)
    image_grad = image_grads.reshape(TOTAL, D)
    projected = lax.optimization_barrier(jnp.sum(image_unit * image_grad, axis=-1, keepdims=True))
    grad_features = (image_grad - image_unit * projected) / image_norm
    grad_feat_b = grad_features.astype(jnp.bfloat16)
    grad_act = jnp.dot(grad_feat_b, w_out.T, preferred_element_type=jnp.float32)
    grad_hidden = (grad_act * gelu_slope(hidden_pre)).astype(jnp.bfloat16)
    grad_image = grad_features + jnp.dot(grad_hidden, w_in.T, preferred_element_type=jnp.float32)
    grad_w_in = jnp.dot(image_feats.T, grad_hidden, preferred_element_type=jnp.float32)
    grad_w_out = jnp.dot(activation.T, grad_feat_b, preferred_element_type=jnp.float32)
    pair_loss = loss_sum / (TOTAL * TOTAL)
    return (pair_loss, grad_text, grad_image, grad_w_in, grad_w_out)
```

```python
import jax
import jax.numpy as jnp
from jax import lax
from jax.experimental import pallas as pl
from jax.experimental.pallas import tpu as pltpu
from jax.sharding import PartitionSpec as P

MESH = pl.DeviceIdType.MESH
F32 = jnp.float32
BF16 = jnp.bfloat16

logit_scale = 4.0
logit_bias = -2.0
norm_eps = 1e-06
root_coef = 0.7978845608028654
cubic_coef = 0.044715

D = 1152
ROWS = 512
OWN = 32
HID = 256
PAIRS = 8192.0 * 8192.0
ext = 128
VMEM_LIMIT = 50 * 2**20

NT = (((1,), (1,)), ((), ()))
TN = (((0,), (0,)), ((), ()))


def dot(a, b):
    return jnp.dot(a, b, preferred_element_type=F32)


def dot_nt(a, b):
    return lax.dot_general(a, b, NT, preferred_element_type=F32)


def dot_tn(a, b):
    return lax.dot_general(a, b, TN, preferred_element_type=F32)


def gelu_tanh(v):
    return 0.5 * v * (1.0 + jnp.tanh(root_coef * (v + cubic_coef * v * v * v)))


def gelu_slope(v):
    t = jnp.tanh(root_coef * (v + cubic_coef * v * v * v))
    return 0.5 * (1.0 + t) + 0.5 * v * (1.0 - t * t) * root_coef * (1.0 + 3.0 * cubic_coef * v * v)


def row_norm(v):
    return jnp.sqrt(jnp.sum(v * v, axis=-1, keepdims=True) + norm_eps)


(TEXT, META, RS1, AG1C, RS2C, RS2Z, TG, LOSS1, LOSSC, LOSSZ, AG2, RS3, ARC_I, ARC_O, ARS_I, ARS_O, AAG_I, AAG_O,
 AFC_I, AFC_O, AG1Z) = range(21)


def rows_at(start, count, step):
    return pl.ds(pl.multiple_of(start, step), count)


def kernel(
    x_ref, t_ref, wi_ref, wo_ref, ib_ref, tb_ref, pos_ref, tab_ref,
    loss_ref, gt_ref, gi_ref, gwi_ref, gwo_ref,
    hp, act, rs1s, rs1r, txt, meta, hot, img, coef, loss_acc, c_send, c_recv, ig, rs2s, rs2r, tgs, tgr,
    l_tile, l1r, lc_tile, lcr, lz_tile, lzr, gfall, gh, rs3s, rs3r,
    arc_si, arc_so, arc_ri, arc_ro, awi, awo, ars_si, ars_so, ars_ri, ars_ro, fwi, fwo,
    ssem, rsem, zsem,
):
    dp, mp = lax.axis_index("dp"), lax.axis_index("mp")
    core, y, xl = lax.rem(dp, 2), lax.rem(dp // 2, 4), dp // 8
    xh, z = lax.rem(mp, 2), mp // 2
    x = xh * 2 + xl
    partner = (dp + 1 - 2 * core, mp)

    def mp_peer(j):
        return (dp, lax.rem(mp + j, 16))

    def z_peer(j):
        return (dp, lax.rem(z + j, 8) * 2 + xh)

    def plane_dev(x2, y2):
        return ((lax.rem(x2, 2) * 4 + y2) * 2 + core, z * 2 + x2 // 2)

    def ar_peer(j):
        xl2, y2 = lax.rem(xl + lax.rem(j, 2), 2), lax.rem(y + j // 2, 4)
        return ((xl2 * 4 + y2) * 2 + core, mp), y2 * 2 + xl2

    def plane_peer(j):
        return plane_dev(lax.rem(x + lax.rem(j, 4), 4), lax.rem(y + j // 4, 4))

    def copy(src, dst, phase, device, recv=None):
        return pltpu.make_async_remote_copy(
            src_ref=src, dst_ref=dst, send_sem=ssem.at[phase],
            recv_sem=rsem.at[phase] if recv is None else recv, device_id=device, device_id_type=MESH,
        )

    def got(ref, phase):
        copy(ref, ref, phase, partner).wait_recv()

    def sent(ref, phase):
        copy(ref, ref, phase, partner).wait_send()

    barrier = pltpu.get_barrier_semaphore()

    def greet(j, _):
        pl.semaphore_signal(barrier, inc=1, device_id=mp_peer(j), device_id_type=MESH)
        pl.semaphore_signal(barrier, inc=1, device_id=plane_peer(j), device_id_type=MESH)
        return 0

    lax.fori_loop(1, 16, greet, 0)
    pl.semaphore_signal(barrier, inc=1, device_id=partner, device_id_type=MESH)

    own_slot = y * 4 + x
    own_text = rows_at(own_slot * OWN, OWN, OWN)
    wide = t_ref[...].astype(F32)
    txt[own_text, :D] = (wide / row_norm(wide)).astype(BF16)
    eye = lax.broadcasted_iota(jnp.int32, (OWN, OWN), 0) == lax.broadcasted_iota(jnp.int32, (OWN, OWN), 1)
    tb_col = jnp.sum(jnp.where(eye, tb_ref[...].astype(F32), 0.0), axis=1, keepdims=True)
    lane = lax.broadcasted_iota(jnp.int32, (OWN, ext), 1)
    level = jnp.where(lane < 24, lax.rem(lane, 8), -1).astype(F32)
    txt[own_text, D:] = jnp.where(level == tb_col, 1.0, 0.0).astype(BF16)

    pos = pos_ref[...]
    pos_hi = pos // 64
    line = lax.broadcasted_iota(jnp.int32, (8, ROWS), 0)
    table_rows = jnp.where(
        line == 0, pos_hi, jnp.where(line == 1, pos - pos_hi * 64, jnp.where(line == 2, ib_ref[...], 0))
    ).astype(F32).astype(BF16)
    took = lax.broadcasted_iota(jnp.int32, (ROWS, 256), 0)
    into = lax.broadcasted_iota(jnp.int32, (ROWS, 256), 1)
    pick = jnp.where(took == (into // 32) * 64 + xh * 32 + lax.rem(into, 32), 1.0, 0.0).astype(BF16)
    meta[core] = dot(table_rows, pick)

    pl.semaphore_wait(barrier, 31)

    def send_text(j, _):
        copy(txt.at[own_text], txt.at[own_text], TEXT, plane_peer(j)).start()
        return 0

    lax.fori_loop(1, 16, send_text, 0)
    copy(meta.at[core], meta.at[core], META, partner).start()

    def forward(t, _):
        b = lax.rem(mp // 4 + 1 + t, 4)
        rows = rows_at(b * 128, 128, 128)
        pre = dot(x_ref[rows, :], wi_ref[...])
        hp[rows, :] = pre
        a = gelu_tanh(pre).astype(BF16)
        act[rows, :] = a
        rs1s[rows, :] = dot(a, wo_ref[...]).astype(BF16)

        def send(i, _):
            k = b * 4 + i
            j = lax.rem(k - mp + 16, 16)

            @pl.when(j != 0)
            def _():
                copy(
                    rs1s.at[rows_at(k * OWN, OWN, OWN)], rs1r.at[rows_at((j - 1) * OWN, OWN, OWN)], RS1, (dp, k)
                ).start()

            return 0

        lax.fori_loop(0, 4, send, 0)
        return 0

    lax.fori_loop(0, 4, forward, 0)
    own_rows = rows_at(mp * OWN, OWN, OWN)
    features = x_ref[own_rows, :].astype(F32) + dot(act[own_rows, :], wo_ref[...])
    got(rs1r, RS1)

    def add_rs1(j, total):
        return total + rs1r[rows_at(j * OWN, OWN, OWN), :].astype(F32)

    features = lax.fori_loop(0, 15, add_rs1, features)
    norm = row_norm(features)
    unit = features / norm

    own_img = rows_at((core * 8 + z) * OWN, OWN, OWN)
    img[own_img, :] = unit.astype(BF16)

    def send_img(j, _):
        copy(img.at[own_img], img.at[own_img], AG1Z, z_peer(j), zsem.at[j - 1]).start()
        return 0

    lax.fori_loop(1, 8, send_img, 0)
    copy(img.at[own_img], img.at[own_img], AG1C, partner).start()

    got(meta.at[1 - core], META)

    def table_of(half):
        m = meta[half]
        bucket = m[2:3, :]
        w = jnp.zeros((8, 256), F32)
        for k in range(8):
            w = w + jnp.where(bucket == float(k), tab_ref[:, k : k + 1], 0.0)
        hi = w.astype(BF16).astype(F32)
        mid = (w - hi).astype(BF16).astype(F32)
        low = w - hi - mid
        return jnp.concatenate([hi, mid, low, jnp.zeros((ext - 24, 256), F32)], axis=0).astype(BF16)

    hot[0] = table_of(core)
    hot[1] = table_of(1 - core)
    match = [m[0:1, :] * 64.0 + m[1:2, :] for m in (meta[core], meta[1 - core])]
    got(txt.at[pl.ds(0, 15 * OWN)], TEXT)

    def forward_img(j, _):
        slot = rows_at((core * 8 + lax.rem(z - j + 8, 8)) * OWN, OWN, OWN)
        copy(img.at[slot], img.at[slot], AG1Z, partner, zsem.at[j - 1]).wait_recv()
        copy(img.at[slot], img.at[slot], AG1C, partner).start()
        return 0

    lax.fori_loop(1, 8, forward_img, 0)

    loss_acc[...] = jnp.zeros_like(loss_acc)

    def pairs(half):
        images = rows_at((core if half == 0 else 1 - core) * 256, 256, 256)

        def step(b, _):
            rows = rows_at(b * 128, 128, 128)
            logits = logit_scale * dot_nt(txt[rows, :D], img[images, :]) + logit_bias
            weight = dot(txt[rows, D:], hot[half])
            slot = b * 128 + lax.broadcasted_iota(jnp.int32, (128, 256), 0)
            p = slot // OWN
            px, py = lax.rem(p, 4), p // 4
            index = (((lax.rem(px, 2) * 4 + py) * 2 + core) * 16 + z * 2 + px // 2) * OWN + lax.rem(slot, OWN)
            hit = index.astype(F32) == match[half]
            against = jnp.where(hit, -logits, logits)
            grown = jnp.exp(against)
            loss_acc[...] += weight * jnp.log(1.0 + grown)
            slope = logit_scale * weight * (grown / (1.0 + grown))
            coef[half, rows, :] = jnp.where(hit, -slope, slope).astype(BF16)
            return 0

        lax.fori_loop(0, 4, step, 0)

    pairs(0)
    got(img.at[pl.ds(0, 8 * OWN)], AG1C)
    pairs(1)

    for b in range(2):
        rows = pl.ds(b * 128, 128)
        c_send[rows, :] = dot_tn(coef[1, :, b * 128 : b * 128 + 128], txt[:, :D]).astype(BF16)
        copy(c_send.at[rows], c_recv.at[rows], RS2C, partner).start()
    for b in range(2):
        rows = pl.ds(b * 128, 128)
        ig[rows, :] = dot_tn(coef[0, :, b * 128 : b * 128 + 128], txt[:, :D])
    got(c_recv, RS2C)

    def send_rs2(j, _):
        rows = rows_at(lax.rem(z + j, 8) * OWN, OWN, OWN)
        rs2s[rows, :] = (ig[rows, :] + c_recv[rows, :].astype(F32)).astype(BF16)
        copy(rs2s.at[rows], rs2r.at[rows_at((j - 1) * OWN, OWN, OWN)], RS2Z, z_peer(j)).start()
        return 0

    lax.fori_loop(1, 8, send_rs2, 0)

    own_half, other_half = rows_at(core * 256, 256, 256), rows_at((1 - core) * 256, 256, 256)

    def text_grad(t, _):
        b = lax.rem(y + 1 + t, 4)
        rows = rows_at(b * 128, 128, 128)
        tgs[rows, :] = (dot(coef[0, rows, :], img[own_half, :]) + dot(coef[1, rows, :], img[other_half, :])).astype(BF16)

        def send(i, _):
            j = lax.rem(b - y + 4, 4) * 4 + lax.rem(i - x + 4, 4)

            @pl.when(j != 0)
            def _():
                copy(
                    tgs.at[rows_at((b * 4 + i) * OWN, OWN, OWN)], tgr.at[rows_at((j - 1) * OWN, OWN, OWN)], TG,
                    plane_dev(i, b),
                ).start()

            return 0

        lax.fori_loop(0, 4, send, 0)
        return 0

    lax.fori_loop(0, 4, text_grad, 0)
    l_tile[...] = jnp.zeros((8, 128), F32) + jnp.sum(loss_acc[...])

    def send_loss(j, _):
        copy(l_tile, l1r.at[rows_at((j - 1) * 8, 8, 8)], LOSS1, plane_peer(j)).start()
        return 0

    lax.fori_loop(1, 16, send_loss, 0)
    grad_text = dot(coef[0, own_text, :], img[own_half, :]) + dot(coef[1, own_text, :], img[other_half, :])

    own_z = rows_at(z * OWN, OWN, OWN)
    own_grad = ig[own_z, :] + c_recv[own_z, :].astype(F32)
    got(rs2r, RS2Z)

    def add_rs2(j, total):
        return total + rs2r[rows_at(j * OWN, OWN, OWN), :].astype(F32)

    own_grad = lax.fori_loop(0, 7, add_rs2, own_grad)
    projected = jnp.sum(unit * own_grad, axis=-1, keepdims=True)
    grad_features = (own_grad - unit * projected) / norm
    gfall[own_rows, :] = grad_features.astype(BF16)

    def send_gf(j, _):
        copy(gfall.at[own_rows], gfall.at[own_rows], AG2, mp_peer(j)).start()
        return 0

    lax.fori_loop(1, 16, send_gf, 0)

    got(l1r, LOSS1)
    loss = l_tile[...]
    for j in range(15):
        loss = loss + l1r[j * 8 : j * 8 + 8, :]
    lc_tile[...] = loss
    copy(lc_tile, lcr, LOSSC, partner).start()
    got(tgr, TG)

    def add_tg(j, total):
        return total + tgr[rows_at(j * OWN, OWN, OWN), :].astype(F32)

    gt_ref[...] = lax.fori_loop(0, 15, add_tg, grad_text)
    got(lcr, LOSSC)
    lz_tile[...] = loss + lcr[...]

    def send_loss_z(j, _):
        copy(lz_tile, lzr.at[rows_at((j - 1) * 8, 8, 8)], LOSSZ, z_peer(j)).start()
        return 0

    lax.fori_loop(1, 8, send_loss_z, 0)
    got(gfall.at[pl.ds(0, 15 * OWN)], AG2)

    def backward(t, _):
        b = lax.rem(mp // 4 + 1 + t, 4)
        rows = rows_at(b * 128, 128, 128)
        g = (dot_nt(gfall[rows, :], wo_ref[...]) * gelu_slope(hp[rows, :])).astype(BF16)
        gh[rows, :] = g
        rs3s[rows, :] = dot_nt(g, wi_ref[...]).astype(BF16)

        def send(i, _):
            k = b * 4 + i
            j = lax.rem(k - mp + 16, 16)

            @pl.when(j != 0)
            def _():
                copy(
                    rs3s.at[rows_at(k * OWN, OWN, OWN)], rs3r.at[rows_at((j - 1) * OWN, OWN, OWN)], RS3, (dp, k)
                ).start()

            return 0

        lax.fori_loop(0, 4, send, 0)
        return 0

    lax.fori_loop(0, 4, backward, 0)

    other_cols, own_cols = rows_at((1 - core) * 128, 128, 128), rows_at(core * 128, 128, 128)

    def w_in_half(cols, out, kind):
        def step(b, _):
            part = rows_at(b * 128, 128, 128)
            out[part, :] = dot_tn(x_ref[:, part], gh[:, cols]).astype(kind)
            return 0

        lax.fori_loop(0, 9, step, 0)

    arc_so[...] = dot_tn(act[:, other_cols], gfall[...]).astype(BF16)
    copy(arc_so, arc_ro, ARC_O, partner).start()
    w_in_half(other_cols, arc_si, BF16)
    copy(arc_si, arc_ri, ARC_I, partner).start()
    awo[...] = dot_tn(act[:, own_cols], gfall[...])
    w_in_half(own_cols, awi, F32)
    got(arc_ro, ARC_O)
    awo[...] += arc_ro[...].astype(F32)
    ars_so[...] = awo[...].astype(BF16)
    got(arc_ri, ARC_I)
    awi[...] += arc_ri[...].astype(F32)
    ars_si[...] = awi[...].astype(BF16)

    def send_ars(j, _):
        device, q = ar_peer(j)
        copy(ars_si.at[rows_at(q * 144, 144, 144)], ars_ri.at[rows_at((j - 1) * 144, 144, 144)], ARS_I, device).start()
        copy(ars_so.at[rows_at(q * 16, 16, 16)], ars_ro.at[rows_at((j - 1) * 16, 16, 16)], ARS_O, device).start()
        return 0

    lax.fori_loop(1, 8, send_ars, 0)
    q = y * 2 + xl
    own_in, own_out = rows_at(q * 144, 144, 144), rows_at(q * 16, 16, 16)
    total_in, total_out = awi[own_in, :], awo[own_out, :]
    got(ars_ri, ARS_I)
    for j in range(7):
        total_in = total_in + ars_ri[j * 144 : j * 144 + 144, :].astype(F32)
    got(ars_ro, ARS_O)
    for j in range(7):
        total_out = total_out + ars_ro[j * 16 : j * 16 + 16, :].astype(F32)
    fwi[core, own_in, :] = total_in.astype(BF16)
    fwo[core, own_out, :] = total_out.astype(BF16)

    def send_aag(j, _):
        device, _ = ar_peer(j)
        copy(fwi.at[core, own_in], fwi.at[core, own_in], AAG_I, device).start()
        copy(fwo.at[core, own_out], fwo.at[core, own_out], AAG_O, device).start()
        return 0

    lax.fori_loop(1, 8, send_aag, 0)

    got(lzr, LOSSZ)
    loss = lz_tile[...]
    for j in range(7):
        loss = loss + lzr[j * 8 : j * 8 + 8, :]
    loss_ref[...] = loss * (1.0 / PAIRS)
    grad_image = grad_features + dot_nt(gh[own_rows, :], wi_ref[...])

    got(fwi.at[core, pl.ds(0, 7 * 144)], AAG_I)
    copy(fwi.at[core], fwi.at[core], AFC_I, partner).start()
    got(fwo.at[core, pl.ds(0, 7 * 16)], AAG_O)
    copy(fwo.at[core], fwo.at[core], AFC_O, partner).start()
    got(rs3r, RS3)

    def add_rs3(j, total):
        return total + rs3r[rows_at(j * OWN, OWN, OWN), :].astype(F32)

    gi_ref[...] = lax.fori_loop(0, 15, add_rs3, grad_image)
    got(fwi.at[1 - core], AFC_I)
    for half in range(2):
        gwi_ref[:, half * 128 : half * 128 + 128] = fwi[half]
    got(fwo.at[1 - core], AFC_O)
    for half in range(2):
        gwo_ref[half * 128 : half * 128 + 128, :] = fwo[half]

    sent(txt.at[pl.ds(0, 15 * OWN)], TEXT)
    sent(meta.at[0], META)
    sent(rs1r, RS1)
    sent(img.at[pl.ds(0, 7 * OWN)], AG1Z)
    sent(img.at[pl.ds(0, 8 * OWN)], AG1C)
    sent(c_send, RS2C)
    sent(rs2r, RS2Z)
    sent(tgr, TG)
    sent(l1r, LOSS1)
    sent(lc_tile, LOSSC)
    sent(lzr, LOSSZ)
    sent(gfall.at[pl.ds(0, 15 * OWN)], AG2)
    sent(rs3r, RS3)
    sent(arc_si, ARC_I)
    sent(arc_so, ARC_O)
    sent(ars_ri, ARS_I)
    sent(ars_ro, ARS_O)
    sent(fwi.at[0, pl.ds(0, 7 * 144)], AAG_I)
    sent(fwo.at[0, pl.ds(0, 7 * 16)], AAG_O)
    sent(fwi.at[0], AFC_I)
    sent(fwo.at[0], AFC_O)


def per_device(
    image_feats, text_feats, w_in, w_out, image_bucket, text_bucket, positive, reward_table
):
    vmem = pl.BlockSpec(memory_space=pltpu.VMEM)

    def buf(shape, kind=BF16):
        return pltpu.VMEM(shape, kind)

    scratch = [
        buf((ROWS, HID), F32),
        buf((ROWS, HID)),
        buf((ROWS, D)),
        buf((15 * OWN, D)),
        buf((ROWS, D + ext)),
        buf((2, 8, 256), F32),
        buf((2, ext, 256)),
        buf((ROWS, D)),
        buf((2, ROWS, 256)),
        buf((128, 256), F32),
        buf((256, D)),
        buf((256, D)),
        buf((256, D), F32),
        buf((256, D)),
        buf((7 * OWN, D)),
        buf((ROWS, D)),
        buf((15 * OWN, D)),
        buf((8, 128), F32),
        buf((15 * 8, 128), F32),
        buf((8, 128), F32),
        buf((8, 128), F32),
        buf((8, 128), F32),
        buf((7 * 8, 128), F32),
        buf((ROWS, D)),
        buf((ROWS, HID)),
        buf((ROWS, D)),
        buf((15 * OWN, D)),
        buf((D, 128)),
        buf((128, D)),
        buf((D, 128)),
        buf((128, D)),
        buf((D, 128), F32),
        buf((128, D), F32),
        buf((D, 128)),
        buf((128, D)),
        buf((7 * 144, 128)),
        buf((7 * 16, D)),
        buf((2, D, 128)),
        buf((2, 128, D)),
        pltpu.SemaphoreType.DMA((21,)),
        pltpu.SemaphoreType.DMA((21,)),
        pltpu.SemaphoreType.DMA((7,)),
    ]
    loss, grad_text, grad_image, grad_w_in, grad_w_out = pl.pallas_call(
        kernel,
        out_shape=(
            jax.ShapeDtypeStruct((8, 128), F32),
            jax.ShapeDtypeStruct((OWN, D), F32),
            jax.ShapeDtypeStruct((OWN, D), F32),
            jax.ShapeDtypeStruct((D, HID), BF16),
            jax.ShapeDtypeStruct((HID, D), BF16),
        ),
        in_specs=[vmem] * 8,
        out_specs=(vmem,) * 5,
        scratch_shapes=scratch,
        compiler_params=pltpu.CompilerParams(
            collective_id=0, has_side_effects=True, vmem_limit_bytes=VMEM_LIMIT
        ),
        name="pairs_and_block",
    )(
        image_feats, text_feats, w_in, w_out, image_bucket[None, :], text_bucket[None, :], positive[None, :],
        reward_table.T,
    )
    return (loss[0, 0], grad_text, grad_image, grad_w_in.astype(F32), grad_w_out.astype(F32))


def solution(mesh):
    return jax.shard_map(
        per_device,
        mesh=mesh,
        in_specs=(
            P("dp", None),
            P(("dp", "mp"), None),
            P(None, "mp"),
            P("mp", None),
            P("dp"),
            P(("dp", "mp")),
            P("dp"),
            P(),
        ),
        out_specs=(P(), P(("dp", "mp"), None), P(("dp", "mp"), None), P(None, "mp"), P("mp", None)),
        check_vma=False,
    )
```

```python
import jax
import jax.numpy as jnp
from jax import lax
from jax.experimental import pallas as pl
from jax.experimental.pallas import tpu as pltpu
from jax.sharding import PartitionSpec as P

MESH = pl.DeviceIdType.MESH
F32 = jnp.float32
BF16 = jnp.bfloat16

logit_scale = 4.0
logit_bias = -2.0
norm_eps = 1e-06
root_coef = 0.7978845608028654
cubic_coef = 0.044715

D = 1152
ROWS = 512
OWN = 32
HID = 256
PAIRS = 8192.0 * 8192.0
ext = 128
VMEM_LIMIT = 50 * 2**20

NT = (((1,), (1,)), ((), ()))
TN = (((0,), (0,)), ((), ()))


def dot(a, b):
    return jnp.dot(a, b, preferred_element_type=F32)


def dot_nt(a, b):
    return lax.dot_general(a, b, NT, preferred_element_type=F32)


def dot_tn(a, b):
    return lax.dot_general(a, b, TN, preferred_element_type=F32)


def gelu_tanh(v):
    return 0.5 * v * (1.0 + jnp.tanh(root_coef * (v + cubic_coef * v * v * v)))


def gelu_slope(v):
    t = jnp.tanh(root_coef * (v + cubic_coef * v * v * v))
    return 0.5 * (1.0 + t) + 0.5 * v * (1.0 - t * t) * root_coef * (1.0 + 3.0 * cubic_coef * v * v)


def row_norm(v):
    return jnp.sqrt(jnp.sum(v * v, axis=-1, keepdims=True) + norm_eps)


(TEXT, META, RS1, RS1X, AG1C, RS2C, RS2Z, TG, LOSS1, LOSSC, LOSSZ, AG2, AG2X, RS3, RS3X, ARC_I, ARC_O, ARS_I, ARS_O,
 AAG_I, AAG_O, AFC_I, AFC_O, AG1Z) = range(24)
FLOW = 16
UP, DOWN = 0, 1


def rows_at(start, count, step):
    return pl.ds(pl.multiple_of(start, step), count)


def kernel(
    x_hbm, t_hbm, wi_hbm, wo_hbm, ib_hbm, tb_hbm, pos_hbm, tab_hbm,
    loss_ref, gt_ref, gi_ref, gwi_ref, gwo_ref,
    x_ref, t_ref, wi_ref, wo_ref, ib_ref, tb_ref, pos_ref, tab_ref,
    hp, act, part, rs1s, rs1r, rs1xs, rs1xr, txt, meta, hot, img, coef, loss_acc, c_send, c_recv, ig, rs2s, rs2r, tgs, tgr,
    l_tile, l1r, lc_tile, lcr, lz_tile, lzr, gfall, gh, rs3s, rs3r, rs3xs, rs3xr,
    arc_si, arc_so, arc_ri, arc_ro, awi, awo, ars_si, ars_so, ars_ri, ars_ro, fwi, fwo,
    lsem, ssem, rsem, zsem, rs1sem, ag2sem, rs3sem,
):
    dp, mp = lax.axis_index("dp"), lax.axis_index("mp")
    core, y, xl = lax.rem(dp, 2), lax.rem(dp // 2, 4), dp // 8
    xh, z = lax.rem(mp, 2), mp // 2
    x = xh * 2 + xl
    partner = (dp + 1 - 2 * core, mp)

    across = (dp, mp + 1 - 2 * xh)

    def z_peer(j):
        return (dp, lax.rem(z + j, 8) * 2 + xh)

    def plane_dev(x2, y2):
        return ((lax.rem(x2, 2) * 4 + y2) * 2 + core, z * 2 + x2 // 2)

    def ar_peer(j):
        xl2, y2 = lax.rem(xl + lax.rem(j, 2), 2), lax.rem(y + j // 2, 4)
        return ((xl2 * 4 + y2) * 2 + core, mp), y2 * 2 + xl2

    def plane_peer(j):
        return plane_dev(lax.rem(x + lax.rem(j, 4), 4), lax.rem(y + j // 4, 4))

    def copy(src, dst, phase, device, recv=None):
        return pltpu.make_async_remote_copy(
            src_ref=src, dst_ref=dst, send_sem=ssem.at[phase],
            recv_sem=rsem.at[phase] if recv is None else recv, device_id=device, device_id_type=MESH,
        )

    def got(ref, phase):
        copy(ref, ref, phase, partner).wait_recv()

    def sent(ref, phase):
        copy(ref, ref, phase, partner).wait_send()

    barrier = pltpu.get_barrier_semaphore()

    def greet(j, _):
        pl.semaphore_signal(barrier, inc=1, device_id=plane_peer(j), device_id_type=MESH)
        return 0

    lax.fori_loop(1, 16, greet, 0)

    def greet_z(j, _):
        pl.semaphore_signal(barrier, inc=1, device_id=z_peer(j), device_id_type=MESH)
        return 0

    lax.fori_loop(1, 8, greet_z, 0)
    pl.semaphore_signal(barrier, inc=1, device_id=partner, device_id_type=MESH)

    loads = [
        pltpu.make_async_copy(src, dst, lsem.at[i])
        for i, (src, dst) in enumerate(
            (
                (t_hbm, t_ref), (tb_hbm, tb_ref), (pos_hbm, pos_ref), (ib_hbm, ib_ref), (tab_hbm, tab_ref),
                (x_hbm, x_ref), (wi_hbm, wi_ref), (wo_hbm, wo_ref),
            )
        )
    ]
    for load in loads:
        load.start()
    for load in loads[:5]:
        load.wait()

    own_slot = y * 4 + x
    own_text = rows_at(own_slot * OWN, OWN, OWN)
    wide = t_ref[...].astype(F32)
    txt[own_text, :D] = (wide / row_norm(wide)).astype(BF16)
    eye = lax.broadcasted_iota(jnp.int32, (OWN, OWN), 0) == lax.broadcasted_iota(jnp.int32, (OWN, OWN), 1)
    tb_col = jnp.sum(jnp.where(eye, tb_ref[...].astype(F32), 0.0), axis=1, keepdims=True)
    lane = lax.broadcasted_iota(jnp.int32, (OWN, ext), 1)
    level = jnp.where(lane < 24, lax.rem(lane, 8), -1).astype(F32)
    txt[own_text, D:] = jnp.where(level == tb_col, 1.0, 0.0).astype(BF16)

    pos = pos_ref[...]
    pos_hi = pos // 64
    line = lax.broadcasted_iota(jnp.int32, (8, ROWS), 0)
    table_rows = jnp.where(
        line == 0, pos_hi, jnp.where(line == 1, pos - pos_hi * 64, jnp.where(line == 2, ib_ref[...], 0))
    ).astype(F32).astype(BF16)
    took = lax.broadcasted_iota(jnp.int32, (ROWS, 256), 0)
    into = lax.broadcasted_iota(jnp.int32, (ROWS, 256), 1)
    pick = jnp.where(took == (into // 32) * 64 + xh * 32 + lax.rem(into, 32), 1.0, 0.0).astype(BF16)
    meta[core] = dot(table_rows, pick)

    pl.semaphore_wait(barrier, 23)

    def send_text(j, _):
        copy(txt.at[own_text], txt.at[own_text], TEXT, plane_peer(j)).start()
        return 0

    lax.fori_loop(1, 16, send_text, 0)
    copy(meta.at[core], meta.at[core], META, partner).start()

    def hops(f, way):
        return 4 if f % 2 == way else 3

    def slot_of(f, way, far, flows):
        return pl.ds(((way * flows + f) * 4 + far - 1) * FLOW, FLOW)

    def neighbour(way):
        return z_peer(1 if way == UP else 7)

    def toward(way, far):
        return lax.rem(z + (far if way == UP else 8 - far), 8)

    def reduce_step(far, flows, row_of, held, sbuf, rbuf, phase, sems):
        for f in range(flows):
            for way in (UP, DOWN):
                if far > hops(f, way):
                    continue
                value = held[rows_at(row_of(f, toward(way, far)), FLOW, FLOW), :]
                if far < hops(f, way):
                    before = slot_of(f, way, far + 1, flows)
                    sem = sems.at[(way * flows + f) * 4 + far]
                    copy(rbuf.at[before], rbuf.at[before], phase, partner, sem).wait_recv()
                    value = value + rbuf[before, :].astype(F32)
                slot = slot_of(f, way, far, flows)
                sbuf[slot, :] = value.astype(BF16)
                sem = sems.at[(way * flows + f) * 4 + far - 1]
                copy(sbuf.at[slot], rbuf.at[slot], phase, neighbour(way), sem).start()

    def reduce_end(f, flows, row_of, held, rbuf, phase, sems):
        value = held[rows_at(row_of(f, z), FLOW, FLOW), :]
        for way in (UP, DOWN):
            slot = slot_of(f, way, 1, flows)
            copy(rbuf.at[slot], rbuf.at[slot], phase, partner, sems.at[(way * flows + f) * 4]).wait_recv()
            value = value + rbuf[slot, :].astype(F32)
        return value

    def gather_step(far, flows, row_of, buf, phase, sems):
        for f in flows:
            for way in (UP, DOWN):
                if far > hops(f, way):
                    continue
                rows = rows_at(row_of(f, toward(1 - way, far - 1)), FLOW, FLOW)
                if far > 1:
                    sem = sems.at[(way * 4 + f) * 4 + far - 2]
                    copy(buf.at[rows], buf.at[rows], phase, partner, sem).wait_recv()
                sem = sems.at[(way * 4 + f) * 4 + far - 1]
                copy(buf.at[rows], buf.at[rows], phase, neighbour(way), sem).start()

    def gather_end(flows, row_of, buf, phase, sems):
        for f in flows:
            for way in (UP, DOWN):
                rows = rows_at(row_of(f, toward(1 - way, hops(f, way))), FLOW, FLOW)
                sem = sems.at[(way * 4 + f) * 4 + hops(f, way) - 1]
                copy(buf.at[rows], buf.at[rows], phase, partner, sem).wait_recv()

    def mp_row(f, z2):
        return (z2 * 2 + (1 - xh if f < 2 else xh)) * OWN + (f % 2) * FLOW

    for load in loads[5:]:
        load.wait()

    def forward(z2):
        rows = rows_at(z2 * 64, 64, 64)
        pre = dot(x_ref[rows, :], wi_ref[...])
        hp[rows, :] = pre
        a = gelu_tanh(pre).astype(BF16)
        act[rows, :] = a
        part[rows, :] = dot(a, wo_ref[...])

    forward(toward(UP, 4))
    for far in (4, 3, 2, 1):
        reduce_step(far, 4, mp_row, part, rs1s, rs1r, RS1, rs1sem)
        forward(toward(UP, far - 1))
        if far > 1:
            forward(toward(DOWN, far - 1))
    own_rows = rows_at(mp * OWN, OWN, OWN)
    for f in (0, 1):
        rs1xs[f * FLOW : f * FLOW + FLOW, :] = reduce_end(f, 4, mp_row, part, rs1r, RS1, rs1sem).astype(BF16)
    copy(rs1xs, rs1xr, RS1X, across).start()
    features = jnp.concatenate([reduce_end(f, 4, mp_row, part, rs1r, RS1, rs1sem) for f in (2, 3)], axis=0)
    features = features + x_ref[own_rows, :].astype(F32)
    got(rs1xr, RS1X)
    features = features + rs1xr[...].astype(F32)
    norm = row_norm(features)
    unit = features / norm

    own_img = rows_at((core * 8 + z) * OWN, OWN, OWN)
    img[own_img, :] = unit.astype(BF16)

    def send_img(j, _):
        copy(img.at[own_img], img.at[own_img], AG1Z, z_peer(j), zsem.at[j - 1]).start()
        return 0

    lax.fori_loop(1, 8, send_img, 0)
    copy(img.at[own_img], img.at[own_img], AG1C, partner).start()

    got(meta.at[1 - core], META)

    eye8 = lax.broadcasted_iota(jnp.int32, (8, 8), 0) == lax.broadcasted_iota(jnp.int32, (8, 8), 1)

    def table_of(half):
        m = meta[half]
        bucket = m[2:3, :]
        w = jnp.zeros((8, 256), F32)
        for k in range(8):
            column = jnp.sum(jnp.where(eye8, tab_ref[k : k + 1, :], 0.0), axis=1, keepdims=True)
            w = w + jnp.where(bucket == float(k), column, 0.0)
        hi = w.astype(BF16).astype(F32)
        mid = (w - hi).astype(BF16).astype(F32)
        low = w - hi - mid
        return jnp.concatenate([hi, mid, low, jnp.zeros((ext - 24, 256), F32)], axis=0).astype(BF16)

    hot[0] = table_of(core)
    hot[1] = table_of(1 - core)
    match = [m[0:1, :] * 64.0 + m[1:2, :] for m in (meta[core], meta[1 - core])]
    got(txt.at[pl.ds(0, 15 * OWN)], TEXT)

    def forward_img(j, _):
        slot = rows_at((core * 8 + lax.rem(z - j + 8, 8)) * OWN, OWN, OWN)
        copy(img.at[slot], img.at[slot], AG1Z, partner, zsem.at[j - 1]).wait_recv()
        copy(img.at[slot], img.at[slot], AG1C, partner).start()
        return 0

    lax.fori_loop(1, 8, forward_img, 0)

    loss_acc[...] = jnp.zeros_like(loss_acc)

    def pairs(half):
        images = rows_at((core if half == 0 else 1 - core) * 256, 256, 256)

        def step(b, _):
            rows = rows_at(b * 128, 128, 128)
            logits = logit_scale * dot_nt(txt[rows, :D], img[images, :]) + logit_bias
            weight = dot(txt[rows, D:], hot[half])
            slot = b * 128 + lax.broadcasted_iota(jnp.int32, (128, 256), 0)
            p = slot // OWN
            px, py = lax.rem(p, 4), p // 4
            index = (((lax.rem(px, 2) * 4 + py) * 2 + core) * 16 + z * 2 + px // 2) * OWN + lax.rem(slot, OWN)
            hit = index.astype(F32) == match[half]
            against = jnp.where(hit, -logits, logits)
            grown = jnp.exp(against)
            loss_acc[...] += weight * jnp.log(1.0 + grown)
            slope = logit_scale * weight * (grown / (1.0 + grown))
            coef[half, rows, :] = jnp.where(hit, -slope, slope).astype(BF16)
            return 0

        lax.fori_loop(0, 4, step, 0)

    pairs(0)
    got(img.at[pl.ds(0, 8 * OWN)], AG1C)
    pairs(1)

    for b in range(2):
        rows = pl.ds(b * 128, 128)
        c_send[rows, :] = dot_tn(coef[1, :, b * 128 : b * 128 + 128], txt[:, :D]).astype(BF16)
        copy(c_send.at[rows], c_recv.at[rows], RS2C, partner).start()
    for b in range(2):
        rows = pl.ds(b * 128, 128)
        ig[rows, :] = dot_tn(coef[0, :, b * 128 : b * 128 + 128], txt[:, :D])
    got(c_recv, RS2C)

    def send_rs2(j, _):
        rows = rows_at(lax.rem(z + j, 8) * OWN, OWN, OWN)
        rs2s[rows, :] = (ig[rows, :] + c_recv[rows, :].astype(F32)).astype(BF16)
        copy(rs2s.at[rows], rs2r.at[rows_at((j - 1) * OWN, OWN, OWN)], RS2Z, z_peer(j)).start()
        return 0

    lax.fori_loop(1, 8, send_rs2, 0)

    own_half, other_half = rows_at(core * 256, 256, 256), rows_at((1 - core) * 256, 256, 256)

    def text_grad(t, _):
        b = lax.rem(y + 1 + t, 4)
        rows = rows_at(b * 128, 128, 128)
        tgs[rows, :] = (dot(coef[0, rows, :], img[own_half, :]) + dot(coef[1, rows, :], img[other_half, :])).astype(BF16)

        def send(i, _):
            j = lax.rem(b - y + 4, 4) * 4 + lax.rem(i - x + 4, 4)

            @pl.when(j != 0)
            def _():
                copy(
                    tgs.at[rows_at((b * 4 + i) * OWN, OWN, OWN)], tgr.at[rows_at((j - 1) * OWN, OWN, OWN)], TG,
                    plane_dev(i, b),
                ).start()

            return 0

        lax.fori_loop(0, 4, send, 0)
        return 0

    lax.fori_loop(0, 4, text_grad, 0)
    l_tile[...] = jnp.zeros((8, 128), F32) + jnp.sum(loss_acc[...])

    def send_loss(j, _):
        copy(l_tile, l1r.at[rows_at((j - 1) * 8, 8, 8)], LOSS1, plane_peer(j)).start()
        return 0

    lax.fori_loop(1, 16, send_loss, 0)
    grad_text = dot(coef[0, own_text, :], img[own_half, :]) + dot(coef[1, own_text, :], img[other_half, :])

    own_z = rows_at(z * OWN, OWN, OWN)
    own_grad = ig[own_z, :] + c_recv[own_z, :].astype(F32)
    got(rs2r, RS2Z)

    def add_rs2(j, total):
        return total + rs2r[rows_at(j * OWN, OWN, OWN), :].astype(F32)

    own_grad = lax.fori_loop(0, 7, add_rs2, own_grad)
    projected = jnp.sum(unit * own_grad, axis=-1, keepdims=True)
    grad_features = (own_grad - unit * projected) / norm
    gfall[own_rows, :] = grad_features.astype(BF16)

    across_rows = rows_at((mp + 1 - 2 * xh) * OWN, OWN, OWN)
    copy(gfall.at[own_rows], gfall.at[own_rows], AG2X, across).start()
    gather_step(1, (2, 3), mp_row, gfall, AG2, ag2sem)

    got(gfall.at[across_rows], AG2X)
    gather_step(1, (0, 1), mp_row, gfall, AG2, ag2sem)
    gather_step(2, (2, 3, 0, 1), mp_row, gfall, AG2, ag2sem)
    gather_step(3, (2, 3, 0, 1), mp_row, gfall, AG2, ag2sem)

    got(l1r, LOSS1)
    loss = l_tile[...]
    for j in range(15):
        loss = loss + l1r[j * 8 : j * 8 + 8, :]
    lc_tile[...] = loss
    copy(lc_tile, lcr, LOSSC, partner).start()
    got(tgr, TG)

    def add_tg(j, total):
        return total + tgr[rows_at(j * OWN, OWN, OWN), :].astype(F32)

    gt_ref[...] = lax.fori_loop(0, 15, add_tg, grad_text)
    got(lcr, LOSSC)
    lz_tile[...] = loss + lcr[...]

    def send_loss_z(j, _):
        copy(lz_tile, lzr.at[rows_at((j - 1) * 8, 8, 8)], LOSSZ, z_peer(j)).start()
        return 0

    lax.fori_loop(1, 8, send_loss_z, 0)
    gather_step(4, (2, 3, 0, 1), mp_row, gfall, AG2, ag2sem)
    gather_end((2, 3, 0, 1), mp_row, gfall, AG2, ag2sem)

    def backward(b, _):
        rows = rows_at(b * 128, 128, 128)
        gh[rows, :] = (dot_nt(gfall[rows, :], wo_ref[...]) * gelu_slope(hp[rows, :])).astype(BF16)
        return 0

    lax.fori_loop(0, 4, backward, 0)

    def to_input(z2):
        rows = rows_at(z2 * 64, 64, 64)
        part[rows, :] = dot_nt(gh[rows, :], wi_ref[...])

    def rs3_step(far):
        reduce_step(far, 4, mp_row, part, rs3s, rs3r, RS3, rs3sem)
        to_input(toward(UP, far - 1))
        if far > 1:
            to_input(toward(DOWN, far - 1))

    other_cols, own_cols = rows_at((1 - core) * 128, 128, 128), rows_at(core * 128, 128, 128)

    def w_in_half(cols, out, kind):
        def step(b, _):
            part = rows_at(b * 128, 128, 128)
            out[part, :] = dot_tn(x_ref[:, part], gh[:, cols]).astype(kind)
            return 0

        lax.fori_loop(0, 9, step, 0)

    arc_so[...] = dot_tn(act[:, other_cols], gfall[...]).astype(BF16)
    copy(arc_so, arc_ro, ARC_O, partner).start()
    w_in_half(other_cols, arc_si, BF16)
    copy(arc_si, arc_ri, ARC_I, partner).start()
    awo[...] = dot_tn(act[:, own_cols], gfall[...])
    got(arc_ro, ARC_O)
    awo[...] += arc_ro[...].astype(F32)
    ars_so[...] = awo[...].astype(BF16)

    def send_ars_out(j, _):
        device, q = ar_peer(j)
        copy(ars_so.at[rows_at(q * 16, 16, 16)], ars_ro.at[rows_at((j - 1) * 16, 16, 16)], ARS_O, device).start()
        return 0

    lax.fori_loop(1, 8, send_ars_out, 0)
    w_in_half(own_cols, awi, F32)
    got(arc_ri, ARC_I)
    awi[...] += arc_ri[...].astype(F32)
    ars_si[...] = awi[...].astype(BF16)

    def send_ars_in(j, _):
        device, q = ar_peer(j)
        copy(ars_si.at[rows_at(q * 144, 144, 144)], ars_ri.at[rows_at((j - 1) * 144, 144, 144)], ARS_I, device).start()
        return 0

    lax.fori_loop(1, 8, send_ars_in, 0)

    to_input(toward(UP, 4))
    rs3_step(4)
    rs3_step(3)
    rs3_step(2)

    q = y * 2 + xl
    own_in, own_out = rows_at(q * 144, 144, 144), rows_at(q * 16, 16, 16)
    total_in, total_out = awi[own_in, :], awo[own_out, :]
    got(ars_ro, ARS_O)
    for j in range(7):
        total_out = total_out + ars_ro[j * 16 : j * 16 + 16, :].astype(F32)
    fwo[core, own_out, :] = total_out.astype(BF16)

    def send_aag_out(j, _):
        device, _ = ar_peer(j)
        copy(fwo.at[core, own_out], fwo.at[core, own_out], AAG_O, device).start()
        return 0

    lax.fori_loop(1, 8, send_aag_out, 0)
    got(ars_ri, ARS_I)
    for j in range(7):
        total_in = total_in + ars_ri[j * 144 : j * 144 + 144, :].astype(F32)
    fwi[core, own_in, :] = total_in.astype(BF16)

    def send_aag_in(j, _):
        device, _ = ar_peer(j)
        copy(fwi.at[core, own_in], fwi.at[core, own_in], AAG_I, device).start()
        return 0

    lax.fori_loop(1, 8, send_aag_in, 0)
    rs3_step(1)
    for f in (0, 1):
        rs3xs[f * FLOW : f * FLOW + FLOW, :] = reduce_end(f, 4, mp_row, part, rs3r, RS3, rs3sem).astype(BF16)
    copy(rs3xs, rs3xr, RS3X, across).start()
    grad_image = jnp.concatenate([reduce_end(f, 4, mp_row, part, rs3r, RS3, rs3sem) for f in (2, 3)], axis=0)
    grad_image = grad_image + grad_features

    got(lzr, LOSSZ)
    loss = lz_tile[...]
    for j in range(7):
        loss = loss + lzr[j * 8 : j * 8 + 8, :]
    loss_ref[...] = loss * (1.0 / PAIRS)

    got(fwo.at[core, pl.ds(0, 7 * 16)], AAG_O)
    copy(fwo.at[core], fwo.at[core], AFC_O, partner).start()
    got(fwi.at[core, pl.ds(0, 7 * 144)], AAG_I)
    copy(fwi.at[core], fwi.at[core], AFC_I, partner).start()
    got(rs3xr, RS3X)
    gi_ref[...] = grad_image + rs3xr[...].astype(F32)
    got(fwo.at[1 - core], AFC_O)
    for half in range(2):
        gwo_ref[half * 128 : half * 128 + 128, :] = fwo[half]
    got(fwi.at[1 - core], AFC_I)
    for half in range(2):
        gwi_ref[:, half * 128 : half * 128 + 128] = fwi[half]

    sent(txt.at[pl.ds(0, 15 * OWN)], TEXT)
    sent(meta.at[0], META)
    sent(rs1s.at[pl.ds(0, 28 * FLOW)], RS1)
    sent(rs1xs, RS1X)
    sent(img.at[pl.ds(0, 7 * OWN)], AG1Z)
    sent(img.at[pl.ds(0, 8 * OWN)], AG1C)
    sent(c_send, RS2C)
    sent(rs2r, RS2Z)
    sent(tgr, TG)
    sent(l1r, LOSS1)
    sent(lc_tile, LOSSC)
    sent(lzr, LOSSZ)
    sent(gfall.at[pl.ds(0, 28 * FLOW)], AG2)
    sent(rs3xs, AG2X)
    sent(rs3s.at[pl.ds(0, 28 * FLOW)], RS3)
    sent(rs3xs, RS3X)
    sent(arc_si, ARC_I)
    sent(arc_so, ARC_O)
    sent(ars_ri, ARS_I)
    sent(ars_ro, ARS_O)
    sent(fwi.at[0, pl.ds(0, 7 * 144)], AAG_I)
    sent(fwo.at[0, pl.ds(0, 7 * 16)], AAG_O)
    sent(fwi.at[0], AFC_I)
    sent(fwo.at[0], AFC_O)


def per_device(
    image_feats, text_feats, w_in, w_out, image_bucket, text_bucket, positive, reward_table
):
    vmem = pl.BlockSpec(memory_space=pltpu.VMEM)

    def buf(shape, kind=BF16):
        return pltpu.VMEM(shape, kind)

    scratch = [
        buf((ROWS, D)),
        buf((OWN, D)),
        buf((D, HID)),
        buf((HID, D)),
        buf((1, ROWS), jnp.int32),
        buf((1, OWN), jnp.int32),
        buf((1, ROWS), jnp.int32),
        buf((8, 8), F32),
        buf((ROWS, HID), F32),
        buf((ROWS, HID)),
        buf((ROWS, D), F32),
        buf((ROWS, D)),
        buf((ROWS, D)),
        buf((OWN, D)),
        buf((OWN, D)),
        buf((ROWS, D + ext)),
        buf((2, 8, 256), F32),
        buf((2, ext, 256)),
        buf((ROWS, D)),
        buf((2, ROWS, 256)),
        buf((128, 256), F32),
        buf((256, D)),
        buf((256, D)),
        buf((256, D), F32),
        buf((256, D)),
        buf((7 * OWN, D)),
        buf((ROWS, D)),
        buf((15 * OWN, D)),
        buf((8, 128), F32),
        buf((15 * 8, 128), F32),
        buf((8, 128), F32),
        buf((8, 128), F32),
        buf((8, 128), F32),
        buf((7 * 8, 128), F32),
        buf((ROWS, D)),
        buf((ROWS, HID)),
        buf((ROWS, D)),
        buf((ROWS, D)),
        buf((OWN, D)),
        buf((OWN, D)),
        buf((D, 128)),
        buf((128, D)),
        buf((D, 128)),
        buf((128, D)),
        buf((D, 128), F32),
        buf((128, D), F32),
        buf((D, 128)),
        buf((128, D)),
        buf((7 * 144, 128)),
        buf((7 * 16, D)),
        buf((2, D, 128)),
        buf((2, 128, D)),
        pltpu.SemaphoreType.DMA((8,)),
        pltpu.SemaphoreType.DMA((24,)),
        pltpu.SemaphoreType.DMA((24,)),
        pltpu.SemaphoreType.DMA((7,)),
        pltpu.SemaphoreType.DMA((32,)),
        pltpu.SemaphoreType.DMA((32,)),
        pltpu.SemaphoreType.DMA((32,)),
    ]
    loss, grad_text, grad_image, grad_w_in, grad_w_out = pl.pallas_call(
        kernel,
        out_shape=(
            jax.ShapeDtypeStruct((8, 128), F32),
            jax.ShapeDtypeStruct((OWN, D), F32),
            jax.ShapeDtypeStruct((OWN, D), F32),
            jax.ShapeDtypeStruct((D, HID), BF16),
            jax.ShapeDtypeStruct((HID, D), BF16),
        ),
        in_specs=[pl.BlockSpec(memory_space=pl.ANY)] * 8,
        out_specs=(vmem,) * 5,
        scratch_shapes=scratch,
        compiler_params=pltpu.CompilerParams(
            collective_id=0, has_side_effects=True, vmem_limit_bytes=VMEM_LIMIT
        ),
        name="pairs_and_block",
    )(
        image_feats, text_feats, w_in, w_out, image_bucket[None, :], text_bucket[None, :], positive[None, :],
        reward_table,
    )
    return (loss[0, 0], grad_text, grad_image, grad_w_in.astype(F32), grad_w_out.astype(F32))


def solution(mesh):
    return jax.shard_map(
        per_device,
        mesh=mesh,
        in_specs=(
            P("dp", None),
            P(("dp", "mp"), None),
            P(None, "mp"),
            P("mp", None),
            P("dp"),
            P(("dp", "mp")),
            P("dp"),
            P(),
        ),
        out_specs=(P(), P(("dp", "mp"), None), P(("dp", "mp"), None), P(None, "mp"), P("mp", None)),
        check_vma=False,
    )
```

```python
import jax
import jax.numpy as jnp
from jax import lax
from jax.experimental import pallas as pl
from jax.experimental.pallas import tpu as pltpu
from jax.sharding import PartitionSpec as P

MESH = pl.DeviceIdType.MESH
F32 = jnp.float32
BF16 = jnp.bfloat16

logit_scale = 4.0
logit_bias = -2.0
norm_eps = 1e-06
root_coef = 0.7978845608028654
cubic_coef = 0.044715

D = 1152
ROWS = 512
OWN = 32
HID = 256
PAIRS = 8192.0 * 8192.0
ext = 128
VMEM_LIMIT = 60 * 2**20

NT = (((1,), (1,)), ((), ()))
TN = (((0,), (0,)), ((), ()))


def dot(a, b):
    return jnp.dot(a, b, preferred_element_type=F32)


def dot_nt(a, b):
    return lax.dot_general(a, b, NT, preferred_element_type=F32)


def dot_tn(a, b):
    return lax.dot_general(a, b, TN, preferred_element_type=F32)


def gelu_tanh(v):
    return 0.5 * v * (1.0 + jnp.tanh(root_coef * (v + cubic_coef * v * v * v)))


def gelu_slope(v):
    t = jnp.tanh(root_coef * (v + cubic_coef * v * v * v))
    return 0.5 * (1.0 + t) + 0.5 * v * (1.0 - t * t) * root_coef * (1.0 + 3.0 * cubic_coef * v * v)


def row_norm(v):
    return jnp.sqrt(jnp.sum(v * v, axis=-1, keepdims=True) + norm_eps)


(TEXT, TEXT2, META, RS1, RS1B, RS1X, AG1C, RS2C, RS2Z, TG, TG2, LOSS1, LOSSC, LOSSZ, AG2, AG2X, RS3, RS3B, RS3X, ARC_I, ARC_O, ARS_I, ARS_O,
 AAG_I, AAG_O, AFC_I, AFC_O, AG1Z, RS1L, RS3L) = range(30)
FLOW = 16
UP, DOWN = 0, 1
SLOTS = ((0, UP), (4, UP), (3, UP), (3, DOWN), (2, UP), (2, DOWN), (1, UP), (1, DOWN))


def slot_at(way, far):
    return 0 if far == 0 else 1 if far == 4 else 8 - 2 * far + way


def rows_at(start, count, step):
    return pl.ds(pl.multiple_of(start, step), count)


def kernel(
    x_hbm, t_hbm, wi_hbm, wo_hbm, ib_hbm, tb_hbm, pos_hbm, tab_hbm,
    loss_ref, gt_ref, gi_ref, gwi_ref, gwo_ref,
    x_ref, t_ref, wi_ref, wo_ref, ib_ref, tb_ref, pos_ref, tab_ref,
    hp, act, part, rs1s, rs1r, rs1bs, rs1br, rs1ls, rs1lr, rs1xs, rs1xr, txt, meta, meta_s, meta_r, hot, img, coef, loss_acc, c_send, c_recv, ig, held, rs2s, rs2r, tgs, tgr, tgo, tgs2, tgr2,
    l_tile, l1r, lc_tile, lcr, lz_tile, lzr, gfall, gh, swi, swo, rs3s, rs3r, rs3bs, rs3br, rs3ls, rs3lr, rs3xs, rs3xr,
    arc_si, arc_so, arc_ri, arc_ro, awi, awo, ars_si, ars_so, ars_ri, ars_ro, fwi, fwo,
    lsem, ssem, rsem, csem, rs1sem, ag1sem, rs2sem, ag2sem, rs3sem, rs1bsem, ag2bsem, rs3bsem, aagsem,
):
    dp, mp = lax.axis_index("dp"), lax.axis_index("mp")
    core, y, xl = lax.rem(dp, 2), lax.rem(dp // 2, 4), dp // 8
    xh, z = lax.rem(mp, 2), mp // 2
    x = xh * 2 + xl
    partner = (dp + 1 - 2 * core, mp)

    across = (dp, mp + 1 - 2 * xh)

    def z_peer(j):
        return (dp, lax.rem(z + j, 8) * 2 + xh)

    def plane_dev(x2, y2):
        return ((lax.rem(x2, 2) * 4 + y2) * 2 + core, z * 2 + x2 // 2)

    def ar_peer(j):
        xl2, y2 = lax.rem(xl + lax.rem(j, 2), 2), lax.rem(y + j // 2, 4)
        return ((xl2 * 4 + y2) * 2 + core, mp), y2 * 2 + xl2

    def plane_peer(j):
        return plane_dev(lax.rem(x + lax.rem(j, 4), 4), lax.rem(y + j // 4, 4))

    def copy(src, dst, phase, device, recv=None):
        return pltpu.make_async_remote_copy(
            src_ref=src, dst_ref=dst, send_sem=ssem.at[phase],
            recv_sem=rsem.at[phase] if recv is None else recv, device_id=device, device_id_type=MESH,
        )

    def got(ref, phase):
        copy(ref, ref, phase, partner).wait_recv()

    def sent(ref, phase):
        copy(ref, ref, phase, partner).wait_send()

    def hops(f, way):
        return 4 if f % 2 == way else 3

    def neighbour(way):
        return z_peer(1 if way == UP else 7)

    def toward(way, far):
        return lax.rem(z + (far if way == UP else 8 - far), 8)

    barrier = pltpu.get_barrier_semaphore()

    def greet(j, _):
        pl.semaphore_signal(barrier, inc=1, device_id=plane_peer(j), device_id_type=MESH)
        return 0

    lax.fori_loop(1, 16, greet, 0)

    def greet_z(j, _):
        pl.semaphore_signal(barrier, inc=1, device_id=z_peer(j), device_id_type=MESH)
        return 0

    lax.fori_loop(1, 8, greet_z, 0)
    pl.semaphore_signal(barrier, inc=1, device_id=partner, device_id_type=MESH)

    loads = [
        pltpu.make_async_copy(src, dst, lsem.at[i])
        for i, (src, dst) in enumerate(
            (
                (t_hbm, t_ref), (tb_hbm, tb_ref), (pos_hbm, pos_ref), (ib_hbm, ib_ref), (tab_hbm, tab_ref),
                (wi_hbm, wi_ref), (wo_hbm, wo_ref),
            )
        )
    ]
    for load in loads:
        load.start()
    for far, way in SLOTS:
        for other in (0, 1):
            from_rows = rows_at((toward(way, far) * 2 + (1 - xh if other else xh)) * OWN, OWN, OWN)
            to_rows = pl.ds(slot_at(way, far) * 64 + other * OWN, OWN)
            pltpu.make_async_copy(x_hbm.at[from_rows], x_ref.at[to_rows], lsem.at[7]).start()
    for load in loads[:5]:
        load.wait()

    own_slot = y * 4 + x
    own_text = rows_at(own_slot * OWN, OWN, OWN)
    wide = t_ref[...].astype(F32)
    txt[own_text, :D] = (wide / row_norm(wide)).astype(BF16)
    eye = lax.broadcasted_iota(jnp.int32, (OWN, OWN), 0) == lax.broadcasted_iota(jnp.int32, (OWN, OWN), 1)
    tb_col = jnp.sum(jnp.where(eye, tb_ref[...].astype(F32), 0.0), axis=1, keepdims=True)
    lane = lax.broadcasted_iota(jnp.int32, (OWN, ext), 1)
    level = jnp.where(lane < 24, lax.rem(lane, 8), -1).astype(F32)
    txt[own_text, D:] = jnp.where(level == tb_col, 1.0, 0.0).astype(BF16)

    pl.semaphore_wait(barrier, 23)

    def send_text(j, _):
        device = plane_dev(lax.rem(x + j, 4), y)
        copy(txt.at[own_text], txt.at[own_text], TEXT, device).start()
        return 0

    lax.fori_loop(1, 4, send_text, 0)

    def text_on():
        got(txt.at[pl.ds(0, 3 * OWN)], TEXT)
        rows = rows_at(y * 128, 128, 128)

        def send(j, _):
            copy(txt.at[rows], txt.at[rows], TEXT2, plane_dev(x, lax.rem(y + j, 4))).start()
            return 0

        lax.fori_loop(1, 4, send, 0)

    def slot_of(f, way, far, flows):
        return pl.ds(((way * flows + f) * 4 + far - 1) * FLOW, FLOW)

    def sem_of(sems, f, way, far, flows):
        return sems.at[(way * flows + f) * 4 + far - 1]

    def last_of(f, way, last):
        return pl.ds((way + 2 * last[3].index(f)) * FLOW, FLOW)

    def reduce_step(far, which, flows, row_of, held, sbuf, rbuf, phase, sems, last):
        for f in which:
            for way in (UP, DOWN):
                if far > hops(f, way):
                    continue
                value = held[pl.ds(row_of(f, slot_at(way, far)), FLOW), :]
                if far < hops(f, way):
                    before = slot_of(f, way, far + 1, flows)
                    copy(rbuf.at[before], rbuf.at[before], phase, partner, sem_of(sems, f, way, far + 1, flows)).wait_recv()
                    value = value + rbuf[before, :].astype(F32)
                sem = sem_of(sems, f, way, far, flows)
                if f in last[3] and far == 1:
                    sbuf1, rbuf1, phase1, _ = last
                    slot = last_of(f, way, last)
                    sbuf1[slot, :] = value
                    copy(sbuf1.at[slot], rbuf1.at[slot], phase1, neighbour(way), sem).start()
                else:
                    slot = slot_of(f, way, far, flows)
                    sbuf[slot, :] = value.astype(BF16)
                    copy(sbuf.at[slot], rbuf.at[slot], phase, neighbour(way), sem).start()

    def reduce_end(f, flows, row_of, held, rbuf, phase, sems, last):
        value = held[pl.ds(row_of(f, 0), FLOW), :]
        for way in (UP, DOWN):
            slot = slot_of(f, way, 1, flows)
            if f in last[3]:
                rbuf, phase, slot = last[1], last[2], last_of(f, way, last)
            copy(rbuf.at[slot], rbuf.at[slot], phase, partner, sem_of(sems, f, way, 1, flows)).wait_recv()
            value = value + rbuf[slot, :].astype(F32)
        return value

    def gather_step(far, which, flows, row_of, buf, phase, sems):
        for f in which:
            for way in (UP, DOWN):
                if far > hops(f, way):
                    continue
                rows = pl.ds(row_of(f, slot_at(1 - way, far)), FLOW)
                if far > 0:
                    copy(buf.at[rows], buf.at[rows], phase, partner, sem_of(sems, f, way, far, flows)).wait_recv()
                if far < hops(f, way):
                    onto = pl.ds(row_of(f, slot_at(1 - way, far + 1)), FLOW)
                    copy(buf.at[rows], buf.at[onto], phase, neighbour(way), sem_of(sems, f, way, far + 1, flows)).start()

    def mp_row(f, slot):
        return slot * 64 + (OWN, 0, FLOW)[f]

    def reduce_mp(held, sbuf, rbuf, bs, br, xs, xr, last, phases, sems, bsems):
        ring_phase, b_phase, x_phase = phases

        def send_across(slots):
            for slot in slots:
                rows = pl.ds(slot * FLOW, FLOW)
                bs[rows, :] = held[slot * 64 + 48 : slot * 64 + 64, :].astype(BF16)
                copy(bs.at[rows], br.at[rows], b_phase, across, bsems.at[slot]).start()

        def ring(far):
            reduce_step(far, (0, 1), 3, mp_row, held, sbuf, rbuf, ring_phase, sems, last)

        def met(slots):
            for slot in slots:
                rows = pl.ds(slot * FLOW, FLOW)
                copy(br.at[rows], br.at[rows], b_phase, partner, bsems.at[slot]).wait_recv()
                held[slot * 64 + FLOW : slot * 64 + 2 * FLOW, :] += br[rows, :].astype(F32)

        def cross(far):
            met((1,) if far == 4 else (slot_at(UP, far), slot_at(DOWN, far)))
            reduce_step(far, (2,), 3, mp_row, held, sbuf, rbuf, ring_phase, sems, last)

        def end_across():
            xs[...] = reduce_end(0, 3, mp_row, held, rbuf, ring_phase, sems, last)
            copy(xs, xr, x_phase, across).start()
            met((0,))

        def end():
            near = reduce_end(1, 3, mp_row, held, rbuf, ring_phase, sems, last)
            mixed = reduce_end(2, 3, mp_row, held, rbuf, ring_phase, sems, last)
            got(xr, x_phase)
            return jnp.concatenate([near + xr[...], mixed], axis=0)

        return send_across, ring, cross, end_across, end

    for load in loads[5:]:
        load.wait()

    pltpu.make_async_copy(x_ref, x_ref, lsem.at[7]).wait()

    def forward(g):
        rows = pl.ds(g * 128, 128)
        pre = dot(x_ref[rows, :], wi_ref[...])
        hp[rows, :] = pre
        a = gelu_tanh(pre).astype(BF16)
        act[rows, :] = a
        part[rows, :] = dot(a, wo_ref[...])

    rs1_across, rs1_ring, rs1_cross, rs1_end_across, rs1_end = reduce_mp(
        part, rs1s, rs1r, rs1bs, rs1br, rs1xs, rs1xr, (rs1ls, rs1lr, RS1L, (2,)), (RS1, RS1B, RS1X), rs1sem, rs1bsem
    )
    forward(0)
    rs1_across((1, 0))
    rs1_ring(4)
    forward(1)
    rs1_across((2, 3))
    rs1_ring(3)
    forward(2)
    rs1_across((4, 5))
    rs1_cross(4)
    rs1_ring(2)
    forward(3)
    rs1_across((6, 7))
    rs1_cross(3)
    rs1_ring(1)
    text_on()
    pos = pos_ref[...]
    pos_hi = pos // 64
    line = lax.broadcasted_iota(jnp.int32, (8, ROWS), 0)
    table_rows = jnp.where(
        line == 0, pos_hi, jnp.where(line == 1, pos - pos_hi * 64, jnp.where(line == 2, ib_ref[...], 0))
    ).astype(F32).astype(BF16)
    took = lax.broadcasted_iota(jnp.int32, (ROWS, ROWS), 0)
    into = lax.broadcasted_iota(jnp.int32, (ROWS, ROWS), 1)
    slot = into // 64
    distance = jnp.where(lax.rem(slot, 2) == 0, 4 - slot // 2, slot // 2 + 4)
    distance = jnp.where(slot == 0, 0, jnp.where(slot == 1, 4, distance))
    right = took == (lax.rem(z + distance, 8) * 2 + xh) * OWN + lax.rem(into, OWN)
    first = lax.rem(into, 64) < OWN
    meta[...] = dot(table_rows, jnp.where(right & first, 1.0, 0.0).astype(BF16))
    meta_s[...] = dot(table_rows, jnp.where(right & jnp.logical_not(first), 1.0, 0.0).astype(BF16))

    copy(meta_s, meta_r, META, partner).start()
    rs1_cross(2)
    rs1_end_across()
    rs1_cross(1)
    features = rs1_end() + x_ref[:OWN, :].astype(F32)
    norm = row_norm(features)
    unit = features / norm

    img[:OWN, :] = unit.astype(BF16)
    def send_img(from_row, to_row, count, sem, distance):
        copy(
            img.at[pl.ds(from_row, count)], img.at[pl.ds(to_row, count)], AG1Z, z_peer(distance % 8), ag1sem.at[sem]
        ).start()

    def got_img(count, sem):
        copy(img.at[pl.ds(0, count)], img.at[pl.ds(0, count)], AG1Z, partner, ag1sem.at[sem]).wait_recv()

    for way, sign in ((UP, 1), (DOWN, -1)):
        send_img(0, slot_at(1 - way, 2) * 64, OWN, way, 2 * sign)
    for way, sign in ((UP, 1), (DOWN, -1)):
        send_img(0, slot_at(1 - way, 1) * 64, OWN, 2 + way, sign)

    def to_partner(slot):
        copy(
            img.at[pl.ds(slot * 64, OWN)], img.at[pl.ds(slot * 64 + OWN, OWN)], AG1C, partner, csem.at[slot // 2 + (4 if slot == 1 else 0)]
        ).start()

    def from_partner(far):
        count = OWN if far in (0, 4) else 2 * OWN
        copy(
            img.at[pl.ds(0, count)], img.at[pl.ds(0, count)], AG1C, partner, csem.at[0 if far == 0 else 4 - far if far < 4 else 4]
        ).wait_recv()

    to_partner(0)

    got(meta_r, META)
    meta[...] += meta_r[...]

    eye8 = lax.broadcasted_iota(jnp.int32, (8, 8), 0) == lax.broadcasted_iota(jnp.int32, (8, 8), 1)

    buckets = meta[2:3, :]
    weights = jnp.zeros((8, ROWS), F32)
    for k in range(8):
        column = jnp.sum(jnp.where(eye8, tab_ref[k : k + 1, :], 0.0), axis=1, keepdims=True)
        weights = weights + jnp.where(buckets == float(k), column, 0.0)
    hi = weights.astype(BF16).astype(F32)
    mid = (weights - hi).astype(BF16).astype(F32)
    low = weights - hi - mid
    hot[...] = jnp.concatenate([hi, mid, low, jnp.zeros((ext - 24, ROWS), F32)], axis=0).astype(BF16)
    meta[0:1, :] = meta[0:1, :] * 64.0 + meta[1:2, :]
    got(txt.at[pl.ds(0, 3 * 128)], TEXT2)

    loss_acc[...] = jnp.zeros_like(loss_acc)

    def pairs(g):
        images = pl.ds(g * 128, 128)

        logits = logit_scale * dot_nt(txt[:, :D], img[images, :]) + logit_bias
        weight = dot(txt[:, D:], hot[:, images])
        slot = lax.broadcasted_iota(jnp.int32, (ROWS, 1), 0)
        p = slot // OWN
        px, py = lax.rem(p, 4), p // 4
        index = (((lax.rem(px, 2) * 4 + py) * 2 + core) * 16 + z * 2 + px // 2) * OWN + lax.rem(slot, OWN)
        hit = index.astype(F32) == meta[0:1, images]
        against = jnp.where(hit, -logits, logits)
        grown = jnp.exp(against)
        loss_acc[...] += jnp.sum((weight * jnp.log(1.0 + grown)).reshape(ROWS // 8, 8, 128), axis=0)
        slope = logit_scale * weight * (grown / (1.0 + grown))
        coef[:, images] = jnp.where(hit, -slope, slope).astype(BF16)

    for way in (UP, DOWN):
        got_img(OWN, 2 + way)
        to_partner(slot_at(1 - way, 1))
    for way, sign in ((UP, 1), (DOWN, -1)):
        got_img(OWN, way)
        row = slot_at(1 - way, 2) * 64
        send_img(row, slot_at(1 - way, 3) * 64, OWN, 4 + way, sign)
        send_img(row + FLOW * way, 64 + FLOW * way, FLOW, 6 + way, 2 * sign)
    for way in (UP, DOWN):
        to_partner(slot_at(1 - way, 2))
    from_partner(1)
    pairs(3)
    for way in (UP, DOWN):
        got_img(OWN, 4 + way)
        to_partner(slot_at(1 - way, 3))
    from_partner(2)
    pairs(2)
    for way in (UP, DOWN):
        got_img(FLOW, 6 + way)
    to_partner(1)
    from_partner(3)
    pairs(1)
    from_partner(0)
    from_partner(4)
    pairs(0)

    def image_grad(g):
        rows = pl.ds(g * 128, 128)
        ig[rows, :] = dot_tn(coef[:, rows], txt[:, :D])
        to = pl.ds(g * 64, 64)
        for slot in (2 * g, 2 * g + 1):
            c_send[slot * OWN : slot * OWN + OWN, :] = ig[slot * 64 + OWN : slot * 64 + 64, :]
        copy(c_send.at[to], c_recv.at[to], RS2C, partner, csem.at[5 + g]).start()

    def both_cores(g):
        to = pl.ds(g * 64, 64)
        copy(c_send.at[to], c_recv.at[to], RS2C, partner, csem.at[5 + g]).wait_recv()
        for slot in (2 * g, 2 * g + 1):
            rows = pl.ds(slot * OWN, OWN)
            held[rows, :] = ig[slot * 64 : slot * 64 + OWN, :] + c_recv[rows, :]

    def send_rs2(value, sem, distance):
        rows = pl.ds(sem * OWN, value.shape[0])
        rs2s[rows, :] = value.astype(BF16)
        copy(rs2s.at[rows], rs2r.at[rows], RS2Z, z_peer(distance % 8), rs2sem.at[sem]).start()

    def got_rs2(sem, count=OWN):
        rows = pl.ds(sem * OWN, count)
        copy(rs2r.at[rows], rs2r.at[rows], RS2Z, partner, rs2sem.at[sem]).wait_recv()
        return rs2r[rows, :].astype(F32)

    def held_at(way, far):
        row = slot_at(way, far) * OWN
        return held[row : row + OWN, :]

    image_grad(0)
    image_grad(1)
    both_cores(0)
    far4 = held_at(UP, 4)
    send_rs2(far4[:FLOW], 0, 2)
    send_rs2(far4[FLOW:], 1, -2)
    image_grad(2)
    both_cores(1)
    send_rs2(held_at(UP, 3), 2, 1)
    send_rs2(held_at(DOWN, 3), 3, -1)
    image_grad(3)
    both_cores(2)
    both_cores(3)
    send_rs2(held_at(UP, 1), 6, 1)
    send_rs2(held_at(DOWN, 1), 7, -1)

    def text_grad(j, _):
        b = lax.rem(y + j, 4)
        rows = rows_at(b * 128, 128, 128)
        tgs[rows, :] = dot(coef[rows, :], img[...]).astype(BF16)
        copy(tgs.at[rows], tgr.at[rows_at((j - 1) * 128, 128, 128)], TG, plane_dev(x, b)).start()
        return 0

    lax.fori_loop(1, 3, text_grad, 0)
    far2 = held_at(UP, 2) + got_rs2(2)
    send_rs2(jnp.concatenate([far2[:FLOW] + got_rs2(0, FLOW), far2[FLOW:]], axis=0), 4, 2)
    far2 = held_at(DOWN, 2) + got_rs2(3)
    send_rs2(jnp.concatenate([far2[:FLOW], far2[FLOW:] + got_rs2(1, FLOW)], axis=0), 5, -2)
    text_grad(3, 0)
    tgo[...] = dot(coef[rows_at(y * 128, 128, 128), :], img[...])

    def text_grad_on():
        got(tgr, TG)
        tgo[...] += tgr[0:128, :].astype(F32) + tgr[128:256, :].astype(F32) + tgr[256:384, :].astype(F32)

        def send(j, _):
            x2 = lax.rem(x + j, 4)
            rows = rows_at(x2 * OWN, OWN, OWN)
            tgs2[rows, :] = tgo[rows, :].astype(BF16)
            copy(tgs2.at[rows], tgr2.at[rows_at((j - 1) * OWN, OWN, OWN)], TG2, plane_dev(x2, y)).start()
            return 0

        lax.fori_loop(1, 4, send, 0)

    l_tile[...] = jnp.zeros((8, 128), F32) + jnp.sum(loss_acc[...])

    def send_loss(j, _):
        copy(l_tile, l1r.at[rows_at((j - 1) * 8, 8, 8)], LOSS1, plane_peer(j)).start()
        return 0

    lax.fori_loop(1, 16, send_loss, 0)

    own_grad = held[0:OWN, :] + got_rs2(6) + got_rs2(7) + got_rs2(4) + got_rs2(5)
    projected = jnp.sum(unit * own_grad, axis=-1, keepdims=True)
    grad_features = (own_grad - unit * projected) / norm
    gfall[:OWN, :] = grad_features.astype(BF16)
    def cross_gf(slot):
        copy(
            gfall.at[pl.ds(slot * 64 + FLOW, FLOW)], gfall.at[pl.ds(slot * 64 + 48, FLOW)], AG2X, across, ag2bsem.at[slot]
        ).start()

    def crossed_gf(slots):
        for slot in slots:
            rows = pl.ds(slot * 64 + 48, FLOW)
            copy(gfall.at[rows], gfall.at[rows], AG2X, partner, ag2bsem.at[slot]).wait_recv()

    def ag2_step(far, which):
        gather_step(far, which, 3, mp_row, gfall, AG2, ag2sem)

    def near_step(far):
        ag2_step(far, (2, 1))
        for slot in (1,) if far == 4 else (slot_at(UP, far), slot_at(DOWN, far)):
            cross_gf(slot)

    other_rows = pl.ds(OWN, FLOW)
    copy(gfall.at[pl.ds(0, FLOW)], gfall.at[other_rows], AG2X, across).start()
    ag2_step(0, (2, 1))
    cross_gf(0)
    near_step(1)
    got(gfall.at[other_rows], AG2X)
    ag2_step(0, (0,))
    near_step(2)

    def backward(g):
        rows = pl.ds(g * 128, 128)
        gh[rows, :] = (dot_nt(gfall[rows, :], wo_ref[...]) * gelu_slope(hp[rows, :])).astype(BF16)

    def to_input(g):
        rows = pl.ds(g * 128, 128)
        part[rows, :] = dot_nt(gh[rows, :], wi_ref[...])

    rs3_across, rs3_ring, rs3_cross, rs3_end_across, rs3_end = reduce_mp(
        part, rs3s, rs3r, rs3bs, rs3br, rs3xs, rs3xr, (rs3ls, rs3lr, RS3L, (0, 1, 2)), (RS3, RS3B, RS3X), rs3sem, rs3bsem
    )

    other_cols, own_cols = rows_at((1 - core) * 128, 128, 128), rows_at(core * 128, 128, 128)
    late, early = pl.ds(0, 256), pl.ds(256, 256)

    def w_in_half(cols, out, kind):
        def step(b, _):
            some = rows_at(b * 128, 128, 128)
            out[some, :] = (swi[some, cols] + dot_tn(x_ref[late, some], gh[late, cols])).astype(kind)
            return 0

        lax.fori_loop(0, 9, step, 0)

    def w_in_early(b, _):
        some = rows_at(b * 128, 128, 128)
        swi[some, :] = dot_tn(x_ref[early, some], gh[early, :])
        return 0

    ag2_step(1, (0,))
    crossed_gf((6, 7))
    backward(3)
    near_step(3)
    ag2_step(2, (0,))
    crossed_gf((4, 5))
    backward(2)
    swo[...] = dot_tn(act[early, :], gfall[early, :])
    near_step(4)
    ag2_step(3, (0,))
    lax.fori_loop(0, 9, w_in_early, 0)
    crossed_gf((2, 3))
    backward(1)
    to_input(2)
    to_input(3)
    to_input(1)
    ag2_step(4, (0,))
    crossed_gf((0, 1))
    arc_so[...] = (swo[other_cols, :] + dot_tn(act[late, other_cols], gfall[late, :])).astype(BF16)
    copy(arc_so, arc_ro, ARC_O, partner).start()
    backward(0)
    w_in_half(other_cols, arc_si, BF16)
    copy(arc_si, arc_ri, ARC_I, partner).start()
    to_input(0)
    rs3_across((1, 2, 3))
    rs3_ring(4)
    rs3_across((4, 5, 6, 7, 0))
    awo[...] = swo[own_cols, :] + dot_tn(act[late, own_cols], gfall[late, :])
    got(arc_ro, ARC_O)
    awo[...] += arc_ro[...].astype(F32)
    ars_so[...] = awo[...].astype(BF16)

    def send_ars_out(j, _):
        device, q = ar_peer(j)
        copy(ars_so.at[rows_at(q * 16, 16, 16)], ars_ro.at[rows_at((j - 1) * 16, 16, 16)], ARS_O, device).start()
        return 0

    lax.fori_loop(1, 8, send_ars_out, 0)
    w_in_half(own_cols, awi, F32)
    got(arc_ri, ARC_I)
    awi[...] += arc_ri[...].astype(F32)
    ars_si[...] = awi[...].astype(BF16)

    def send_ars_in(j, _):
        device, q = ar_peer(j)
        copy(ars_si.at[rows_at(q * 144, 144, 144)], ars_ri.at[rows_at((j - 1) * 144, 144, 144)], ARS_I, device).start()
        return 0

    lax.fori_loop(1, 8, send_ars_in, 0)
    text_grad_on()
    rs3_ring(3)
    rs3_cross(4)
    got(l1r, LOSS1)
    loss = l_tile[...]
    for j in range(15):
        loss = loss + l1r[j * 8 : j * 8 + 8, :]
    lc_tile[...] = loss
    copy(lc_tile, lcr, LOSSC, partner).start()

    rs3_ring(2)
    rs3_cross(3)
    got(lcr, LOSSC)
    lz_tile[...] = loss + lcr[...]

    def send_loss_z(j, _):
        copy(lz_tile, lzr.at[rows_at((j - 1) * 8, 8, 8)], LOSSZ, z_peer(j)).start()
        return 0

    lax.fori_loop(1, 8, send_loss_z, 0)
    rs3_ring(1)
    rs3_cross(2)

    q = y * 2 + xl
    own_in, own_out = rows_at(q * 144, 144, 144), rows_at(q * 16, 16, 16)
    total_in, total_out = awi[own_in, :], awo[own_out, :]
    got(ars_ro, ARS_O)
    for j in range(7):
        total_out = total_out + ars_ro[j * 16 : j * 16 + 16, :].astype(F32)
    fwo[core, own_out, :] = total_out.astype(BF16)

    def send_aag_out(j, _):
        device, _ = ar_peer(j)
        copy(fwo.at[core, own_out], fwo.at[core, own_out], AAG_O, device, aagsem.at[7 + j]).start()
        return 0

    lax.fori_loop(1, 8, send_aag_out, 0)
    copy(fwo.at[core, own_out], fwo.at[core, own_out], AFC_O, partner).start()
    got(ars_ri, ARS_I)
    for j in range(7):
        total_in = total_in + ars_ri[j * 144 : j * 144 + 144, :].astype(F32)
    fwi[core, own_in, :] = total_in.astype(BF16)

    def send_aag_in(j, _):
        device, _ = ar_peer(j)
        copy(fwi.at[core, own_in], fwi.at[core, own_in], AAG_I, device, aagsem.at[j - 1]).start()
        return 0

    lax.fori_loop(1, 8, send_aag_in, 0)
    copy(fwi.at[core, own_in], fwi.at[core, own_in], AFC_I, partner).start()
    rs3_end_across()
    rs3_cross(1)
    grad_image = rs3_end() + grad_features

    got(tgr2, TG2)
    grad_text = tgo[rows_at(x * OWN, OWN, OWN), :]
    for j in range(3):
        grad_text = grad_text + tgr2[j * OWN : j * OWN + OWN, :].astype(F32)
    gt_ref[...] = grad_text
    got(lzr, LOSSZ)
    loss = lz_tile[...]
    for j in range(7):
        loss = loss + lzr[j * 8 : j * 8 + 8, :]
    loss_ref[...] = loss * (1.0 / PAIRS)

    def weights_on(j, _):
        xl2, y2 = lax.rem(xl + lax.rem(j, 2), 2), lax.rem(y + 4 - j // 2, 4)
        q2 = y2 * 2 + xl2
        out, into = rows_at(q2 * 16, 16, 16), rows_at(q2 * 144, 144, 144)
        copy(fwo.at[core, out], fwo.at[core, out], AAG_O, partner, aagsem.at[7 + j]).wait_recv()
        copy(fwo.at[core, out], fwo.at[core, out], AFC_O, partner).start()
        copy(fwi.at[core, into], fwi.at[core, into], AAG_I, partner, aagsem.at[j - 1]).wait_recv()
        copy(fwi.at[core, into], fwi.at[core, into], AFC_I, partner).start()
        return 0

    lax.fori_loop(1, 8, weights_on, 0)
    gi_ref[...] = grad_image
    got(fwo.at[1 - core], AFC_O)
    for half in range(2):
        gwo_ref[half * 128 : half * 128 + 128, :] = fwo[half]
    got(fwi.at[1 - core], AFC_I)
    for half in range(2):
        gwi_ref[:, half * 128 : half * 128 + 128] = fwi[half]

    sent(txt.at[pl.ds(0, 3 * OWN)], TEXT)
    sent(txt.at[pl.ds(0, 3 * 128)], TEXT2)
    sent(meta_s, META)
    sent(rs1s.at[pl.ds(0, 19 * FLOW)], RS1)
    sent(rs1bs, RS1B)
    sent(rs1ls, RS1L)
    sent(rs1xs, RS1X)
    sent(img.at[pl.ds(0, 14 * FLOW)], AG1Z)
    sent(img.at[pl.ds(0, 8 * OWN)], AG1C)
    sent(c_send, RS2C)
    sent(rs2s.at[pl.ds(0, 14 * FLOW)], RS2Z)
    sent(tgr, TG)
    sent(tgr2, TG2)
    sent(l1r, LOSS1)
    sent(lc_tile, LOSSC)
    sent(lzr, LOSSZ)
    sent(gfall.at[pl.ds(0, 21 * FLOW)], AG2)
    sent(gfall.at[pl.ds(0, 9 * FLOW)], AG2X)
    sent(rs3s.at[pl.ds(0, 15 * FLOW)], RS3)
    sent(rs3bs, RS3B)
    sent(rs3ls, RS3L)
    sent(rs3xs, RS3X)
    sent(arc_si, ARC_I)
    sent(arc_so, ARC_O)
    sent(ars_ri, ARS_I)
    sent(ars_ro, ARS_O)
    sent(fwi.at[0, pl.ds(0, 7 * 144)], AAG_I)
    sent(fwo.at[0, pl.ds(0, 7 * 16)], AAG_O)
    sent(fwi.at[0], AFC_I)
    sent(fwo.at[0], AFC_O)


def widen(loss_in, gt_in, gi_in, gwi_in, gwo_in, loss_ref, gt_ref, gi_ref, gwi_ref, gwo_ref):
    loss_ref[0, 0] = jnp.max(loss_in[...])
    gt_ref[...] = gt_in[...]
    gi_ref[...] = gi_in[...]
    gwi_ref[...] = gwi_in[...].astype(F32)
    gwo_ref[...] = gwo_in[...].astype(F32)


def per_device(
    image_feats, text_feats, w_in, w_out, image_bucket, text_bucket, positive, reward_table
):
    vmem = pl.BlockSpec(memory_space=pltpu.VMEM)

    def buf(shape, kind=BF16):
        return pltpu.VMEM(shape, kind)

    scratch = [
        buf((ROWS, D)),
        buf((OWN, D)),
        buf((D, HID)),
        buf((HID, D)),
        buf((1, ROWS), jnp.int32),
        buf((1, OWN), jnp.int32),
        buf((1, ROWS), jnp.int32),
        buf((8, 8), F32),
        buf((ROWS, HID), F32),
        buf((ROWS, HID)),
        buf((ROWS, D), F32),
        buf((ROWS, D)),
        buf((ROWS, D)),
        buf((8 * FLOW, D)),
        buf((8 * FLOW, D)),
        buf((2 * FLOW, D), F32),
        buf((2 * FLOW, D), F32),
        buf((FLOW, D), F32),
        buf((FLOW, D), F32),
        buf((ROWS, D + ext)),
        buf((8, ROWS), F32),
        buf((8, ROWS), F32),
        buf((8, ROWS), F32),
        buf((ext, ROWS)),
        buf((ROWS, D)),
        buf((ROWS, ROWS)),
        buf((8, 128), F32),
        buf((256, D), F32),
        buf((256, D), F32),
        buf((ROWS, D), F32),
        buf((256, D), F32),
        buf((256, D)),
        buf((256, D)),
        buf((ROWS, D)),
        buf((3 * 128, D)),
        buf((128, D), F32),
        buf((128, D)),
        buf((3 * OWN, D)),
        buf((8, 128), F32),
        buf((15 * 8, 128), F32),
        buf((8, 128), F32),
        buf((8, 128), F32),
        buf((8, 128), F32),
        buf((7 * 8, 128), F32),
        buf((ROWS, D)),
        buf((ROWS, HID)),
        buf((D, HID), F32),
        buf((HID, D), F32),
        buf((ROWS, D)),
        buf((ROWS, D)),
        buf((8 * FLOW, D)),
        buf((8 * FLOW, D)),
        buf((6 * FLOW, D), F32),
        buf((6 * FLOW, D), F32),
        buf((FLOW, D), F32),
        buf((FLOW, D), F32),
        buf((D, 128)),
        buf((128, D)),
        buf((D, 128)),
        buf((128, D)),
        buf((D, 128), F32),
        buf((128, D), F32),
        buf((D, 128)),
        buf((128, D)),
        buf((7 * 144, 128)),
        buf((7 * 16, D)),
        buf((2, D, 128)),
        buf((2, 128, D)),
        pltpu.SemaphoreType.DMA((8,)),
        pltpu.SemaphoreType.DMA((30,)),
        pltpu.SemaphoreType.DMA((30,)),
        pltpu.SemaphoreType.DMA((9,)),
        pltpu.SemaphoreType.DMA((24,)),
        pltpu.SemaphoreType.DMA((8,)),
        pltpu.SemaphoreType.DMA((8,)),
        pltpu.SemaphoreType.DMA((24,)),
        pltpu.SemaphoreType.DMA((24,)),
        pltpu.SemaphoreType.DMA((8,)),
        pltpu.SemaphoreType.DMA((8,)),
        pltpu.SemaphoreType.DMA((8,)),
        pltpu.SemaphoreType.DMA((15,)),
    ]
    partial = pl.pallas_call(
        kernel,
        out_shape=(
            jax.ShapeDtypeStruct((8, 128), F32),
            jax.ShapeDtypeStruct((OWN, D), F32),
            jax.ShapeDtypeStruct((OWN, D), F32),
            jax.ShapeDtypeStruct((D, HID), BF16),
            jax.ShapeDtypeStruct((HID, D), BF16),
        ),
        in_specs=[pl.BlockSpec(memory_space=pltpu.HBM)] * 8,
        out_specs=(vmem,) * 5,
        scratch_shapes=scratch,
        compiler_params=pltpu.CompilerParams(
            collective_id=0, has_side_effects=True, vmem_limit_bytes=VMEM_LIMIT
        ),
        name="pairs_and_block",
    )(
        image_feats, text_feats, w_in, w_out, image_bucket[None, :], text_bucket[None, :], positive[None, :],
        reward_table,
    )
    loss, grad_text, grad_image, grad_w_in, grad_w_out = pl.pallas_call(
        widen,
        out_shape=(
            jax.ShapeDtypeStruct((1, 1), F32),
            jax.ShapeDtypeStruct((OWN, D), F32),
            jax.ShapeDtypeStruct((OWN, D), F32),
            jax.ShapeDtypeStruct((D, HID), F32),
            jax.ShapeDtypeStruct((HID, D), F32),
        ),
        in_specs=[vmem] * 5,
        out_specs=(pl.BlockSpec(memory_space=pltpu.SMEM),) + (vmem,) * 4,
        compiler_params=pltpu.CompilerParams(vmem_limit_bytes=VMEM_LIMIT),
        name="widen",
    )(*partial)
    return (loss.reshape(()), grad_text, grad_image, grad_w_in, grad_w_out)


def solution(mesh):
    return jax.shard_map(
        per_device,
        mesh=mesh,
        in_specs=(
            P("dp", None),
            P(("dp", "mp"), None),
            P(None, "mp"),
            P("mp", None),
            P("dp"),
            P(("dp", "mp")),
            P("dp"),
            P(),
        ),
        out_specs=(P(), P(("dp", "mp"), None), P(("dp", "mp"), None), P(None, "mp"), P("mp", None)),
        check_vma=False,
    )
```

```python
import jax
import jax.numpy as jnp
from jax import lax
from jax.experimental import pallas as pl
from jax.experimental.pallas import tpu as pltpu
from jax.sharding import PartitionSpec as P

MESH = pl.DeviceIdType.MESH
F32 = jnp.float32
BF16 = jnp.bfloat16

logit_scale = 4.0
logit_bias = -2.0
norm_eps = 1e-06
root_coef = 0.7978845608028654
cubic_coef = 0.044715

D = 1152
ROWS = 512
OWN = 32
HID = 256
PAIRS = 8192.0 * 8192.0
ext = 128
VMEM_LIMIT = 60 * 2**20

NT = (((1,), (1,)), ((), ()))
TN = (((0,), (0,)), ((), ()))


def dot(a, b):
    return jnp.dot(a, b, preferred_element_type=F32)


def dot_nt(a, b):
    return lax.dot_general(a, b, NT, preferred_element_type=F32)


def dot_tn(a, b):
    return lax.dot_general(a, b, TN, preferred_element_type=F32)


def gelu_tanh(v):
    return 0.5 * v * (1.0 + jnp.tanh(root_coef * (v + cubic_coef * v * v * v)))


def gelu_slope(v):
    t = jnp.tanh(root_coef * (v + cubic_coef * v * v * v))
    return 0.5 * (1.0 + t) + 0.5 * v * (1.0 - t * t) * root_coef * (1.0 + 3.0 * cubic_coef * v * v)


def row_norm(v):
    return jnp.sqrt(jnp.sum(v * v, axis=-1, keepdims=True) + norm_eps)


(TEXT, TEXT2, META, RS1, RS1B, RS1X, AG1C, RS2C, RS2Z, TG, TG2, LOSS1, LOSSC, LOSSZ, AG2, AG2X, RS3, RS3B, RS3X, ARC_I, ARC_O, ARS_I, ARS_O,
 AAG_I, AAG_O, AFC_I, AFC_O, AG1Z, RS1L, RS3L) = range(30)
FLOW = 16
UP, DOWN = 0, 1
SLOTS = ((0, UP), (4, UP), (3, UP), (3, DOWN), (2, UP), (2, DOWN), (1, UP), (1, DOWN))


def slot_at(way, far):
    return 0 if far == 0 else 1 if far == 4 else 8 - 2 * far + way


def rows_at(start, count, step):
    return pl.ds(pl.multiple_of(start, step), count)


def kernel(
    x_hbm, t_hbm, wi_hbm, wo_hbm, ib_hbm, tb_hbm, pos_hbm, tab_hbm,
    loss_ref, gt_ref, gi_ref, gwi_ref, gwo_ref,
    x_ref, t_ref, wi_ref, wo_ref, ib_ref, tb_ref, pos_ref, tab_ref,
    xt, hp, act, part, rs1s, rs1r, rs1bs, rs1br, rs1ls, rs1lr, rs1xs, rs1xr, txt, meta, meta_s, meta_r, hot, img, coef, loss_acc, c_send, c_recv, ig, held, rs2s, rs2r, tgs, tgr, tgo, tgs2, tgr2,
    l_tile, l1r, lc_tile, lcr, lz_tile, lzr, gfall, gh, swi, swo, rs3s, rs3r, rs3bs, rs3br, rs3ls, rs3lr, rs3xs, rs3xr,
    arc_si, arc_so, arc_ri, arc_ro, awi, awo, ars_si, ars_so, ars_ri, ars_ro, fwi, fwo,
    lsem, ssem, rsem, csem, rs1sem, ag1sem, rs2sem, ag2sem, rs3sem, rs1bsem, ag2bsem, rs3bsem, aagsem,
):
    dp, mp = lax.axis_index("dp"), lax.axis_index("mp")
    core, y, xl = lax.rem(dp, 2), lax.rem(dp // 2, 4), dp // 8
    xh, z = lax.rem(mp, 2), mp // 2
    x = xh * 2 + xl
    partner = (dp + 1 - 2 * core, mp)

    across = (dp, mp + 1 - 2 * xh)

    def z_peer(j):
        return (dp, lax.rem(z + j, 8) * 2 + xh)

    def plane_dev(x2, y2):
        return ((lax.rem(x2, 2) * 4 + y2) * 2 + core, z * 2 + x2 // 2)

    def ar_peer(j):
        xl2, y2 = lax.rem(xl + lax.rem(j, 2), 2), lax.rem(y + j // 2, 4)
        return ((xl2 * 4 + y2) * 2 + core, mp), y2 * 2 + xl2

    def plane_peer(j):
        return plane_dev(lax.rem(x + lax.rem(j, 4), 4), lax.rem(y + j // 4, 4))

    def copy(src, dst, phase, device, recv=None):
        return pltpu.make_async_remote_copy(
            src_ref=src, dst_ref=dst, send_sem=ssem.at[phase],
            recv_sem=rsem.at[phase] if recv is None else recv, device_id=device, device_id_type=MESH,
        )

    def got(ref, phase):
        copy(ref, ref, phase, partner).wait_recv()

    def sent(ref, phase):
        copy(ref, ref, phase, partner).wait_send()

    def hops(f, way):
        return 4 if f % 2 == way else 3

    def neighbour(way, distance=1):
        return z_peer(distance if way == UP else 8 - distance)

    def toward(way, far):
        return lax.rem(z + (far if way == UP else 8 - far), 8)

    barrier = pltpu.get_barrier_semaphore()

    def greet(j, _):
        pl.semaphore_signal(barrier, inc=1, device_id=plane_peer(j), device_id_type=MESH)
        return 0

    lax.fori_loop(1, 16, greet, 0)

    def greet_z(j, _):
        pl.semaphore_signal(barrier, inc=1, device_id=z_peer(j), device_id_type=MESH)
        return 0

    lax.fori_loop(1, 8, greet_z, 0)
    pl.semaphore_signal(barrier, inc=1, device_id=partner, device_id_type=MESH)

    loads = [
        pltpu.make_async_copy(src, dst, lsem.at[i])
        for i, (src, dst) in enumerate(
            (
                (t_hbm, t_ref), (tb_hbm, tb_ref), (pos_hbm, pos_ref), (ib_hbm, ib_ref), (tab_hbm, tab_ref),
                (wi_hbm, wi_ref), (wo_hbm, wo_ref),
            )
        )
    ]
    for load in loads:
        load.start()
    for far, way in SLOTS:
        for other in (0, 1):
            from_rows = rows_at((toward(way, far) * 2 + (1 - xh if other else xh)) * OWN, OWN, OWN)
            to_rows = pl.ds(slot_at(way, far) * 64 + other * OWN, OWN)
            pltpu.make_async_copy(x_hbm.at[from_rows], x_ref.at[to_rows], lsem.at[7]).start()
    for load in loads[:5]:
        load.wait()

    own_slot = y * 4 + x
    own_text = rows_at(own_slot * OWN, OWN, OWN)
    wide = t_ref[...].astype(F32)
    txt[own_text, :D] = (wide / row_norm(wide)).astype(BF16)
    eye = lax.broadcasted_iota(jnp.int32, (OWN, OWN), 0) == lax.broadcasted_iota(jnp.int32, (OWN, OWN), 1)
    tb_col = jnp.sum(jnp.where(eye, tb_ref[...].astype(F32), 0.0), axis=1, keepdims=True)
    lane = lax.broadcasted_iota(jnp.int32, (OWN, ext), 1)
    level = jnp.where(lane < 24, lax.rem(lane, 8), -1).astype(F32)
    txt[own_text, D:] = jnp.where(level == tb_col, 1.0, 0.0).astype(BF16)

    pl.semaphore_wait(barrier, 23)

    def send_text(j, _):
        device = plane_dev(lax.rem(x + j, 4), y)
        copy(txt.at[own_text], txt.at[own_text], TEXT, device).start()
        return 0

    lax.fori_loop(1, 4, send_text, 0)

    def text_on():
        got(txt.at[pl.ds(0, 3 * OWN)], TEXT)
        rows = rows_at(y * 128, 128, 128)

        def send(j, _):
            copy(txt.at[rows], txt.at[rows], TEXT2, plane_dev(x, lax.rem(y + j, 4))).start()
            return 0

        lax.fori_loop(1, 4, send, 0)

    def slot_of(f, way, far, flows):
        return pl.ds(((way * flows + f) * 4 + far - 1) * FLOW, FLOW)

    def sem_of(sems, f, way, far, flows):
        return sems.at[(way * flows + f) * 4 + far - 1]

    def last_of(f, way, last):
        return pl.ds((way + 2 * last[3].index(f)) * FLOW, FLOW)

    def reduce_step(far, which, flows, row_of, held, sbuf, rbuf, phase, sems, last):
        for f in which:
            for way in (UP, DOWN):
                if far > hops(f, way):
                    continue
                value = held[pl.ds(row_of(f, slot_at(way, far)), FLOW), :]
                for beyond in {1: (2,), 2: (3, 4)}.get(far, ()):
                    if beyond <= hops(f, way):
                        before = slot_of(f, way, beyond, flows)
                        copy(rbuf.at[before], rbuf.at[before], phase, partner, sem_of(sems, f, way, beyond, flows)).wait_recv()
                        value = value + rbuf[before, :].astype(F32)
                sem = sem_of(sems, f, way, far, flows)
                if f in last[3] and far == 1:
                    sbuf1, rbuf1, phase1, _ = last
                    slot = last_of(f, way, last)
                    sbuf1[slot, :] = value
                    copy(sbuf1.at[slot], rbuf1.at[slot], phase1, neighbour(way), sem).start()
                else:
                    slot = slot_of(f, way, far, flows)
                    sbuf[slot, :] = value.astype(BF16)
                    copy(sbuf.at[slot], rbuf.at[slot], phase, neighbour(way, 2 if far == 4 else 1), sem).start()

    def reduce_end(f, flows, row_of, held, rbuf, phase, sems, last):
        value = held[pl.ds(row_of(f, 0), FLOW), :]
        for way in (UP, DOWN):
            slot = slot_of(f, way, 1, flows)
            if f in last[3]:
                rbuf, phase, slot = last[1], last[2], last_of(f, way, last)
            copy(rbuf.at[slot], rbuf.at[slot], phase, partner, sem_of(sems, f, way, 1, flows)).wait_recv()
            value = value + rbuf[slot, :].astype(F32)
        return value

    def gather_step(far, which, flows, row_of, buf, phase, sems):
        for f in which:
            for way in (UP, DOWN):
                if far > hops(f, way):
                    continue
                rows = pl.ds(row_of(f, slot_at(1 - way, far)), FLOW)
                if far > 0:
                    copy(buf.at[rows], buf.at[rows], phase, partner, sem_of(sems, f, way, far, flows)).wait_recv()
                for distance in {0: (1,), 1: (1,), 2: (1, 2)}.get(far, ()):
                    if far + distance <= hops(f, way):
                        onto = pl.ds(row_of(f, slot_at(1 - way, far + distance)), FLOW)
                        sem = sem_of(sems, f, way, far + distance, flows)
                        copy(buf.at[rows], buf.at[onto], phase, neighbour(way, distance), sem).start()

    def mp_row(f, slot):
        return slot * 64 + (OWN, 0, FLOW)[f]

    def reduce_mp(held, sbuf, rbuf, bs, br, xs, xr, last, phases, sems, bsems):
        ring_phase, b_phase, x_phase = phases

        def send_across(slots):
            for slot in slots:
                rows = pl.ds(slot * FLOW, FLOW)
                bs[rows, :] = held[slot * 64 + 48 : slot * 64 + 64, :].astype(BF16)
                copy(bs.at[rows], br.at[rows], b_phase, across, bsems.at[slot]).start()

        def ring(far):
            reduce_step(far, (0, 1), 3, mp_row, held, sbuf, rbuf, ring_phase, sems, last)

        def met(slots):
            for slot in slots:
                rows = pl.ds(slot * FLOW, FLOW)
                copy(br.at[rows], br.at[rows], b_phase, partner, bsems.at[slot]).wait_recv()
                held[slot * 64 + FLOW : slot * 64 + 2 * FLOW, :] += br[rows, :].astype(F32)

        def cross(far):
            met((1,) if far == 4 else (slot_at(UP, far), slot_at(DOWN, far)))
            reduce_step(far, (2,), 3, mp_row, held, sbuf, rbuf, ring_phase, sems, last)

        def end_across():
            xs[...] = reduce_end(0, 3, mp_row, held, rbuf, ring_phase, sems, last)
            copy(xs, xr, x_phase, across).start()
            met((0,))

        def end():
            near = reduce_end(1, 3, mp_row, held, rbuf, ring_phase, sems, last)
            mixed = reduce_end(2, 3, mp_row, held, rbuf, ring_phase, sems, last)
            got(xr, x_phase)
            return jnp.concatenate([near + xr[...], mixed], axis=0)

        return send_across, ring, cross, end_across, end

    for load in loads[5:]:
        load.wait()

    pltpu.make_async_copy(x_ref, x_ref, lsem.at[7]).wait()

    def forward(g):
        rows = pl.ds(g * 128, 128)
        pre = dot(x_ref[rows, :], wi_ref[...])
        hp[rows, :] = pre
        a = gelu_tanh(pre).astype(BF16)
        act[rows, :] = a
        part[rows, :] = dot(a, wo_ref[...])

    rs1_across, rs1_ring, rs1_cross, rs1_end_across, rs1_end = reduce_mp(
        part, rs1s, rs1r, rs1bs, rs1br, rs1xs, rs1xr, (rs1ls, rs1lr, RS1L, (2,)), (RS1, RS1B, RS1X), rs1sem, rs1bsem
    )
    forward(0)
    rs1_across((1, 0))
    rs1_ring(4)
    forward(1)
    rs1_across((2, 3))
    rs1_ring(3)
    forward(2)
    rs1_across((4, 5))
    rs1_cross(4)
    text_on()
    rs1_ring(2)
    forward(3)
    rs1_across((6, 7))
    rs1_cross(3)
    rs1_ring(1)
    for g in range(4):
        xt[:, g * 128 : g * 128 + 128] = x_ref[g * 128 : g * 128 + 128, :].T
    pos = pos_ref[...]
    pos_hi = pos // 64
    line = lax.broadcasted_iota(jnp.int32, (8, ROWS), 0)
    table_rows = jnp.where(
        line == 0, pos_hi, jnp.where(line == 1, pos - pos_hi * 64, jnp.where(line == 2, ib_ref[...], 0))
    ).astype(F32).astype(BF16)
    took = lax.broadcasted_iota(jnp.int32, (ROWS, ROWS), 0)
    into = lax.broadcasted_iota(jnp.int32, (ROWS, ROWS), 1)
    slot = into // 64
    distance = jnp.where(lax.rem(slot, 2) == 0, 4 - slot // 2, slot // 2 + 4)
    distance = jnp.where(slot == 0, 0, jnp.where(slot == 1, 4, distance))
    right = took == (lax.rem(z + distance, 8) * 2 + xh) * OWN + lax.rem(into, OWN)
    first = lax.rem(into, 64) < OWN
    meta[...] = dot(table_rows, jnp.where(right & first, 1.0, 0.0).astype(BF16))
    meta_s[...] = dot(table_rows, jnp.where(right & jnp.logical_not(first), 1.0, 0.0).astype(BF16))

    copy(meta_s, meta_r, META, partner).start()
    rs1_cross(2)
    rs1_end_across()
    rs1_cross(1)
    features = rs1_end() + x_ref[:OWN, :].astype(F32)
    norm = row_norm(features)
    unit = features / norm

    img[:OWN, :] = unit.astype(BF16)
    def send_img(from_row, to_row, count, sem, distance):
        copy(
            img.at[pl.ds(from_row, count)], img.at[pl.ds(to_row, count)], AG1Z, z_peer(distance % 8), ag1sem.at[sem]
        ).start()

    def got_img(count, sem):
        copy(img.at[pl.ds(0, count)], img.at[pl.ds(0, count)], AG1Z, partner, ag1sem.at[sem]).wait_recv()

    for way, sign in ((UP, 1), (DOWN, -1)):
        send_img(0, slot_at(1 - way, 2) * 64, OWN, way, 2 * sign)
    for way, sign in ((UP, 1), (DOWN, -1)):
        send_img(0, slot_at(1 - way, 1) * 64, OWN, 2 + way, sign)

    def to_partner(slot):
        copy(
            img.at[pl.ds(slot * 64, OWN)], img.at[pl.ds(slot * 64 + OWN, OWN)], AG1C, partner, csem.at[slot // 2 + (4 if slot == 1 else 0)]
        ).start()

    def from_partner(far):
        count = OWN if far in (0, 4) else 2 * OWN
        copy(
            img.at[pl.ds(0, count)], img.at[pl.ds(0, count)], AG1C, partner, csem.at[0 if far == 0 else 4 - far if far < 4 else 4]
        ).wait_recv()

    to_partner(0)

    got(meta_r, META)
    meta[...] += meta_r[...]

    eye8 = lax.broadcasted_iota(jnp.int32, (8, 8), 0) == lax.broadcasted_iota(jnp.int32, (8, 8), 1)

    buckets = meta[2:3, :]
    weights = jnp.zeros((8, ROWS), F32)
    for k in range(8):
        column = jnp.sum(jnp.where(eye8, tab_ref[k : k + 1, :], 0.0), axis=1, keepdims=True)
        weights = weights + jnp.where(buckets == float(k), column, 0.0)
    hi = weights.astype(BF16).astype(F32)
    mid = (weights - hi).astype(BF16).astype(F32)
    low = weights - hi - mid
    hot[...] = jnp.concatenate([hi, mid, low, jnp.zeros((ext - 24, ROWS), F32)], axis=0).astype(BF16)
    meta[0:1, :] = meta[0:1, :] * 64.0 + meta[1:2, :]
    got(txt.at[pl.ds(0, 3 * 128)], TEXT2)

    loss_acc[...] = jnp.zeros_like(loss_acc)

    def pairs(g):
        images = pl.ds(g * 128, 128)

        logits = logit_scale * dot_nt(txt[:, :D], img[images, :]) + logit_bias
        weight = dot(txt[:, D:], hot[:, images])
        slot = lax.broadcasted_iota(jnp.int32, (ROWS, 1), 0)
        p = slot // OWN
        px, py = lax.rem(p, 4), p // 4
        index = (((lax.rem(px, 2) * 4 + py) * 2 + core) * 16 + z * 2 + px // 2) * OWN + lax.rem(slot, OWN)
        hit = index.astype(F32) == meta[0:1, images]
        against = jnp.where(hit, -logits, logits)
        grown = jnp.exp(against)
        loss_acc[...] += jnp.sum((weight * jnp.log(1.0 + grown)).reshape(ROWS // 8, 8, 128), axis=0)
        slope = logit_scale * weight * (grown / (1.0 + grown))
        coef[:, images] = jnp.where(hit, -slope, slope).astype(BF16)

    for way in (UP, DOWN):
        got_img(OWN, 2 + way)
        to_partner(slot_at(1 - way, 1))
    for way, sign in ((UP, 1), (DOWN, -1)):
        got_img(OWN, way)
        row = slot_at(1 - way, 2) * 64
        send_img(row, slot_at(1 - way, 3) * 64, OWN, 4 + way, sign)
        send_img(row + FLOW * way, 64 + FLOW * way, FLOW, 6 + way, 2 * sign)
    for way in (UP, DOWN):
        to_partner(slot_at(1 - way, 2))
    from_partner(1)
    pairs(3)
    for way in (UP, DOWN):
        got_img(OWN, 4 + way)
        to_partner(slot_at(1 - way, 3))
    from_partner(2)
    pairs(2)
    for way in (UP, DOWN):
        got_img(FLOW, 6 + way)
    to_partner(1)
    from_partner(3)
    pairs(1)
    from_partner(0)
    from_partner(4)
    pairs(0)

    def image_grad(g):
        rows = pl.ds(g * 128, 128)
        ig[rows, :] = dot_tn(coef[:, rows], txt[:, :D])
        to = pl.ds(g * 64, 64)
        for slot in (2 * g, 2 * g + 1):
            c_send[slot * OWN : slot * OWN + OWN, :] = ig[slot * 64 + OWN : slot * 64 + 64, :]
        copy(c_send.at[to], c_recv.at[to], RS2C, partner, csem.at[5 + g]).start()

    def both_cores(g):
        to = pl.ds(g * 64, 64)
        copy(c_send.at[to], c_recv.at[to], RS2C, partner, csem.at[5 + g]).wait_recv()
        for slot in (2 * g, 2 * g + 1):
            rows = pl.ds(slot * OWN, OWN)
            held[rows, :] = ig[slot * 64 : slot * 64 + OWN, :] + c_recv[rows, :]

    def send_rs2(value, sem, distance):
        rows = pl.ds(sem * OWN, value.shape[0])
        rs2s[rows, :] = value.astype(BF16)
        copy(rs2s.at[rows], rs2r.at[rows], RS2Z, z_peer(distance % 8), rs2sem.at[sem]).start()

    def got_rs2(sem, count=OWN):
        rows = pl.ds(sem * OWN, count)
        copy(rs2r.at[rows], rs2r.at[rows], RS2Z, partner, rs2sem.at[sem]).wait_recv()
        return rs2r[rows, :].astype(F32)

    def held_at(way, far):
        row = slot_at(way, far) * OWN
        return held[row : row + OWN, :]

    image_grad(0)
    image_grad(1)
    both_cores(0)
    far4 = held_at(UP, 4)
    send_rs2(far4[:FLOW], 0, 2)
    send_rs2(far4[FLOW:], 1, -2)
    image_grad(2)
    both_cores(1)
    send_rs2(held_at(UP, 3), 2, 1)
    send_rs2(held_at(DOWN, 3), 3, -1)
    image_grad(3)
    both_cores(2)
    both_cores(3)
    send_rs2(held_at(UP, 1), 6, 1)
    send_rs2(held_at(DOWN, 1), 7, -1)

    def text_grad(j, _):
        b = lax.rem(y + j, 4)
        rows = rows_at(b * 128, 128, 128)
        tgs[rows, :] = dot(coef[rows, :], img[...]).astype(BF16)
        copy(tgs.at[rows], tgr.at[rows_at((j - 1) * 128, 128, 128)], TG, plane_dev(x, b)).start()
        return 0

    lax.fori_loop(1, 3, text_grad, 0)
    far2 = held_at(UP, 2) + got_rs2(2)
    send_rs2(jnp.concatenate([far2[:FLOW] + got_rs2(0, FLOW), far2[FLOW:]], axis=0), 4, 2)
    far2 = held_at(DOWN, 2) + got_rs2(3)
    send_rs2(jnp.concatenate([far2[:FLOW], far2[FLOW:] + got_rs2(1, FLOW)], axis=0), 5, -2)
    text_grad(3, 0)
    tgo[...] = dot(coef[rows_at(y * 128, 128, 128), :], img[...])

    def text_grad_on():
        got(tgr, TG)
        tgo[...] += tgr[0:128, :].astype(F32) + tgr[128:256, :].astype(F32) + tgr[256:384, :].astype(F32)

        def send(j, _):
            x2 = lax.rem(x + j, 4)
            rows = rows_at(x2 * OWN, OWN, OWN)
            tgs2[rows, :] = tgo[rows, :].astype(BF16)
            copy(tgs2.at[rows], tgr2.at[rows_at((j - 1) * OWN, OWN, OWN)], TG2, plane_dev(x2, y)).start()
            return 0

        lax.fori_loop(1, 4, send, 0)

    l_tile[...] = jnp.zeros((8, 128), F32) + jnp.sum(loss_acc[...])

    def send_loss(j, _):
        copy(l_tile, l1r.at[rows_at((j - 1) * 8, 8, 8)], LOSS1, plane_peer(j)).start()
        return 0

    lax.fori_loop(1, 16, send_loss, 0)

    own_grad = held[0:OWN, :] + got_rs2(6) + got_rs2(7) + got_rs2(4) + got_rs2(5)
    projected = jnp.sum(unit * own_grad, axis=-1, keepdims=True)
    grad_features = (own_grad - unit * projected) / norm
    gfall[:OWN, :] = grad_features.astype(BF16)
    def cross_gf(slot):
        copy(
            gfall.at[pl.ds(slot * 64 + FLOW, FLOW)], gfall.at[pl.ds(slot * 64 + 48, FLOW)], AG2X, across, ag2bsem.at[slot]
        ).start()

    def crossed_gf(slots):
        for slot in slots:
            rows = pl.ds(slot * 64 + 48, FLOW)
            copy(gfall.at[rows], gfall.at[rows], AG2X, partner, ag2bsem.at[slot]).wait_recv()

    def ag2_step(far, which):
        gather_step(far, which, 3, mp_row, gfall, AG2, ag2sem)

    def near_step(far):
        ag2_step(far, (2, 1))
        for slot in (1,) if far == 4 else (slot_at(UP, far), slot_at(DOWN, far)):
            cross_gf(slot)

    other_rows = pl.ds(OWN, FLOW)
    copy(gfall.at[pl.ds(0, FLOW)], gfall.at[other_rows], AG2X, across).start()
    ag2_step(0, (2, 1))
    cross_gf(0)
    near_step(1)
    got(gfall.at[other_rows], AG2X)
    ag2_step(0, (0,))
    near_step(2)

    def backward(g):
        rows = pl.ds(g * 128, 128)
        gh[rows, :] = (dot_nt(gfall[rows, :], wo_ref[...]) * gelu_slope(hp[rows, :])).astype(BF16)

    def to_input(g):
        rows = pl.ds(g * 128, 128)
        part[rows, :] = dot_nt(gh[rows, :], wi_ref[...])

    rs3_across, rs3_ring, rs3_cross, rs3_end_across, rs3_end = reduce_mp(
        part, rs3s, rs3r, rs3bs, rs3br, rs3xs, rs3xr, (rs3ls, rs3lr, RS3L, (0, 1, 2)), (RS3, RS3B, RS3X), rs3sem, rs3bsem
    )

    other_cols, own_cols = rows_at((1 - core) * 128, 128, 128), rows_at(core * 128, 128, 128)
    late, early = pl.ds(0, 256), pl.ds(256, 256)

    def w_in_half(cols, out, kind):
        out[...] = (swi[:, cols] + dot(xt[:, late], gh[late, cols])).astype(kind)

    ag2_step(1, (0,))
    crossed_gf((6, 7))
    backward(3)
    near_step(3)
    ag2_step(2, (0,))
    crossed_gf((4, 5))
    backward(2)
    swo[...] = dot_tn(act[early, :], gfall[early, :])
    near_step(4)
    ag2_step(3, (0,))
    swi[...] = dot(xt[:, early], gh[early, :])
    crossed_gf((2, 3))
    backward(1)
    to_input(2)
    to_input(3)
    to_input(1)
    text_grad_on()
    ag2_step(4, (0,))
    crossed_gf((0, 1))
    arc_so[...] = (swo[other_cols, :] + dot_tn(act[late, other_cols], gfall[late, :])).astype(BF16)
    copy(arc_so, arc_ro, ARC_O, partner).start()
    backward(0)
    w_in_half(other_cols, arc_si, BF16)
    copy(arc_si, arc_ri, ARC_I, partner).start()
    to_input(0)
    rs3_across((1, 2, 3))
    rs3_ring(4)
    rs3_across((4, 5, 6, 7, 0))
    awo[...] = swo[own_cols, :] + dot_tn(act[late, own_cols], gfall[late, :])
    got(arc_ro, ARC_O)
    awo[...] += arc_ro[...].astype(F32)
    ars_so[...] = awo[...].astype(BF16)

    def send_ars_out(j, _):
        device, q = ar_peer(j)
        copy(ars_so.at[rows_at(q * 16, 16, 16)], ars_ro.at[rows_at((j - 1) * 16, 16, 16)], ARS_O, device).start()
        return 0

    lax.fori_loop(1, 8, send_ars_out, 0)
    w_in_half(own_cols, awi, F32)
    got(arc_ri, ARC_I)
    awi[...] += arc_ri[...].astype(F32)
    ars_si[...] = awi[...].astype(BF16)

    def send_ars_in(j, _):
        device, q = ar_peer(j)
        copy(ars_si.at[rows_at(q * 144, 144, 144)], ars_ri.at[rows_at((j - 1) * 144, 144, 144)], ARS_I, device).start()
        return 0

    lax.fori_loop(1, 8, send_ars_in, 0)
    rs3_ring(3)
    rs3_cross(4)
    got(l1r, LOSS1)
    loss = l_tile[...]
    for j in range(15):
        loss = loss + l1r[j * 8 : j * 8 + 8, :]
    lc_tile[...] = loss
    copy(lc_tile, lcr, LOSSC, partner).start()

    rs3_ring(2)
    rs3_cross(3)
    got(lcr, LOSSC)
    lz_tile[...] = loss + lcr[...]

    def send_loss_z(j, _):
        copy(lz_tile, lzr.at[rows_at((j - 1) * 8, 8, 8)], LOSSZ, z_peer(j)).start()
        return 0

    lax.fori_loop(1, 8, send_loss_z, 0)
    rs3_ring(1)
    rs3_cross(2)

    q = y * 2 + xl
    own_in, own_out = rows_at(q * 144, 144, 144), rows_at(q * 16, 16, 16)
    total_in, total_out = awi[own_in, :], awo[own_out, :]
    got(ars_ro, ARS_O)
    for j in range(7):
        total_out = total_out + ars_ro[j * 16 : j * 16 + 16, :].astype(F32)
    fwo[core, own_out, :] = total_out.astype(BF16)

    def send_aag_out(j, _):
        device, _ = ar_peer(j)
        copy(fwo.at[core, own_out], fwo.at[core, own_out], AAG_O, device, aagsem.at[7 + j]).start()
        return 0

    lax.fori_loop(1, 8, send_aag_out, 0)
    copy(fwo.at[core, own_out], fwo.at[core, own_out], AFC_O, partner).start()
    got(ars_ri, ARS_I)
    for j in range(7):
        total_in = total_in + ars_ri[j * 144 : j * 144 + 144, :].astype(F32)
    fwi[core, own_in, :] = total_in.astype(BF16)

    def send_aag_in(j, _):
        device, _ = ar_peer(j)
        copy(fwi.at[core, own_in], fwi.at[core, own_in], AAG_I, device, aagsem.at[j - 1]).start()
        return 0

    lax.fori_loop(1, 8, send_aag_in, 0)
    copy(fwi.at[core, own_in], fwi.at[core, own_in], AFC_I, partner).start()
    rs3_end_across()
    rs3_cross(1)
    grad_image = rs3_end() + grad_features

    got(tgr2, TG2)
    grad_text = tgo[rows_at(x * OWN, OWN, OWN), :]
    for j in range(3):
        grad_text = grad_text + tgr2[j * OWN : j * OWN + OWN, :].astype(F32)
    gt_ref[...] = grad_text
    got(lzr, LOSSZ)
    loss = lz_tile[...]
    for j in range(7):
        loss = loss + lzr[j * 8 : j * 8 + 8, :]
    loss_ref[...] = loss * (1.0 / PAIRS)

    def weights_on(j, _):
        xl2, y2 = lax.rem(xl + lax.rem(j, 2), 2), lax.rem(y + 4 - j // 2, 4)
        q2 = y2 * 2 + xl2
        out, into = rows_at(q2 * 16, 16, 16), rows_at(q2 * 144, 144, 144)
        copy(fwo.at[core, out], fwo.at[core, out], AAG_O, partner, aagsem.at[7 + j]).wait_recv()
        copy(fwo.at[core, out], fwo.at[core, out], AFC_O, partner).start()
        copy(fwi.at[core, into], fwi.at[core, into], AAG_I, partner, aagsem.at[j - 1]).wait_recv()
        copy(fwi.at[core, into], fwi.at[core, into], AFC_I, partner).start()
        return 0

    lax.fori_loop(1, 8, weights_on, 0)
    gi_ref[...] = grad_image
    got(fwo.at[1 - core], AFC_O)
    for half in range(2):
        gwo_ref[half * 128 : half * 128 + 128, :] = fwo[half]
    got(fwi.at[1 - core], AFC_I)
    for half in range(2):
        gwi_ref[:, half * 128 : half * 128 + 128] = fwi[half]

    sent(txt.at[pl.ds(0, 3 * OWN)], TEXT)
    sent(txt.at[pl.ds(0, 3 * 128)], TEXT2)
    sent(meta_s, META)
    sent(rs1s.at[pl.ds(0, 19 * FLOW)], RS1)
    sent(rs1bs, RS1B)
    sent(rs1ls, RS1L)
    sent(rs1xs, RS1X)
    sent(img.at[pl.ds(0, 14 * FLOW)], AG1Z)
    sent(img.at[pl.ds(0, 8 * OWN)], AG1C)
    sent(c_send, RS2C)
    sent(rs2s.at[pl.ds(0, 14 * FLOW)], RS2Z)
    sent(tgr, TG)
    sent(tgr2, TG2)
    sent(l1r, LOSS1)
    sent(lc_tile, LOSSC)
    sent(lzr, LOSSZ)
    sent(gfall.at[pl.ds(0, 21 * FLOW)], AG2)
    sent(gfall.at[pl.ds(0, 9 * FLOW)], AG2X)
    sent(rs3s.at[pl.ds(0, 15 * FLOW)], RS3)
    sent(rs3bs, RS3B)
    sent(rs3ls, RS3L)
    sent(rs3xs, RS3X)
    sent(arc_si, ARC_I)
    sent(arc_so, ARC_O)
    sent(ars_ri, ARS_I)
    sent(ars_ro, ARS_O)
    sent(fwi.at[0, pl.ds(0, 7 * 144)], AAG_I)
    sent(fwo.at[0, pl.ds(0, 7 * 16)], AAG_O)
    sent(fwi.at[0], AFC_I)
    sent(fwo.at[0], AFC_O)


def widen(loss_in, gt_in, gi_in, gwi_in, gwo_in, loss_ref, gt_ref, gi_ref, gwi_ref, gwo_ref):
    loss_ref[0, 0] = jnp.max(loss_in[...])
    gt_ref[...] = gt_in[...]
    gi_ref[...] = gi_in[...]
    gwi_ref[...] = gwi_in[...].astype(F32)
    gwo_ref[...] = gwo_in[...].astype(F32)


def per_device(
    image_feats, text_feats, w_in, w_out, image_bucket, text_bucket, positive, reward_table
):
    vmem = pl.BlockSpec(memory_space=pltpu.VMEM)

    def buf(shape, kind=BF16):
        return pltpu.VMEM(shape, kind)

    scratch = [
        buf((ROWS, D)),
        buf((OWN, D)),
        buf((D, HID)),
        buf((HID, D)),
        buf((1, ROWS), jnp.int32),
        buf((1, OWN), jnp.int32),
        buf((1, ROWS), jnp.int32),
        buf((8, 8), F32),
        buf((D, ROWS)),
        buf((ROWS, HID), F32),
        buf((ROWS, HID)),
        buf((ROWS, D), F32),
        buf((ROWS, D)),
        buf((ROWS, D)),
        buf((8 * FLOW, D)),
        buf((8 * FLOW, D)),
        buf((2 * FLOW, D), F32),
        buf((2 * FLOW, D), F32),
        buf((FLOW, D), F32),
        buf((FLOW, D), F32),
        buf((ROWS, D + ext)),
        buf((8, ROWS), F32),
        buf((8, ROWS), F32),
        buf((8, ROWS), F32),
        buf((ext, ROWS)),
        buf((ROWS, D)),
        buf((ROWS, ROWS)),
        buf((8, 128), F32),
        buf((256, D), F32),
        buf((256, D), F32),
        buf((ROWS, D), F32),
        buf((256, D), F32),
        buf((256, D)),
        buf((256, D)),
        buf((ROWS, D)),
        buf((3 * 128, D)),
        buf((128, D), F32),
        buf((128, D)),
        buf((3 * OWN, D)),
        buf((8, 128), F32),
        buf((15 * 8, 128), F32),
        buf((8, 128), F32),
        buf((8, 128), F32),
        buf((8, 128), F32),
        buf((7 * 8, 128), F32),
        buf((ROWS, D)),
        buf((ROWS, HID)),
        buf((D, HID), F32),
        buf((HID, D), F32),
        buf((ROWS, D)),
        buf((ROWS, D)),
        buf((8 * FLOW, D)),
        buf((8 * FLOW, D)),
        buf((6 * FLOW, D), F32),
        buf((6 * FLOW, D), F32),
        buf((FLOW, D), F32),
        buf((FLOW, D), F32),
        buf((D, 128)),
        buf((128, D)),
        buf((D, 128)),
        buf((128, D)),
        buf((D, 128), F32),
        buf((128, D), F32),
        buf((D, 128)),
        buf((128, D)),
        buf((7 * 144, 128)),
        buf((7 * 16, D)),
        buf((2, D, 128)),
        buf((2, 128, D)),
        pltpu.SemaphoreType.DMA((8,)),
        pltpu.SemaphoreType.DMA((30,)),
        pltpu.SemaphoreType.DMA((30,)),
        pltpu.SemaphoreType.DMA((9,)),
        pltpu.SemaphoreType.DMA((24,)),
        pltpu.SemaphoreType.DMA((8,)),
        pltpu.SemaphoreType.DMA((8,)),
        pltpu.SemaphoreType.DMA((24,)),
        pltpu.SemaphoreType.DMA((24,)),
        pltpu.SemaphoreType.DMA((8,)),
        pltpu.SemaphoreType.DMA((8,)),
        pltpu.SemaphoreType.DMA((8,)),
        pltpu.SemaphoreType.DMA((15,)),
    ]
    partial = pl.pallas_call(
        kernel,
        out_shape=(
            jax.ShapeDtypeStruct((8, 128), F32),
            jax.ShapeDtypeStruct((OWN, D), F32),
            jax.ShapeDtypeStruct((OWN, D), F32),
            jax.ShapeDtypeStruct((D, HID), BF16),
            jax.ShapeDtypeStruct((HID, D), BF16),
        ),
        in_specs=[pl.BlockSpec(memory_space=pltpu.HBM)] * 8,
        out_specs=(vmem,) * 5,
        scratch_shapes=scratch,
        compiler_params=pltpu.CompilerParams(
            collective_id=0, has_side_effects=True, vmem_limit_bytes=VMEM_LIMIT
        ),
        name="pairs_and_block",
    )(
        image_feats, text_feats, w_in, w_out, image_bucket[None, :], text_bucket[None, :], positive[None, :],
        reward_table,
    )
    loss, grad_text, grad_image, grad_w_in, grad_w_out = pl.pallas_call(
        widen,
        out_shape=(
            jax.ShapeDtypeStruct((1, 1), F32),
            jax.ShapeDtypeStruct((OWN, D), F32),
            jax.ShapeDtypeStruct((OWN, D), F32),
            jax.ShapeDtypeStruct((D, HID), F32),
            jax.ShapeDtypeStruct((HID, D), F32),
        ),
        in_specs=[vmem] * 5,
        out_specs=(pl.BlockSpec(memory_space=pltpu.SMEM),) + (vmem,) * 4,
        compiler_params=pltpu.CompilerParams(vmem_limit_bytes=VMEM_LIMIT),
        name="widen",
    )(*partial)
    return (loss.reshape(()), grad_text, grad_image, grad_w_in, grad_w_out)


def solution(mesh):
    return jax.shard_map(
        per_device,
        mesh=mesh,
        in_specs=(
            P("dp", None),
            P(("dp", "mp"), None),
            P(None, "mp"),
            P("mp", None),
            P("dp"),
            P(("dp", "mp")),
            P("dp"),
            P(),
        ),
        out_specs=(P(), P(("dp", "mp"), None), P(("dp", "mp"), None), P(None, "mp"), P("mp", None)),
        check_vma=False,
    )
```

```python
import jax
import jax.numpy as jnp
from jax import lax
from jax.experimental import pallas as pl
from jax.experimental.pallas import tpu as pltpu
from jax.sharding import PartitionSpec as P

MESH = pl.DeviceIdType.MESH
F32 = jnp.float32
BF16 = jnp.bfloat16

logit_scale = 4.0
logit_bias = -2.0
norm_eps = 1e-06
root_coef = 0.7978845608028654
cubic_coef = 0.044715

D = 1152
ROWS = 512
OWN = 32
HID = 256
PAIRS = 8192.0 * 8192.0
ext = 128
VMEM_LIMIT = 60 * 2**20

NT = (((1,), (1,)), ((), ()))
TN = (((0,), (0,)), ((), ()))


def dot(a, b):
    return jnp.dot(a, b, preferred_element_type=F32)


def dot_nt(a, b):
    return lax.dot_general(a, b, NT, preferred_element_type=F32)


def dot_tn(a, b):
    return lax.dot_general(a, b, TN, preferred_element_type=F32)


def gelu_tanh(v):
    return 0.5 * v * (1.0 + jnp.tanh(root_coef * (v + cubic_coef * v * v * v)))


def gelu_slope(v):
    t = jnp.tanh(root_coef * (v + cubic_coef * v * v * v))
    return 0.5 * (1.0 + t) + 0.5 * v * (1.0 - t * t) * root_coef * (1.0 + 3.0 * cubic_coef * v * v)


def row_norm(v):
    return jnp.sqrt(jnp.sum(v * v, axis=-1, keepdims=True) + norm_eps)


(TEXT, TEXT2, META, RS1, RS1B, RS1X, AG1C, RS2C, RS2Z, TG, TG2, LOSS1, LOSSC, LOSSZ, AG2, AG2X, RS3, RS3X, ARC_I, ARC_O, ARS_I, ARS_O,
 AAG_I, AAG_O, AFC_I, AFC_O, AG1Z, RS1L) = range(28)
FLOW = 16
UP, DOWN = 0, 1
SLOTS = ((0, UP), (4, UP), (3, UP), (3, DOWN), (2, UP), (2, DOWN), (1, UP), (1, DOWN))


def slot_at(way, far):
    return 0 if far == 0 else 1 if far == 4 else 8 - 2 * far + way


def rows_at(start, count, step):
    return pl.ds(pl.multiple_of(start, step), count)


def kernel(
    x_hbm, t_hbm, wi_hbm, wo_hbm, ib_hbm, tb_hbm, pos_hbm, tab_hbm,
    loss_ref, gt_ref, gi_ref, gwi_ref, gwo_ref,
    x_ref, t_ref, wi_ref, wo_ref, ib_ref, tb_ref, pos_ref, tab_ref,
    xt, hp, act, part, rs1s, rs1r, rs1bs, rs1br, rs1ls, rs1lr, rs1xs, rs1xr, txt, meta, meta_s, meta_r, hot, img, coef, loss_acc, c_send, c_recv, ig, held, rs2s, rs2r, tgs, tgr, tgo, tgs2, tgr2,
    l_tile, l1r, lc_tile, lcr, lz_tile, lzr, gfall, gh, swi, swo, rs3s, rs3r, rs3xs, rs3xr,
    arc_si, arc_so, arc_ri, arc_ro, awi, awo, ars_si, ars_so, ars_ri, ars_ro, fwi, fwo,
    lsem, ssem, rsem, csem, rs1sem, ag1sem, rs2sem, ag2sem, rs3sem, rs1bsem, ag2bsem, aagsem,
):
    dp, mp = lax.axis_index("dp"), lax.axis_index("mp")
    core, y, xl = lax.rem(dp, 2), lax.rem(dp // 2, 4), dp // 8
    xh, z = lax.rem(mp, 2), mp // 2
    x = xh * 2 + xl
    partner = (dp + 1 - 2 * core, mp)

    across = (dp, mp + 1 - 2 * xh)

    def z_peer(j):
        return (dp, lax.rem(z + j, 8) * 2 + xh)

    def plane_dev(x2, y2):
        return ((lax.rem(x2, 2) * 4 + y2) * 2 + core, z * 2 + x2 // 2)

    def ar_peer(j):
        xl2, y2 = lax.rem(xl + lax.rem(j, 2), 2), lax.rem(y + j // 2, 4)
        return ((xl2 * 4 + y2) * 2 + core, mp), y2 * 2 + xl2

    def plane_peer(j):
        return plane_dev(lax.rem(x + lax.rem(j, 4), 4), lax.rem(y + j // 4, 4))

    def copy(src, dst, phase, device, recv=None):
        return pltpu.make_async_remote_copy(
            src_ref=src, dst_ref=dst, send_sem=ssem.at[phase],
            recv_sem=rsem.at[phase] if recv is None else recv, device_id=device, device_id_type=MESH,
        )

    def got(ref, phase):
        copy(ref, ref, phase, partner).wait_recv()

    def sent(ref, phase):
        copy(ref, ref, phase, partner).wait_send()

    def hops(f, way):
        return 4 if f % 2 == way else 3

    def neighbour(way, distance=1):
        return z_peer(distance if way == UP else 8 - distance)

    def toward(way, far):
        return lax.rem(z + (far if way == UP else 8 - far), 8)

    barrier = pltpu.get_barrier_semaphore()

    def greet(j, _):
        pl.semaphore_signal(barrier, inc=1, device_id=plane_peer(j), device_id_type=MESH)
        return 0

    lax.fori_loop(1, 16, greet, 0)

    def greet_z(j, _):
        pl.semaphore_signal(barrier, inc=1, device_id=z_peer(j), device_id_type=MESH)
        return 0

    lax.fori_loop(1, 8, greet_z, 0)
    pl.semaphore_signal(barrier, inc=1, device_id=partner, device_id_type=MESH)

    loads = [
        pltpu.make_async_copy(src, dst, lsem.at[i])
        for i, (src, dst) in enumerate(
            (
                (t_hbm, t_ref), (tb_hbm, tb_ref), (pos_hbm, pos_ref), (ib_hbm, ib_ref), (tab_hbm, tab_ref),
                (wi_hbm, wi_ref), (wo_hbm, wo_ref),
            )
        )
    ]
    for load in loads:
        load.start()
    for far, way in SLOTS:
        for other in (0, 1):
            from_rows = rows_at((toward(way, far) * 2 + (1 - xh if other else xh)) * OWN, OWN, OWN)
            to_rows = pl.ds(slot_at(way, far) * 64 + other * OWN, OWN)
            pltpu.make_async_copy(x_hbm.at[from_rows], x_ref.at[to_rows], lsem.at[7]).start()
    for load in loads[:5]:
        load.wait()

    own_slot = y * 4 + x
    own_text = rows_at(own_slot * OWN, OWN, OWN)
    wide = t_ref[...].astype(F32)
    txt[own_text, :D] = (wide / row_norm(wide)).astype(BF16)
    eye = lax.broadcasted_iota(jnp.int32, (OWN, OWN), 0) == lax.broadcasted_iota(jnp.int32, (OWN, OWN), 1)
    tb_col = jnp.sum(jnp.where(eye, tb_ref[...].astype(F32), 0.0), axis=1, keepdims=True)
    lane = lax.broadcasted_iota(jnp.int32, (OWN, ext), 1)
    level = jnp.where(lane < 24, lax.rem(lane, 8), -1).astype(F32)
    txt[own_text, D:] = jnp.where(level == tb_col, 1.0, 0.0).astype(BF16)

    pl.semaphore_wait(barrier, 23)

    def send_text(j, _):
        device = plane_dev(lax.rem(x + j, 4), y)
        copy(txt.at[own_text], txt.at[own_text], TEXT, device).start()
        return 0

    lax.fori_loop(1, 4, send_text, 0)

    def text_on():
        got(txt.at[pl.ds(0, 3 * OWN)], TEXT)
        rows = rows_at(y * 128, 128, 128)

        def send(j, _):
            copy(txt.at[rows], txt.at[rows], TEXT2, plane_dev(x, lax.rem(y + j, 4))).start()
            return 0

        lax.fori_loop(1, 4, send, 0)

    def slot_of(f, way, far, flows):
        return pl.ds(((way * flows + f) * 4 + far - 1) * FLOW, FLOW)

    def sem_of(sems, f, way, far, flows):
        return sems.at[(way * flows + f) * 4 + far - 1]

    def last_of(f, way, last):
        return pl.ds((way + 2 * last[3].index(f)) * FLOW, FLOW)

    def reduce_step(far, which, flows, row_of, held, sbuf, rbuf, phase, sems, last):
        for f in which:
            for way in (UP, DOWN):
                if far > hops(f, way):
                    continue
                value = held[pl.ds(row_of(f, slot_at(way, far)), FLOW), :]
                for beyond in {1: (2,), 2: (3, 4)}.get(far, ()):
                    if beyond <= hops(f, way):
                        before = slot_of(f, way, beyond, flows)
                        copy(rbuf.at[before], rbuf.at[before], phase, partner, sem_of(sems, f, way, beyond, flows)).wait_recv()
                        value = value + rbuf[before, :].astype(F32)
                sem = sem_of(sems, f, way, far, flows)
                if f in last[3] and far == 1:
                    sbuf1, rbuf1, phase1, _ = last
                    slot = last_of(f, way, last)
                    sbuf1[slot, :] = value
                    copy(sbuf1.at[slot], rbuf1.at[slot], phase1, neighbour(way), sem).start()
                else:
                    slot = slot_of(f, way, far, flows)
                    sbuf[slot, :] = value.astype(BF16)
                    copy(sbuf.at[slot], rbuf.at[slot], phase, neighbour(way, 2 if far == 4 else 1), sem).start()

    def reduce_end(f, flows, row_of, held, rbuf, phase, sems, last):
        value = held[pl.ds(row_of(f, 0), FLOW), :]
        for way in (UP, DOWN):
            slot = slot_of(f, way, 1, flows)
            if f in last[3]:
                rbuf, phase, slot = last[1], last[2], last_of(f, way, last)
            copy(rbuf.at[slot], rbuf.at[slot], phase, partner, sem_of(sems, f, way, 1, flows)).wait_recv()
            value = value + rbuf[slot, :].astype(F32)
        return value

    def gather_step(far, which, flows, row_of, buf, phase, sems):
        for f in which:
            for way in (UP, DOWN):
                if far > hops(f, way):
                    continue
                rows = pl.ds(row_of(f, slot_at(1 - way, far)), FLOW)
                if far > 0:
                    copy(buf.at[rows], buf.at[rows], phase, partner, sem_of(sems, f, way, far, flows)).wait_recv()
                for distance in {0: (1,), 1: (1,), 2: (1, 2)}.get(far, ()):
                    if far + distance <= hops(f, way):
                        onto = pl.ds(row_of(f, slot_at(1 - way, far + distance)), FLOW)
                        sem = sem_of(sems, f, way, far + distance, flows)
                        copy(buf.at[rows], buf.at[onto], phase, neighbour(way, distance), sem).start()

    def mp_row(f, slot):
        return slot * 64 + (OWN, 0, FLOW, OWN + FLOW)[f]

    def reduce_mp(held, sbuf, rbuf, bs, br, xs, xr, last, phases, sems, bsems):
        ring_phase, b_phase, x_phase = phases

        def send_across(slots):
            for slot in slots:
                rows = pl.ds(slot * FLOW, FLOW)
                bs[rows, :] = held[slot * 64 + 48 : slot * 64 + 64, :].astype(BF16)
                copy(bs.at[rows], br.at[rows], b_phase, across, bsems.at[slot]).start()

        def ring(far):
            reduce_step(far, (0, 1), 3, mp_row, held, sbuf, rbuf, ring_phase, sems, last)

        def met(slots):
            for slot in slots:
                rows = pl.ds(slot * FLOW, FLOW)
                copy(br.at[rows], br.at[rows], b_phase, partner, bsems.at[slot]).wait_recv()
                held[slot * 64 + FLOW : slot * 64 + 2 * FLOW, :] += br[rows, :].astype(F32)

        def cross(far):
            met((1,) if far == 4 else (slot_at(UP, far), slot_at(DOWN, far)))
            reduce_step(far, (2,), 3, mp_row, held, sbuf, rbuf, ring_phase, sems, last)

        def end_across():
            xs[...] = reduce_end(0, 3, mp_row, held, rbuf, ring_phase, sems, last)
            copy(xs, xr, x_phase, across).start()
            met((0,))

        def end():
            near = reduce_end(1, 3, mp_row, held, rbuf, ring_phase, sems, last)
            mixed = reduce_end(2, 3, mp_row, held, rbuf, ring_phase, sems, last)
            got(xr, x_phase)
            return jnp.concatenate([near + xr[...], mixed], axis=0)

        return send_across, ring, cross, end_across, end

    for load in loads[5:]:
        load.wait()

    pltpu.make_async_copy(x_ref, x_ref, lsem.at[7]).wait()

    def forward(g):
        rows = pl.ds(g * 128, 128)
        pre = dot(x_ref[rows, :], wi_ref[...])
        hp[rows, :] = pre
        a = gelu_tanh(pre).astype(BF16)
        act[rows, :] = a
        part[rows, :] = dot(a, wo_ref[...])

    rs1_across, rs1_ring, rs1_cross, rs1_end_across, rs1_end = reduce_mp(
        part, rs1s, rs1r, rs1bs, rs1br, rs1xs, rs1xr, (rs1ls, rs1lr, RS1L, (2,)), (RS1, RS1B, RS1X), rs1sem, rs1bsem
    )
    forward(0)
    rs1_across((1, 0))
    rs1_ring(4)
    forward(1)
    rs1_across((2, 3))
    rs1_ring(3)
    forward(2)
    rs1_across((4, 5))
    rs1_cross(4)
    text_on()
    rs1_ring(2)
    forward(3)
    rs1_across((6, 7))
    rs1_cross(3)
    rs1_ring(1)
    for g in range(4):
        xt[:, g * 128 : g * 128 + 128] = x_ref[g * 128 : g * 128 + 128, :].T
    pos = pos_ref[...]
    pos_hi = pos // 64
    line = lax.broadcasted_iota(jnp.int32, (8, ROWS), 0)
    table_rows = jnp.where(
        line == 0, pos_hi, jnp.where(line == 1, pos - pos_hi * 64, jnp.where(line == 2, ib_ref[...], 0))
    ).astype(F32).astype(BF16)
    took = lax.broadcasted_iota(jnp.int32, (ROWS, ROWS), 0)
    into = lax.broadcasted_iota(jnp.int32, (ROWS, ROWS), 1)
    slot = into // 64
    distance = jnp.where(lax.rem(slot, 2) == 0, 4 - slot // 2, slot // 2 + 4)
    distance = jnp.where(slot == 0, 0, jnp.where(slot == 1, 4, distance))
    right = took == (lax.rem(z + distance, 8) * 2 + xh) * OWN + lax.rem(into, OWN)
    first = lax.rem(into, 64) < OWN
    meta[...] = dot(table_rows, jnp.where(right & first, 1.0, 0.0).astype(BF16))
    meta_s[...] = dot(table_rows, jnp.where(right & jnp.logical_not(first), 1.0, 0.0).astype(BF16))

    copy(meta_s, meta_r, META, partner).start()
    rs1_cross(2)
    rs1_end_across()
    rs1_cross(1)
    features = rs1_end() + x_ref[:OWN, :].astype(F32)
    norm = row_norm(features)
    unit = features / norm

    img[:OWN, :] = unit.astype(BF16)
    def send_img(from_row, to_row, count, sem, distance):
        copy(
            img.at[pl.ds(from_row, count)], img.at[pl.ds(to_row, count)], AG1Z, z_peer(distance % 8), ag1sem.at[sem]
        ).start()

    def got_img(count, sem):
        copy(img.at[pl.ds(0, count)], img.at[pl.ds(0, count)], AG1Z, partner, ag1sem.at[sem]).wait_recv()

    for way, sign in ((UP, 1), (DOWN, -1)):
        send_img(0, slot_at(1 - way, 2) * 64, OWN, way, 2 * sign)
    for way, sign in ((UP, 1), (DOWN, -1)):
        send_img(0, slot_at(1 - way, 1) * 64, OWN, 2 + way, sign)

    def to_partner(slot):
        copy(
            img.at[pl.ds(slot * 64, OWN)], img.at[pl.ds(slot * 64 + OWN, OWN)], AG1C, partner, csem.at[slot // 2 + (4 if slot == 1 else 0)]
        ).start()

    def from_partner(far):
        count = OWN if far in (0, 4) else 2 * OWN
        copy(
            img.at[pl.ds(0, count)], img.at[pl.ds(0, count)], AG1C, partner, csem.at[0 if far == 0 else 4 - far if far < 4 else 4]
        ).wait_recv()

    to_partner(0)

    got(meta_r, META)
    meta[...] += meta_r[...]

    eye8 = lax.broadcasted_iota(jnp.int32, (8, 8), 0) == lax.broadcasted_iota(jnp.int32, (8, 8), 1)

    buckets = meta[2:3, :]
    weights = jnp.zeros((8, ROWS), F32)
    for k in range(8):
        column = jnp.sum(jnp.where(eye8, tab_ref[k : k + 1, :], 0.0), axis=1, keepdims=True)
        weights = weights + jnp.where(buckets == float(k), column, 0.0)
    hi = weights.astype(BF16).astype(F32)
    mid = (weights - hi).astype(BF16).astype(F32)
    low = weights - hi - mid
    hot[...] = jnp.concatenate([hi, mid, low, jnp.zeros((ext - 24, ROWS), F32)], axis=0).astype(BF16)
    meta[0:1, :] = meta[0:1, :] * 64.0 + meta[1:2, :]
    got(txt.at[pl.ds(0, 3 * 128)], TEXT2)

    loss_acc[...] = jnp.zeros_like(loss_acc)

    def pairs(g):
        images = pl.ds(g * 128, 128)

        logits = logit_scale * dot_nt(txt[:, :D], img[images, :]) + logit_bias
        weight = dot(txt[:, D:], hot[:, images])
        slot = lax.broadcasted_iota(jnp.int32, (ROWS, 1), 0)
        p = slot // OWN
        px, py = lax.rem(p, 4), p // 4
        index = (((lax.rem(px, 2) * 4 + py) * 2 + core) * 16 + z * 2 + px // 2) * OWN + lax.rem(slot, OWN)
        hit = index.astype(F32) == meta[0:1, images]
        against = jnp.where(hit, -logits, logits)
        grown = jnp.exp(against)
        loss_acc[...] += jnp.sum((weight * jnp.log(1.0 + grown)).reshape(ROWS // 8, 8, 128), axis=0)
        slope = logit_scale * weight * (grown / (1.0 + grown))
        coef[:, images] = jnp.where(hit, -slope, slope).astype(BF16)

    for way in (UP, DOWN):
        got_img(OWN, 2 + way)
        to_partner(slot_at(1 - way, 1))
    for way, sign in ((UP, 1), (DOWN, -1)):
        got_img(OWN, way)
        row = slot_at(1 - way, 2) * 64
        send_img(row, slot_at(1 - way, 3) * 64, OWN, 4 + way, sign)
        send_img(row + FLOW * way, 64 + FLOW * way, FLOW, 6 + way, 2 * sign)
    for way in (UP, DOWN):
        to_partner(slot_at(1 - way, 2))
    from_partner(1)
    pairs(3)
    for way in (UP, DOWN):
        got_img(OWN, 4 + way)
        to_partner(slot_at(1 - way, 3))
    from_partner(2)
    pairs(2)
    for way in (UP, DOWN):
        got_img(FLOW, 6 + way)
    to_partner(1)
    from_partner(3)
    pairs(1)
    from_partner(0)
    from_partner(4)
    pairs(0)

    def image_grad(g):
        rows = pl.ds(g * 128, 128)
        ig[rows, :] = dot_tn(coef[:, rows], txt[:, :D])
        to = pl.ds(g * 64, 64)
        for slot in (2 * g, 2 * g + 1):
            c_send[slot * OWN : slot * OWN + OWN, :] = ig[slot * 64 + OWN : slot * 64 + 64, :]
        copy(c_send.at[to], c_recv.at[to], RS2C, partner, csem.at[5 + g]).start()

    def both_cores(g):
        to = pl.ds(g * 64, 64)
        copy(c_send.at[to], c_recv.at[to], RS2C, partner, csem.at[5 + g]).wait_recv()
        for slot in (2 * g, 2 * g + 1):
            rows = pl.ds(slot * OWN, OWN)
            held[rows, :] = ig[slot * 64 : slot * 64 + OWN, :] + c_recv[rows, :]

    def send_rs2(value, sem, distance):
        rows = pl.ds(sem * OWN, value.shape[0])
        rs2s[rows, :] = value.astype(BF16)
        copy(rs2s.at[rows], rs2r.at[rows], RS2Z, z_peer(distance % 8), rs2sem.at[sem]).start()

    def got_rs2(sem, count=OWN):
        rows = pl.ds(sem * OWN, count)
        copy(rs2r.at[rows], rs2r.at[rows], RS2Z, partner, rs2sem.at[sem]).wait_recv()
        return rs2r[rows, :].astype(F32)

    def held_at(way, far):
        row = slot_at(way, far) * OWN
        return held[row : row + OWN, :]

    image_grad(0)
    image_grad(1)
    both_cores(0)
    far4 = held_at(UP, 4)
    send_rs2(far4[:FLOW], 0, 2)
    send_rs2(far4[FLOW:], 1, -2)
    image_grad(2)
    both_cores(1)
    send_rs2(held_at(UP, 3), 2, 1)
    send_rs2(held_at(DOWN, 3), 3, -1)
    image_grad(3)
    both_cores(2)
    both_cores(3)
    send_rs2(held_at(UP, 1), 6, 1)
    send_rs2(held_at(DOWN, 1), 7, -1)

    def text_grad(j, _):
        b = lax.rem(y + j, 4)
        rows = rows_at(b * 128, 128, 128)
        tgs[rows, :] = dot(coef[rows, :], img[...]).astype(BF16)
        copy(tgs.at[rows], tgr.at[rows_at((j - 1) * 128, 128, 128)], TG, plane_dev(x, b)).start()
        return 0

    lax.fori_loop(1, 3, text_grad, 0)
    far2 = held_at(UP, 2) + got_rs2(2)
    send_rs2(jnp.concatenate([far2[:FLOW] + got_rs2(0, FLOW), far2[FLOW:]], axis=0), 4, 2)
    far2 = held_at(DOWN, 2) + got_rs2(3)
    send_rs2(jnp.concatenate([far2[:FLOW], far2[FLOW:] + got_rs2(1, FLOW)], axis=0), 5, -2)
    text_grad(3, 0)
    tgo[...] = dot(coef[rows_at(y * 128, 128, 128), :], img[...])

    def text_grad_on():
        got(tgr, TG)
        tgo[...] += tgr[0:128, :].astype(F32) + tgr[128:256, :].astype(F32) + tgr[256:384, :].astype(F32)

        def send(j, _):
            x2 = lax.rem(x + j, 4)
            rows = rows_at(x2 * OWN, OWN, OWN)
            tgs2[rows, :] = tgo[rows, :].astype(BF16)
            copy(tgs2.at[rows], tgr2.at[rows_at((j - 1) * OWN, OWN, OWN)], TG2, plane_dev(x2, y)).start()
            return 0

        lax.fori_loop(1, 4, send, 0)

    l_tile[...] = jnp.zeros((8, 128), F32) + jnp.sum(loss_acc[...])

    def send_loss(j, _):
        copy(l_tile, l1r.at[rows_at((j - 1) * 8, 8, 8)], LOSS1, plane_peer(j)).start()
        return 0

    lax.fori_loop(1, 16, send_loss, 0)

    own_grad = held[0:OWN, :] + got_rs2(6) + got_rs2(7) + got_rs2(4) + got_rs2(5)
    projected = jnp.sum(unit * own_grad, axis=-1, keepdims=True)
    grad_features = (own_grad - unit * projected) / norm
    gfall[:OWN, :] = grad_features.astype(BF16)
    def cross_gf(slot):
        copy(
            gfall.at[pl.ds(slot * 64 + FLOW, FLOW)], gfall.at[pl.ds(slot * 64 + 48, FLOW)], AG2X, across, ag2bsem.at[slot]
        ).start()

    def crossed_gf(slots):
        for slot in slots:
            rows = pl.ds(slot * 64 + 48, FLOW)
            copy(gfall.at[rows], gfall.at[rows], AG2X, partner, ag2bsem.at[slot]).wait_recv()

    def ag2_step(far, which):
        gather_step(far, which, 3, mp_row, gfall, AG2, ag2sem)

    def near_step(far):
        ag2_step(far, (2, 1))
        for slot in (1,) if far == 4 else (slot_at(UP, far), slot_at(DOWN, far)):
            cross_gf(slot)

    other_rows = pl.ds(OWN, FLOW)
    copy(gfall.at[pl.ds(0, FLOW)], gfall.at[other_rows], AG2X, across).start()
    ag2_step(0, (2, 1))
    cross_gf(0)
    near_step(1)
    got(gfall.at[other_rows], AG2X)
    ag2_step(0, (0,))
    near_step(2)

    def backward(g):
        rows = pl.ds(g * 128, 128)
        gh[rows, :] = (dot_nt(gfall[rows, :], wo_ref[...]) * gelu_slope(hp[rows, :])).astype(BF16)

    def to_input(g):
        rows = pl.ds(g * 128, 128)
        part[rows, :] = dot_nt(gh[rows, :], wi_ref[...])

    rs3_last = (None, None, None, ())

    def rs3_ring(far):
        reduce_step(far, (0, 3, 1, 2), 4, mp_row, part, rs3s, rs3r, RS3, rs3sem, rs3_last)

    def rs3_end(flows):
        return jnp.concatenate([reduce_end(f, 4, mp_row, part, rs3r, RS3, rs3sem, rs3_last) for f in flows], axis=0)

    other_cols, own_cols = rows_at((1 - core) * 128, 128, 128), rows_at(core * 128, 128, 128)
    late, early = pl.ds(0, 256), pl.ds(256, 256)

    def w_in_half(cols, out, kind):
        out[...] = (swi[:, cols] + dot(xt[:, late], gh[late, cols])).astype(kind)

    ag2_step(1, (0,))
    crossed_gf((6, 7))
    backward(3)
    near_step(3)
    ag2_step(2, (0,))
    crossed_gf((4, 5))
    backward(2)
    swo[...] = dot_tn(act[early, :], gfall[early, :])
    near_step(4)
    ag2_step(3, (0,))
    swi[...] = dot(xt[:, early], gh[early, :])
    crossed_gf((2, 3))
    backward(1)
    to_input(2)
    to_input(3)
    to_input(1)
    ag2_step(4, (0,))
    crossed_gf((0, 1))
    arc_so[...] = (swo[other_cols, :] + dot_tn(act[late, other_cols], gfall[late, :])).astype(BF16)
    copy(arc_so, arc_ro, ARC_O, partner).start()
    backward(0)
    w_in_half(other_cols, arc_si, BF16)
    copy(arc_si, arc_ri, ARC_I, partner).start()
    to_input(0)
    rs3_ring(4)
    rs3_ring(3)
    awo[...] = swo[own_cols, :] + dot_tn(act[late, own_cols], gfall[late, :])
    got(arc_ro, ARC_O)
    awo[...] += arc_ro[...].astype(F32)
    ars_so[...] = awo[...].astype(BF16)

    def send_ars_out(j, _):
        device, q = ar_peer(j)
        copy(ars_so.at[rows_at(q * 16, 16, 16)], ars_ro.at[rows_at((j - 1) * 16, 16, 16)], ARS_O, device).start()
        return 0

    lax.fori_loop(1, 8, send_ars_out, 0)
    w_in_half(own_cols, awi, F32)
    got(arc_ri, ARC_I)
    awi[...] += arc_ri[...].astype(F32)
    ars_si[...] = awi[...].astype(BF16)

    def send_ars_in(j, _):
        device, q = ar_peer(j)
        copy(ars_si.at[rows_at(q * 144, 144, 144)], ars_ri.at[rows_at((j - 1) * 144, 144, 144)], ARS_I, device).start()
        return 0

    lax.fori_loop(1, 8, send_ars_in, 0)
    text_grad_on()
    rs3_ring(2)
    got(l1r, LOSS1)
    loss = l_tile[...]
    for j in range(15):
        loss = loss + l1r[j * 8 : j * 8 + 8, :]
    lc_tile[...] = loss
    copy(lc_tile, lcr, LOSSC, partner).start()

    rs3_ring(1)

    q = y * 2 + xl
    own_in, own_out = rows_at(q * 144, 144, 144), rows_at(q * 16, 16, 16)
    total_in, total_out = awi[own_in, :], awo[own_out, :]
    got(ars_ro, ARS_O)
    for j in range(7):
        total_out = total_out + ars_ro[j * 16 : j * 16 + 16, :].astype(F32)
    fwo[core, own_out, :] = total_out.astype(BF16)

    def send_aag_out(j, _):
        device, _ = ar_peer(j)
        copy(fwo.at[core, own_out], fwo.at[core, own_out], AAG_O, device, aagsem.at[7 + j]).start()
        return 0

    lax.fori_loop(1, 8, send_aag_out, 0)
    copy(fwo.at[core, own_out], fwo.at[core, own_out], AFC_O, partner).start()
    got(ars_ri, ARS_I)
    for j in range(7):
        total_in = total_in + ars_ri[j * 144 : j * 144 + 144, :].astype(F32)
    fwi[core, own_in, :] = total_in.astype(BF16)

    def send_aag_in(j, _):
        device, _ = ar_peer(j)
        copy(fwi.at[core, own_in], fwi.at[core, own_in], AAG_I, device, aagsem.at[j - 1]).start()
        return 0

    lax.fori_loop(1, 8, send_aag_in, 0)
    copy(fwi.at[core, own_in], fwi.at[core, own_in], AFC_I, partner).start()
    got(lcr, LOSSC)
    lz_tile[...] = loss + lcr[...]

    def send_loss_z(j, _):
        copy(lz_tile, lzr.at[rows_at((j - 1) * 8, 8, 8)], LOSSZ, z_peer(j)).start()
        return 0

    lax.fori_loop(1, 8, send_loss_z, 0)
    rs3xs[...] = rs3_end((0, 3))
    copy(rs3xs, rs3xr, RS3X, across).start()
    grad_image = rs3_end((1, 2)) + grad_features

    def weights_on(j, _):
        xl2, y2 = lax.rem(xl + lax.rem(j, 2), 2), lax.rem(y + 4 - j // 2, 4)
        q2 = y2 * 2 + xl2
        out, into = rows_at(q2 * 16, 16, 16), rows_at(q2 * 144, 144, 144)
        copy(fwo.at[core, out], fwo.at[core, out], AAG_O, partner, aagsem.at[7 + j]).wait_recv()
        copy(fwo.at[core, out], fwo.at[core, out], AFC_O, partner).start()
        copy(fwi.at[core, into], fwi.at[core, into], AAG_I, partner, aagsem.at[j - 1]).wait_recv()
        copy(fwi.at[core, into], fwi.at[core, into], AFC_I, partner).start()
        return 0

    lax.fori_loop(1, 8, weights_on, 0)
    got(tgr2, TG2)
    grad_text = tgo[rows_at(x * OWN, OWN, OWN), :]
    for j in range(3):
        grad_text = grad_text + tgr2[j * OWN : j * OWN + OWN, :].astype(F32)
    gt_ref[...] = grad_text
    got(lzr, LOSSZ)
    loss = lz_tile[...]
    for j in range(7):
        loss = loss + lzr[j * 8 : j * 8 + 8, :]
    loss_ref[...] = loss * (1.0 / PAIRS)

    got(rs3xr, RS3X)
    gi_ref[...] = grad_image + rs3xr[...]
    got(fwo.at[1 - core], AFC_O)
    for half in range(2):
        gwo_ref[half * 128 : half * 128 + 128, :] = fwo[half]
    got(fwi.at[1 - core], AFC_I)
    for half in range(2):
        gwi_ref[:, half * 128 : half * 128 + 128] = fwi[half]

    sent(txt.at[pl.ds(0, 3 * OWN)], TEXT)
    sent(txt.at[pl.ds(0, 3 * 128)], TEXT2)
    sent(meta_s, META)
    sent(rs1s.at[pl.ds(0, 19 * FLOW)], RS1)
    sent(rs1bs, RS1B)
    sent(rs1ls, RS1L)
    sent(rs1xs, RS1X)
    sent(img.at[pl.ds(0, 14 * FLOW)], AG1Z)
    sent(img.at[pl.ds(0, 8 * OWN)], AG1C)
    sent(c_send, RS2C)
    sent(rs2s.at[pl.ds(0, 14 * FLOW)], RS2Z)
    sent(tgr, TG)
    sent(tgr2, TG2)
    sent(l1r, LOSS1)
    sent(lc_tile, LOSSC)
    sent(lzr, LOSSZ)
    sent(gfall.at[pl.ds(0, 21 * FLOW)], AG2)
    sent(gfall.at[pl.ds(0, 9 * FLOW)], AG2X)
    sent(rs3s.at[pl.ds(0, 28 * FLOW)], RS3)
    sent(rs3xs, RS3X)
    sent(arc_si, ARC_I)
    sent(arc_so, ARC_O)
    sent(ars_ri, ARS_I)
    sent(ars_ro, ARS_O)
    sent(fwi.at[0, pl.ds(0, 7 * 144)], AAG_I)
    sent(fwo.at[0, pl.ds(0, 7 * 16)], AAG_O)
    sent(fwi.at[0], AFC_I)
    sent(fwo.at[0], AFC_O)


def widen(loss_in, gt_in, gi_in, gwi_in, gwo_in, loss_ref, gt_ref, gi_ref, gwi_ref, gwo_ref):
    loss_ref[0, 0] = jnp.max(loss_in[...])
    gt_ref[...] = gt_in[...]
    gi_ref[...] = gi_in[...]
    gwi_ref[...] = gwi_in[...].astype(F32)
    gwo_ref[...] = gwo_in[...].astype(F32)


def per_device(
    image_feats, text_feats, w_in, w_out, image_bucket, text_bucket, positive, reward_table
):
    vmem = pl.BlockSpec(memory_space=pltpu.VMEM)

    def buf(shape, kind=BF16):
        return pltpu.VMEM(shape, kind)

    scratch = [
        buf((ROWS, D)),
        buf((OWN, D)),
        buf((D, HID)),
        buf((HID, D)),
        buf((1, ROWS), jnp.int32),
        buf((1, OWN), jnp.int32),
        buf((1, ROWS), jnp.int32),
        buf((8, 8), F32),
        buf((D, ROWS)),
        buf((ROWS, HID), F32),
        buf((ROWS, HID)),
        buf((ROWS, D), F32),
        buf((ROWS, D)),
        buf((ROWS, D)),
        buf((8 * FLOW, D)),
        buf((8 * FLOW, D)),
        buf((2 * FLOW, D), F32),
        buf((2 * FLOW, D), F32),
        buf((FLOW, D), F32),
        buf((FLOW, D), F32),
        buf((ROWS, D + ext)),
        buf((8, ROWS), F32),
        buf((8, ROWS), F32),
        buf((8, ROWS), F32),
        buf((ext, ROWS)),
        buf((ROWS, D)),
        buf((ROWS, ROWS)),
        buf((8, 128), F32),
        buf((256, D), F32),
        buf((256, D), F32),
        buf((ROWS, D), F32),
        buf((256, D), F32),
        buf((256, D)),
        buf((256, D)),
        buf((ROWS, D)),
        buf((3 * 128, D)),
        buf((128, D), F32),
        buf((128, D)),
        buf((3 * OWN, D)),
        buf((8, 128), F32),
        buf((15 * 8, 128), F32),
        buf((8, 128), F32),
        buf((8, 128), F32),
        buf((8, 128), F32),
        buf((7 * 8, 128), F32),
        buf((ROWS, D)),
        buf((ROWS, HID)),
        buf((D, HID), F32),
        buf((HID, D), F32),
        buf((ROWS, D)),
        buf((ROWS, D)),
        buf((OWN, D), F32),
        buf((OWN, D), F32),
        buf((D, 128)),
        buf((128, D)),
        buf((D, 128)),
        buf((128, D)),
        buf((D, 128), F32),
        buf((128, D), F32),
        buf((D, 128)),
        buf((128, D)),
        buf((7 * 144, 128)),
        buf((7 * 16, D)),
        buf((2, D, 128)),
        buf((2, 128, D)),
        pltpu.SemaphoreType.DMA((8,)),
        pltpu.SemaphoreType.DMA((28,)),
        pltpu.SemaphoreType.DMA((28,)),
        pltpu.SemaphoreType.DMA((9,)),
        pltpu.SemaphoreType.DMA((24,)),
        pltpu.SemaphoreType.DMA((8,)),
        pltpu.SemaphoreType.DMA((8,)),
        pltpu.SemaphoreType.DMA((24,)),
        pltpu.SemaphoreType.DMA((32,)),
        pltpu.SemaphoreType.DMA((8,)),
        pltpu.SemaphoreType.DMA((8,)),
        pltpu.SemaphoreType.DMA((15,)),
    ]
    partial = pl.pallas_call(
        kernel,
        out_shape=(
            jax.ShapeDtypeStruct((8, 128), F32),
            jax.ShapeDtypeStruct((OWN, D), F32),
            jax.ShapeDtypeStruct((OWN, D), F32),
            jax.ShapeDtypeStruct((D, HID), BF16),
            jax.ShapeDtypeStruct((HID, D), BF16),
        ),
        in_specs=[pl.BlockSpec(memory_space=pltpu.HBM)] * 8,
        out_specs=(vmem,) * 5,
        scratch_shapes=scratch,
        compiler_params=pltpu.CompilerParams(
            collective_id=0, has_side_effects=True, vmem_limit_bytes=VMEM_LIMIT
        ),
        name="pairs_and_block",
    )(
        image_feats, text_feats, w_in, w_out, image_bucket[None, :], text_bucket[None, :], positive[None, :],
        reward_table,
    )
    loss, grad_text, grad_image, grad_w_in, grad_w_out = pl.pallas_call(
        widen,
        out_shape=(
            jax.ShapeDtypeStruct((1, 1), F32),
            jax.ShapeDtypeStruct((OWN, D), F32),
            jax.ShapeDtypeStruct((OWN, D), F32),
            jax.ShapeDtypeStruct((D, HID), F32),
            jax.ShapeDtypeStruct((HID, D), F32),
        ),
        in_specs=[vmem] * 5,
        out_specs=(pl.BlockSpec(memory_space=pltpu.SMEM),) + (vmem,) * 4,
        compiler_params=pltpu.CompilerParams(vmem_limit_bytes=VMEM_LIMIT),
        name="widen",
    )(*partial)
    return (loss.reshape(()), grad_text, grad_image, grad_w_in, grad_w_out)


def solution(mesh):
    return jax.shard_map(
        per_device,
        mesh=mesh,
        in_specs=(
            P("dp", None),
            P(("dp", "mp"), None),
            P(None, "mp"),
            P("mp", None),
            P("dp"),
            P(("dp", "mp")),
            P("dp"),
            P(),
        ),
        out_specs=(P(), P(("dp", "mp"), None), P(("dp", "mp"), None), P(None, "mp"), P("mp", None)),
        check_vma=False,
    )
```

```python
import jax
import jax.numpy as jnp
from jax import lax
from jax.experimental import pallas as pl
from jax.experimental.pallas import tpu as pltpu
from jax.sharding import PartitionSpec as P

MESH = pl.DeviceIdType.MESH
F32 = jnp.float32
BF16 = jnp.bfloat16

logit_scale = 4.0
logit_bias = -2.0
norm_eps = 1e-06
root_coef = 0.7978845608028654
cubic_coef = 0.044715

D = 1152
ROWS = 512
OWN = 32
HID = 256
PAIRS = 8192.0 * 8192.0
ext = 128
VMEM_LIMIT = 60 * 2**20

NT = (((1,), (1,)), ((), ()))
TN = (((0,), (0,)), ((), ()))


def dot(a, b):
    return jnp.dot(a, b, preferred_element_type=F32)


def dot_nt(a, b):
    return lax.dot_general(a, b, NT, preferred_element_type=F32)


def dot_tn(a, b):
    return lax.dot_general(a, b, TN, preferred_element_type=F32)


def gelu_tanh(v):
    return 0.5 * v * (1.0 + jnp.tanh(root_coef * (v + cubic_coef * v * v * v)))


def gelu_slope(v):
    t = jnp.tanh(root_coef * (v + cubic_coef * v * v * v))
    return 0.5 * (1.0 + t) + 0.5 * v * (1.0 - t * t) * root_coef * (1.0 + 3.0 * cubic_coef * v * v)


def row_norm(v):
    return jnp.sqrt(jnp.sum(v * v, axis=-1, keepdims=True) + norm_eps)


(TEXT, TEXT2, META, RS1, RS1B, RS1X, AG1C, RS2C, RS2Z, TG, TG2, LOSS1, LOSSC, LOSSZ, AG2, AG2X, RS3, RS3X, ARC_I, ARC_O, ARS_I, ARS_O,
 AAG_I, AAG_O, AFC_I, AFC_O, AG1Z, RS1L) = range(28)
FLOW = 16
UP, DOWN = 0, 1
FAR_FIRST = (5, 4, 7, 3, 6, 2, 1)
SLOTS = ((0, UP), (4, UP), (3, UP), (3, DOWN), (2, UP), (2, DOWN), (1, UP), (1, DOWN))


def slot_at(way, far):
    return 0 if far == 0 else 1 if far == 4 else 8 - 2 * far + way


def rows_at(start, count, step):
    return pl.ds(pl.multiple_of(start, step), count)


def kernel(
    x_hbm, t_hbm, wi_hbm, wo_hbm, ib_hbm, tb_hbm, pos_hbm, tab_hbm,
    loss_ref, gt_ref, gi_ref, gwi_ref, gwo_ref,
    x_ref, t_ref, wi_ref, wo_ref, ib_ref, tb_ref, pos_ref, tab_ref,
    xt, hp, act, part, rs1s, rs1r, rs1bs, rs1br, rs1ls, rs1lr, rs1xs, rs1xr, txt, meta, meta_s, meta_r, hot, img, coef, loss_acc, c_send, c_recv, ig, held, rs2s, rs2r, tgs, tgr, tgo, tgs2, tgr2,
    l_tile, l1r, lc_tile, lcr, lz_tile, lzr, gfall, gh, swi, swo, rs3s, rs3r, rs3xs, rs3xr,
    arc_si, arc_so, arc_ri, arc_ro, awi, awo, ars_si, ars_so, ars_ri, ars_ro, fwi, fwo,
    lsem, ssem, rsem, csem, rs1sem, ag1sem, rs2sem, ag2sem, rs3sem, rs1bsem, ag2bsem, aagsem,
):
    dp, mp = lax.axis_index("dp"), lax.axis_index("mp")
    core, y, xl = lax.rem(dp, 2), lax.rem(dp // 2, 4), dp // 8
    xh, z = lax.rem(mp, 2), mp // 2
    x = xh * 2 + xl
    partner = (dp + 1 - 2 * core, mp)

    across = (dp, mp + 1 - 2 * xh)

    def z_peer(j):
        return (dp, lax.rem(z + j, 8) * 2 + xh)

    def plane_dev(x2, y2):
        return ((lax.rem(x2, 2) * 4 + y2) * 2 + core, z * 2 + x2 // 2)

    def ar_peer(j):
        xl2, y2 = lax.rem(xl + lax.rem(j, 2), 2), lax.rem(y + j // 2, 4)
        return ((xl2 * 4 + y2) * 2 + core, mp), y2 * 2 + xl2

    def plane_peer(j):
        return plane_dev(lax.rem(x + lax.rem(j, 4), 4), lax.rem(y + j // 4, 4))

    def copy(src, dst, phase, device, recv=None):
        return pltpu.make_async_remote_copy(
            src_ref=src, dst_ref=dst, send_sem=ssem.at[phase],
            recv_sem=rsem.at[phase] if recv is None else recv, device_id=device, device_id_type=MESH,
        )

    def got(ref, phase):
        copy(ref, ref, phase, partner).wait_recv()

    def sent(ref, phase):
        copy(ref, ref, phase, partner).wait_send()

    def hops(f, way):
        return 4 if f % 2 == way else 3

    def neighbour(way, distance=1):
        return z_peer(distance if way == UP else 8 - distance)

    def toward(way, far):
        return lax.rem(z + (far if way == UP else 8 - far), 8)

    barrier = pltpu.get_barrier_semaphore()

    def greet(j, _):
        pl.semaphore_signal(barrier, inc=1, device_id=plane_peer(j), device_id_type=MESH)
        return 0

    lax.fori_loop(1, 16, greet, 0)

    def greet_z(j, _):
        pl.semaphore_signal(barrier, inc=1, device_id=z_peer(j), device_id_type=MESH)
        return 0

    lax.fori_loop(1, 8, greet_z, 0)
    pl.semaphore_signal(barrier, inc=1, device_id=partner, device_id_type=MESH)

    loads = [
        pltpu.make_async_copy(src, dst, lsem.at[i])
        for i, (src, dst) in enumerate(
            (
                (t_hbm, t_ref), (tb_hbm, tb_ref), (pos_hbm, pos_ref), (ib_hbm, ib_ref), (tab_hbm, tab_ref),
                (wi_hbm, wi_ref), (wo_hbm, wo_ref),
            )
        )
    ]
    for load in loads:
        load.start()
    for far, way in SLOTS:
        for other in (0, 1):
            from_rows = rows_at((toward(way, far) * 2 + (1 - xh if other else xh)) * OWN, OWN, OWN)
            to_rows = pl.ds(slot_at(way, far) * 64 + other * OWN, OWN)
            pltpu.make_async_copy(x_hbm.at[from_rows], x_ref.at[to_rows], lsem.at[7]).start()
    for load in loads[:5]:
        load.wait()

    own_slot = y * 4 + x
    own_text = rows_at(own_slot * OWN, OWN, OWN)
    wide = t_ref[...].astype(F32)
    txt[own_text, :D] = (wide / row_norm(wide)).astype(BF16)
    eye = lax.broadcasted_iota(jnp.int32, (OWN, OWN), 0) == lax.broadcasted_iota(jnp.int32, (OWN, OWN), 1)
    tb_col = jnp.sum(jnp.where(eye, tb_ref[...].astype(F32), 0.0), axis=1, keepdims=True)
    lane = lax.broadcasted_iota(jnp.int32, (OWN, ext), 1)
    level = jnp.where(lane < 24, lax.rem(lane, 8), -1).astype(F32)
    txt[own_text, D:] = jnp.where(level == tb_col, 1.0, 0.0).astype(BF16)

    pl.semaphore_wait(barrier, 23)

    def send_text_y(slot_x, j):
        rows = rows_at((y * 4 + slot_x) * OWN, OWN, OWN)
        copy(txt.at[rows], txt.at[rows], TEXT2, plane_dev(x, lax.rem(y + j, 4))).start()

    def send_own_y(j, _):
        send_text_y(x, j)
        return 0

    lax.fori_loop(1, 4, send_own_y, 0)

    def text_on():
        got(txt.at[pl.ds(0, 3 * OWN)], TEXT)

        def send(i, _):
            send_text_y(lax.rem(x + 1 + i // 3, 4), 1 + lax.rem(i, 3))
            return 0

        lax.fori_loop(0, 9, send, 0)

    def slot_of(f, way, far, flows):
        return pl.ds(((way * flows + f) * 4 + far - 1) * FLOW, FLOW)

    def sem_of(sems, f, way, far, flows):
        return sems.at[(way * flows + f) * 4 + far - 1]

    def last_of(f, way, last):
        return pl.ds((way + 2 * last[3].index(f)) * FLOW, FLOW)

    def reduce_step(far, which, flows, row_of, held, sbuf, rbuf, phase, sems, last):
        for f in which:
            for way in (UP, DOWN):
                if far > hops(f, way):
                    continue
                value = held[pl.ds(row_of(f, slot_at(way, far)), FLOW), :]
                for beyond in {1: (2,), 2: (3, 4)}.get(far, ()):
                    if beyond <= hops(f, way):
                        before = slot_of(f, way, beyond, flows)
                        copy(rbuf.at[before], rbuf.at[before], phase, partner, sem_of(sems, f, way, beyond, flows)).wait_recv()
                        value = value + rbuf[before, :].astype(F32)
                sem = sem_of(sems, f, way, far, flows)
                if f in last[3] and far == 1:
                    sbuf1, rbuf1, phase1, _ = last
                    slot = last_of(f, way, last)
                    sbuf1[slot, :] = value
                    copy(sbuf1.at[slot], rbuf1.at[slot], phase1, neighbour(way), sem).start()
                else:
                    slot = slot_of(f, way, far, flows)
                    sbuf[slot, :] = value.astype(BF16)
                    copy(sbuf.at[slot], rbuf.at[slot], phase, neighbour(way, 2 if far == 4 else 1), sem).start()

    def reduce_end(f, flows, row_of, held, rbuf, phase, sems, last):
        value = held[pl.ds(row_of(f, 0), FLOW), :]
        for way in (UP, DOWN):
            slot = slot_of(f, way, 1, flows)
            if f in last[3]:
                rbuf, phase, slot = last[1], last[2], last_of(f, way, last)
            copy(rbuf.at[slot], rbuf.at[slot], phase, partner, sem_of(sems, f, way, 1, flows)).wait_recv()
            value = value + rbuf[slot, :].astype(F32)
        return value

    def gather_step(far, which, flows, row_of, buf, phase, sems):
        for f in which:
            for way in (UP, DOWN):
                if far > hops(f, way):
                    continue
                rows = pl.ds(row_of(f, slot_at(1 - way, far)), FLOW)
                if far > 0:
                    copy(buf.at[rows], buf.at[rows], phase, partner, sem_of(sems, f, way, far, flows)).wait_recv()
                for distance in {0: (1,), 1: (1,), 2: (1, 2)}.get(far, ()):
                    if far + distance <= hops(f, way):
                        onto = pl.ds(row_of(f, slot_at(1 - way, far + distance)), FLOW)
                        sem = sem_of(sems, f, way, far + distance, flows)
                        copy(buf.at[rows], buf.at[onto], phase, neighbour(way, distance), sem).start()

    def mp_row(f, slot):
        return slot * 64 + (OWN, 0, FLOW, OWN + FLOW)[f]

    def reduce_mp(held, sbuf, rbuf, bs, br, xs, xr, last, phases, sems, bsems):
        ring_phase, b_phase, x_phase = phases

        def send_across(slots):
            for slot in slots:
                rows = pl.ds(slot * FLOW, FLOW)
                bs[rows, :] = held[slot * 64 + 48 : slot * 64 + 64, :].astype(BF16)
                copy(bs.at[rows], br.at[rows], b_phase, across, bsems.at[slot]).start()

        def ring(far):
            reduce_step(far, (0, 1), 3, mp_row, held, sbuf, rbuf, ring_phase, sems, last)

        def met(slots):
            for slot in slots:
                rows = pl.ds(slot * FLOW, FLOW)
                copy(br.at[rows], br.at[rows], b_phase, partner, bsems.at[slot]).wait_recv()
                held[slot * 64 + FLOW : slot * 64 + 2 * FLOW, :] += br[rows, :].astype(F32)

        def cross(far):
            met((1,) if far == 4 else (slot_at(UP, far), slot_at(DOWN, far)))
            reduce_step(far, (2,), 3, mp_row, held, sbuf, rbuf, ring_phase, sems, last)

        def end_across():
            xs[...] = reduce_end(0, 3, mp_row, held, rbuf, ring_phase, sems, last)
            copy(xs, xr, x_phase, across).start()
            met((0,))

        def end():
            near = reduce_end(1, 3, mp_row, held, rbuf, ring_phase, sems, last)
            mixed = reduce_end(2, 3, mp_row, held, rbuf, ring_phase, sems, last)
            got(xr, x_phase)
            return jnp.concatenate([near + xr[...], mixed], axis=0)

        return send_across, ring, cross, end_across, end

    for load in loads[5:]:
        load.wait()

    pltpu.make_async_copy(x_ref, x_ref, lsem.at[7]).wait()

    def forward(g):
        rows = pl.ds(g * 128, 128)
        pre = dot(x_ref[rows, :], wi_ref[...])
        hp[rows, :] = pre
        a = gelu_tanh(pre).astype(BF16)
        act[rows, :] = a
        part[rows, :] = dot(a, wo_ref[...])

    rs1_across, rs1_ring, rs1_cross, rs1_end_across, rs1_end = reduce_mp(
        part, rs1s, rs1r, rs1bs, rs1br, rs1xs, rs1xr, (rs1ls, rs1lr, RS1L, (2,)), (RS1, RS1B, RS1X), rs1sem, rs1bsem
    )
    forward(0)
    rs1_across((1, 0))
    def send_text(j, _):
        device = plane_dev(lax.rem(x + j, 4), y)
        copy(txt.at[own_text], txt.at[own_text], TEXT, device).start()
        return 0

    lax.fori_loop(1, 4, send_text, 0)
    rs1_ring(4)
    forward(1)
    rs1_across((2, 3))
    rs1_ring(3)
    forward(2)
    rs1_across((4, 5))
    rs1_cross(4)
    text_on()
    rs1_ring(2)
    forward(3)
    rs1_across((6, 7))
    rs1_cross(3)
    rs1_ring(1)
    for g in range(4):
        xt[:, g * 128 : g * 128 + 128] = x_ref[g * 128 : g * 128 + 128, :].T
    pos = pos_ref[...]
    pos_hi = pos // 64
    line = lax.broadcasted_iota(jnp.int32, (8, ROWS), 0)
    table_rows = jnp.where(
        line == 0, pos_hi, jnp.where(line == 1, pos - pos_hi * 64, jnp.where(line == 2, ib_ref[...], 0))
    ).astype(F32).astype(BF16)
    took = lax.broadcasted_iota(jnp.int32, (ROWS, ROWS), 0)
    into = lax.broadcasted_iota(jnp.int32, (ROWS, ROWS), 1)
    slot = into // 64
    distance = jnp.where(lax.rem(slot, 2) == 0, 4 - slot // 2, slot // 2 + 4)
    distance = jnp.where(slot == 0, 0, jnp.where(slot == 1, 4, distance))
    right = took == (lax.rem(z + distance, 8) * 2 + xh) * OWN + lax.rem(into, OWN)
    first = lax.rem(into, 64) < OWN
    meta[...] = dot(table_rows, jnp.where(right & first, 1.0, 0.0).astype(BF16))
    meta_s[...] = dot(table_rows, jnp.where(right & jnp.logical_not(first), 1.0, 0.0).astype(BF16))

    copy(meta_s, meta_r, META, partner).start()
    rs1_cross(2)
    rs1_end_across()
    rs1_cross(1)
    features = rs1_end() + x_ref[:OWN, :].astype(F32)
    norm = row_norm(features)
    unit = features / norm

    img[:OWN, :] = unit.astype(BF16)
    def send_img(from_row, to_row, count, sem, distance):
        copy(
            img.at[pl.ds(from_row, count)], img.at[pl.ds(to_row, count)], AG1Z, z_peer(distance % 8), ag1sem.at[sem]
        ).start()

    def got_img(count, sem):
        copy(img.at[pl.ds(0, count)], img.at[pl.ds(0, count)], AG1Z, partner, ag1sem.at[sem]).wait_recv()

    for way, sign in ((UP, 1), (DOWN, -1)):
        send_img(0, slot_at(1 - way, 2) * 64, OWN, way, 2 * sign)
    for way, sign in ((UP, 1), (DOWN, -1)):
        send_img(0, slot_at(1 - way, 1) * 64, OWN, 2 + way, sign)

    def to_partner(slot):
        copy(
            img.at[pl.ds(slot * 64, OWN)], img.at[pl.ds(slot * 64 + OWN, OWN)], AG1C, partner, csem.at[slot // 2 + (4 if slot == 1 else 0)]
        ).start()

    def from_partner(far):
        count = OWN if far in (0, 4) else 2 * OWN
        copy(
            img.at[pl.ds(0, count)], img.at[pl.ds(0, count)], AG1C, partner, csem.at[0 if far == 0 else 4 - far if far < 4 else 4]
        ).wait_recv()

    to_partner(0)

    got(meta_r, META)
    meta[...] += meta_r[...]

    eye8 = lax.broadcasted_iota(jnp.int32, (8, 8), 0) == lax.broadcasted_iota(jnp.int32, (8, 8), 1)

    buckets = meta[2:3, :]
    weights = jnp.zeros((8, ROWS), F32)
    for k in range(8):
        column = jnp.sum(jnp.where(eye8, tab_ref[k : k + 1, :], 0.0), axis=1, keepdims=True)
        weights = weights + jnp.where(buckets == float(k), column, 0.0)
    hi = weights.astype(BF16).astype(F32)
    mid = (weights - hi).astype(BF16).astype(F32)
    low = weights - hi - mid
    hot[...] = jnp.concatenate([hi, mid, low, jnp.zeros((ext - 24, ROWS), F32)], axis=0).astype(BF16)
    meta[0:1, :] = meta[0:1, :] * 64.0 + meta[1:2, :]

    loss_acc[...] = jnp.zeros_like(loss_acc)

    def pairs(g):
        images = pl.ds(g * 128, 128)

        logits = logit_scale * dot_nt(txt[:, :D], img[images, :]) + logit_bias
        weight = dot(txt[:, D:], hot[:, images])
        slot = lax.broadcasted_iota(jnp.int32, (ROWS, 1), 0)
        p = slot // OWN
        px, py = lax.rem(p, 4), p // 4
        index = (((lax.rem(px, 2) * 4 + py) * 2 + core) * 16 + z * 2 + px // 2) * OWN + lax.rem(slot, OWN)
        hit = index.astype(F32) == meta[0:1, images]
        against = jnp.where(hit, -logits, logits)
        grown = jnp.exp(against)
        loss_acc[...] += jnp.sum((weight * jnp.log(1.0 + grown)).reshape(ROWS // 8, 8, 128), axis=0)
        slope = logit_scale * weight * (grown / (1.0 + grown))
        coef[:, images] = jnp.where(hit, -slope, slope).astype(BF16)

    def image_grad(g):
        rows = pl.ds(g * 128, 128)
        ig[rows, :] = dot_tn(coef[:, rows], txt[:, :D])
        to = pl.ds(g * 64, 64)
        for slot in (2 * g, 2 * g + 1):
            c_send[slot * OWN : slot * OWN + OWN, :] = ig[slot * 64 + OWN : slot * 64 + 64, :]
        copy(c_send.at[to], c_recv.at[to], RS2C, partner, csem.at[5 + g]).start()

    def both_cores(g):
        to = pl.ds(g * 64, 64)
        copy(c_send.at[to], c_recv.at[to], RS2C, partner, csem.at[5 + g]).wait_recv()
        for slot in (2 * g, 2 * g + 1):
            rows = pl.ds(slot * OWN, OWN)
            held[rows, :] = ig[slot * 64 : slot * 64 + OWN, :] + c_recv[rows, :]

    for way in (UP, DOWN):
        got_img(OWN, 2 + way)
        to_partner(slot_at(1 - way, 1))
    for way, sign in ((UP, 1), (DOWN, -1)):
        got_img(OWN, way)
        row = slot_at(1 - way, 2) * 64
        send_img(row, slot_at(1 - way, 3) * 64, OWN, 4 + way, sign)
        send_img(row + FLOW * way, 64 + FLOW * way, FLOW, 6 + way, 2 * sign)
    for way in (UP, DOWN):
        to_partner(slot_at(1 - way, 2))
    got(txt.at[pl.ds(0, 3 * 128)], TEXT2)
    from_partner(1)
    pairs(3)
    for way in (UP, DOWN):
        got_img(OWN, 4 + way)
        to_partner(slot_at(1 - way, 3))
    from_partner(2)
    pairs(2)
    image_grad(3)
    for way in (UP, DOWN):
        got_img(FLOW, 6 + way)
    to_partner(1)
    from_partner(3)
    pairs(1)
    image_grad(1)
    from_partner(0)
    from_partner(4)
    pairs(0)

    def send_rs2(value, sem, distance):
        rows = pl.ds(sem * OWN, value.shape[0])
        rs2s[rows, :] = value.astype(BF16)
        copy(rs2s.at[rows], rs2r.at[rows], RS2Z, z_peer(distance % 8), rs2sem.at[sem]).start()

    def got_rs2(sem, count=OWN):
        rows = pl.ds(sem * OWN, count)
        copy(rs2r.at[rows], rs2r.at[rows], RS2Z, partner, rs2sem.at[sem]).wait_recv()
        return rs2r[rows, :].astype(F32)

    def held_at(way, far):
        row = slot_at(way, far) * OWN
        return held[row : row + OWN, :]

    image_grad(0)
    both_cores(1)
    send_rs2(held_at(UP, 3), 2, 1)
    send_rs2(held_at(DOWN, 3), 3, -1)
    both_cores(0)
    far4 = held_at(UP, 4)
    send_rs2(far4[:FLOW], 0, 2)
    send_rs2(far4[FLOW:], 1, -2)
    image_grad(2)
    both_cores(3)
    send_rs2(held_at(UP, 1), 6, 1)
    send_rs2(held_at(DOWN, 1), 7, -1)

    def text_grad(j, _):
        b = lax.rem(y + j, 4)
        rows = rows_at(b * 128, 128, 128)
        tgs[rows, :] = dot(coef[rows, :], img[...]).astype(BF16)
        copy(tgs.at[rows], tgr.at[rows_at((j - 1) * 128, 128, 128)], TG, plane_dev(x, b)).start()
        return 0

    lax.fori_loop(1, 3, text_grad, 0)
    both_cores(2)
    far2 = held_at(UP, 2) + got_rs2(2)
    send_rs2(jnp.concatenate([far2[:FLOW] + got_rs2(0, FLOW), far2[FLOW:]], axis=0), 4, 2)
    far2 = held_at(DOWN, 2) + got_rs2(3)
    send_rs2(jnp.concatenate([far2[:FLOW], far2[FLOW:] + got_rs2(1, FLOW)], axis=0), 5, -2)
    text_grad(3, 0)
    tgo[...] = dot(coef[rows_at(y * 128, 128, 128), :], img[...])

    def text_grad_on():
        got(tgr, TG)
        tgo[...] += tgr[0:128, :].astype(F32) + tgr[128:256, :].astype(F32) + tgr[256:384, :].astype(F32)

        def send(j, _):
            x2 = lax.rem(x + j, 4)
            rows = rows_at(x2 * OWN, OWN, OWN)
            tgs2[rows, :] = tgo[rows, :].astype(BF16)
            copy(tgs2.at[rows], tgr2.at[rows_at((j - 1) * OWN, OWN, OWN)], TG2, plane_dev(x2, y)).start()
            return 0

        lax.fori_loop(1, 4, send, 0)

    l_tile[...] = jnp.zeros((8, 128), F32) + jnp.sum(loss_acc[...])

    def send_loss(j, _):
        copy(l_tile, l1r.at[rows_at((j - 1) * 8, 8, 8)], LOSS1, plane_peer(j)).start()
        return 0

    lax.fori_loop(1, 16, send_loss, 0)

    own_grad = held[0:OWN, :] + got_rs2(6) + got_rs2(7) + got_rs2(4) + got_rs2(5)
    projected = jnp.sum(unit * own_grad, axis=-1, keepdims=True)
    grad_features = (own_grad - unit * projected) / norm
    gfall[:OWN, :] = grad_features.astype(BF16)
    def cross_gf(slot):
        copy(
            gfall.at[pl.ds(slot * 64 + FLOW, FLOW)], gfall.at[pl.ds(slot * 64 + 48, FLOW)], AG2X, across, ag2bsem.at[slot]
        ).start()

    def crossed_gf(slots):
        for slot in slots:
            rows = pl.ds(slot * 64 + 48, FLOW)
            copy(gfall.at[rows], gfall.at[rows], AG2X, partner, ag2bsem.at[slot]).wait_recv()

    def ag2_step(far, which):
        gather_step(far, which, 3, mp_row, gfall, AG2, ag2sem)

    def near_step(far):
        ag2_step(far, (2, 1))
        for slot in (1,) if far == 4 else (slot_at(UP, far), slot_at(DOWN, far)):
            cross_gf(slot)

    other_rows = pl.ds(OWN, FLOW)
    copy(gfall.at[pl.ds(0, FLOW)], gfall.at[other_rows], AG2X, across).start()
    ag2_step(0, (2, 1))
    cross_gf(0)
    near_step(1)
    got(gfall.at[other_rows], AG2X)
    ag2_step(0, (0,))
    near_step(2)

    def backward(g):
        rows = pl.ds(g * 128, 128)
        gh[rows, :] = (dot_nt(gfall[rows, :], wo_ref[...]) * gelu_slope(hp[rows, :])).astype(BF16)

    def to_input(g):
        rows = pl.ds(g * 128, 128)
        part[rows, :] = dot_nt(gh[rows, :], wi_ref[...])

    rs3_last = (None, None, None, ())

    def rs3_ring(far):
        reduce_step(far, (0, 3, 1, 2), 4, mp_row, part, rs3s, rs3r, RS3, rs3sem, rs3_last)

    def rs3_end(flows):
        return jnp.concatenate([reduce_end(f, 4, mp_row, part, rs3r, RS3, rs3sem, rs3_last) for f in flows], axis=0)

    other_cols, own_cols = rows_at((1 - core) * 128, 128, 128), rows_at(core * 128, 128, 128)
    late, early = pl.ds(0, 256), pl.ds(256, 256)

    def w_in_half(cols, out, kind):
        out[...] = (swi[:, cols] + dot(xt[:, late], gh[late, cols])).astype(kind)

    ag2_step(1, (0,))
    crossed_gf((6, 7))
    backward(3)
    near_step(3)
    ag2_step(2, (0,))
    crossed_gf((4, 5))
    backward(2)
    swo[...] = dot_tn(act[early, :], gfall[early, :])
    near_step(4)
    ag2_step(3, (0,))
    swi[...] = dot(xt[:, early], gh[early, :])
    crossed_gf((2, 3))
    backward(1)
    to_input(2)
    to_input(3)
    to_input(1)
    ag2_step(4, (0,))
    crossed_gf((0, 1))
    arc_so[...] = (swo[other_cols, :] + dot_tn(act[late, other_cols], gfall[late, :])).astype(BF16)
    copy(arc_so, arc_ro, ARC_O, partner).start()
    backward(0)
    w_in_half(other_cols, arc_si, BF16)
    copy(arc_si, arc_ri, ARC_I, partner).start()
    to_input(0)
    rs3_ring(4)
    rs3_ring(3)
    awo[...] = swo[own_cols, :] + dot_tn(act[late, own_cols], gfall[late, :])
    got(arc_ro, ARC_O)
    awo[...] += arc_ro[...].astype(F32)
    ars_so[...] = awo[...].astype(BF16)

    def send_ars_out(j, _):
        device, q = ar_peer(j)
        copy(ars_so.at[rows_at(q * 16, 16, 16)], ars_ro.at[rows_at((j - 1) * 16, 16, 16)], ARS_O, device).start()
        return 0

    for peer in FAR_FIRST:
        send_ars_out(peer, 0)
    w_in_half(own_cols, awi, F32)
    got(arc_ri, ARC_I)
    awi[...] += arc_ri[...].astype(F32)
    ars_si[...] = awi[...].astype(BF16)

    def send_ars_in(j, _):
        device, q = ar_peer(j)
        copy(ars_si.at[rows_at(q * 144, 144, 144)], ars_ri.at[rows_at((j - 1) * 144, 144, 144)], ARS_I, device).start()
        return 0

    for peer in FAR_FIRST:
        send_ars_in(peer, 0)
    text_grad_on()
    rs3_ring(2)
    got(l1r, LOSS1)
    loss = l_tile[...]
    for j in range(15):
        loss = loss + l1r[j * 8 : j * 8 + 8, :]
    lc_tile[...] = loss
    copy(lc_tile, lcr, LOSSC, partner).start()

    rs3_ring(1)

    q = y * 2 + xl
    own_in, own_out = rows_at(q * 144, 144, 144), rows_at(q * 16, 16, 16)
    total_in, total_out = awi[own_in, :], awo[own_out, :]
    got(ars_ro, ARS_O)
    for j in range(7):
        total_out = total_out + ars_ro[j * 16 : j * 16 + 16, :].astype(F32)
    fwo[core, own_out, :] = total_out.astype(BF16)

    def send_aag_out(j, _):
        device, _ = ar_peer(j)
        copy(fwo.at[core, own_out], fwo.at[core, own_out], AAG_O, device, aagsem.at[7 + j]).start()
        return 0

    for peer in FAR_FIRST:
        send_aag_out(peer, 0)
    copy(fwo.at[core, own_out], fwo.at[core, own_out], AFC_O, partner).start()
    got(ars_ri, ARS_I)
    for j in range(7):
        total_in = total_in + ars_ri[j * 144 : j * 144 + 144, :].astype(F32)
    fwi[core, own_in, :] = total_in.astype(BF16)

    def send_aag_in(j, _):
        device, _ = ar_peer(j)
        copy(fwi.at[core, own_in], fwi.at[core, own_in], AAG_I, device, aagsem.at[j - 1]).start()
        return 0

    for peer in FAR_FIRST:
        send_aag_in(peer, 0)
    copy(fwi.at[core, own_in], fwi.at[core, own_in], AFC_I, partner).start()
    got(lcr, LOSSC)
    lz_tile[...] = loss + lcr[...]

    def send_loss_z(j, _):
        copy(lz_tile, lzr.at[rows_at((j - 1) * 8, 8, 8)], LOSSZ, z_peer(j)).start()
        return 0

    lax.fori_loop(1, 8, send_loss_z, 0)
    rs3xs[...] = rs3_end((0, 3))
    copy(rs3xs, rs3xr, RS3X, across).start()
    grad_image = rs3_end((1, 2)) + grad_features

    def weights_on(j, _):
        xl2, y2 = lax.rem(xl + lax.rem(j, 2), 2), lax.rem(y + 4 - j // 2, 4)
        q2 = y2 * 2 + xl2
        out, into = rows_at(q2 * 16, 16, 16), rows_at(q2 * 144, 144, 144)
        copy(fwo.at[core, out], fwo.at[core, out], AAG_O, partner, aagsem.at[7 + j]).wait_recv()
        copy(fwo.at[core, out], fwo.at[core, out], AFC_O, partner).start()
        copy(fwi.at[core, into], fwi.at[core, into], AAG_I, partner, aagsem.at[j - 1]).wait_recv()
        copy(fwi.at[core, into], fwi.at[core, into], AFC_I, partner).start()
        return 0

    for peer in FAR_FIRST:
        weights_on(peer, 0)
    got(tgr2, TG2)
    grad_text = tgo[rows_at(x * OWN, OWN, OWN), :]
    for j in range(3):
        grad_text = grad_text + tgr2[j * OWN : j * OWN + OWN, :].astype(F32)
    gt_ref[...] = grad_text
    got(lzr, LOSSZ)
    loss = lz_tile[...]
    for j in range(7):
        loss = loss + lzr[j * 8 : j * 8 + 8, :]
    loss_ref[...] = loss * (1.0 / PAIRS)

    sent(txt.at[pl.ds(0, 3 * OWN)], TEXT)
    sent(txt.at[pl.ds(0, 3 * 128)], TEXT2)
    sent(meta_s, META)
    sent(rs1s.at[pl.ds(0, 19 * FLOW)], RS1)
    sent(rs1bs, RS1B)
    sent(rs1ls, RS1L)
    sent(rs1xs, RS1X)
    sent(img.at[pl.ds(0, 14 * FLOW)], AG1Z)
    sent(img.at[pl.ds(0, 8 * OWN)], AG1C)
    sent(c_send, RS2C)
    sent(rs2s.at[pl.ds(0, 14 * FLOW)], RS2Z)
    sent(tgr, TG)
    sent(l1r, LOSS1)
    sent(lc_tile, LOSSC)
    sent(gfall.at[pl.ds(0, 21 * FLOW)], AG2)
    sent(gfall.at[pl.ds(0, 9 * FLOW)], AG2X)
    sent(arc_si, ARC_I)
    sent(arc_so, ARC_O)
    got(rs3xr, RS3X)
    gi_ref[...] = grad_image + rs3xr[...]
    got(fwo.at[1 - core], AFC_O)
    for half in range(2):
        gwo_ref[half * 128 : half * 128 + 128, :] = fwo[half]
    got(fwi.at[1 - core], AFC_I)
    for half in range(2):
        gwi_ref[:, half * 128 : half * 128 + 128] = fwi[half]

    sent(tgr2, TG2)
    sent(lzr, LOSSZ)
    sent(rs3s.at[pl.ds(0, 28 * FLOW)], RS3)
    sent(rs3xs, RS3X)
    sent(ars_ri, ARS_I)
    sent(ars_ro, ARS_O)
    sent(fwi.at[0, pl.ds(0, 7 * 144)], AAG_I)
    sent(fwo.at[0, pl.ds(0, 7 * 16)], AAG_O)
    sent(fwi.at[0], AFC_I)
    sent(fwo.at[0], AFC_O)


def widen(loss_in, gt_in, gi_in, gwi_in, gwo_in, loss_ref, gt_ref, gi_ref, gwi_ref, gwo_ref):
    loss_ref[0, 0] = jnp.max(loss_in[...])
    gt_ref[...] = gt_in[...]
    gi_ref[...] = gi_in[...]
    gwi_ref[...] = gwi_in[...].astype(F32)
    gwo_ref[...] = gwo_in[...].astype(F32)


def per_device(
    image_feats, text_feats, w_in, w_out, image_bucket, text_bucket, positive, reward_table
):
    vmem = pl.BlockSpec(memory_space=pltpu.VMEM)

    def buf(shape, kind=BF16):
        return pltpu.VMEM(shape, kind)

    scratch = [
        buf((ROWS, D)),
        buf((OWN, D)),
        buf((D, HID)),
        buf((HID, D)),
        buf((1, ROWS), jnp.int32),
        buf((1, OWN), jnp.int32),
        buf((1, ROWS), jnp.int32),
        buf((8, 8), F32),
        buf((D, ROWS)),
        buf((ROWS, HID), F32),
        buf((ROWS, HID)),
        buf((ROWS, D), F32),
        buf((ROWS, D)),
        buf((ROWS, D)),
        buf((8 * FLOW, D)),
        buf((8 * FLOW, D)),
        buf((2 * FLOW, D), F32),
        buf((2 * FLOW, D), F32),
        buf((FLOW, D), F32),
        buf((FLOW, D), F32),
        buf((ROWS, D + ext)),
        buf((8, ROWS), F32),
        buf((8, ROWS), F32),
        buf((8, ROWS), F32),
        buf((ext, ROWS)),
        buf((ROWS, D)),
        buf((ROWS, ROWS)),
        buf((8, 128), F32),
        buf((256, D), F32),
        buf((256, D), F32),
        buf((ROWS, D), F32),
        buf((256, D), F32),
        buf((256, D)),
        buf((256, D)),
        buf((ROWS, D)),
        buf((3 * 128, D)),
        buf((128, D), F32),
        buf((128, D)),
        buf((3 * OWN, D)),
        buf((8, 128), F32),
        buf((15 * 8, 128), F32),
        buf((8, 128), F32),
        buf((8, 128), F32),
        buf((8, 128), F32),
        buf((7 * 8, 128), F32),
        buf((ROWS, D)),
        buf((ROWS, HID)),
        buf((D, HID), F32),
        buf((HID, D), F32),
        buf((ROWS, D)),
        buf((ROWS, D)),
        buf((OWN, D), F32),
        buf((OWN, D), F32),
        buf((D, 128)),
        buf((128, D)),
        buf((D, 128)),
        buf((128, D)),
        buf((D, 128), F32),
        buf((128, D), F32),
        buf((D, 128)),
        buf((128, D)),
        buf((7 * 144, 128)),
        buf((7 * 16, D)),
        buf((2, D, 128)),
        buf((2, 128, D)),
        pltpu.SemaphoreType.DMA((8,)),
        pltpu.SemaphoreType.DMA((28,)),
        pltpu.SemaphoreType.DMA((28,)),
        pltpu.SemaphoreType.DMA((9,)),
        pltpu.SemaphoreType.DMA((24,)),
        pltpu.SemaphoreType.DMA((8,)),
        pltpu.SemaphoreType.DMA((8,)),
        pltpu.SemaphoreType.DMA((24,)),
        pltpu.SemaphoreType.DMA((32,)),
        pltpu.SemaphoreType.DMA((8,)),
        pltpu.SemaphoreType.DMA((8,)),
        pltpu.SemaphoreType.DMA((15,)),
    ]
    partial = pl.pallas_call(
        kernel,
        out_shape=(
            jax.ShapeDtypeStruct((8, 128), F32),
            jax.ShapeDtypeStruct((OWN, D), F32),
            jax.ShapeDtypeStruct((OWN, D), F32),
            jax.ShapeDtypeStruct((D, HID), BF16),
            jax.ShapeDtypeStruct((HID, D), BF16),
        ),
        in_specs=[pl.BlockSpec(memory_space=pltpu.HBM)] * 8,
        out_specs=(vmem,) * 5,
        scratch_shapes=scratch,
        compiler_params=pltpu.CompilerParams(
            collective_id=0, has_side_effects=True, vmem_limit_bytes=VMEM_LIMIT
        ),
        name="pairs_and_block",
    )(
        image_feats, text_feats, w_in, w_out, image_bucket[None, :], text_bucket[None, :], positive[None, :],
        reward_table,
    )
    loss, grad_text, grad_image, grad_w_in, grad_w_out = pl.pallas_call(
        widen,
        out_shape=(
            jax.ShapeDtypeStruct((1, 1), F32),
            jax.ShapeDtypeStruct((OWN, D), F32),
            jax.ShapeDtypeStruct((OWN, D), F32),
            jax.ShapeDtypeStruct((D, HID), F32),
            jax.ShapeDtypeStruct((HID, D), F32),
        ),
        in_specs=[vmem] * 5,
        out_specs=(pl.BlockSpec(memory_space=pltpu.SMEM),) + (vmem,) * 4,
        compiler_params=pltpu.CompilerParams(vmem_limit_bytes=VMEM_LIMIT),
        name="widen",
    )(*partial)
    return (loss.reshape(()), grad_text, grad_image, grad_w_in, grad_w_out)


def solution(mesh):
    return jax.shard_map(
        per_device,
        mesh=mesh,
        in_specs=(
            P("dp", None),
            P(("dp", "mp"), None),
            P(None, "mp"),
            P("mp", None),
            P("dp"),
            P(("dp", "mp")),
            P("dp"),
            P(),
        ),
        out_specs=(P(), P(("dp", "mp"), None), P(("dp", "mp"), None), P(None, "mp"), P("mp", None)),
        check_vma=False,
    )
```

```python
import jax
import jax.numpy as jnp
from jax import lax
from jax.experimental import pallas as pl
from jax.experimental.pallas import tpu as pltpu
from jax.sharding import PartitionSpec as P

MESH = pl.DeviceIdType.MESH
F32 = jnp.float32
BF16 = jnp.bfloat16

logit_scale = 4.0
logit_bias = -2.0
norm_eps = 1e-06
root_coef = 0.7978845608028654
cubic_coef = 0.044715

D = 1152
ROWS = 512
OWN = 32
HID = 256
PAIRS = 8192.0 * 8192.0
ext = 128
VMEM_LIMIT = 60 * 2**20

NT = (((1,), (1,)), ((), ()))
TN = (((0,), (0,)), ((), ()))


def dot(a, b):
    return jnp.dot(a, b, preferred_element_type=F32)


def dot_nt(a, b):
    return lax.dot_general(a, b, NT, preferred_element_type=F32)


def dot_tn(a, b):
    return lax.dot_general(a, b, TN, preferred_element_type=F32)


def gelu_tanh(v):
    return 0.5 * v * (1.0 + jnp.tanh(root_coef * (v + cubic_coef * v * v * v)))


def gelu_slope(v):
    t = jnp.tanh(root_coef * (v + cubic_coef * v * v * v))
    return 0.5 * (1.0 + t) + 0.5 * v * (1.0 - t * t) * root_coef * (1.0 + 3.0 * cubic_coef * v * v)


def row_norm(v):
    return jnp.sqrt(jnp.sum(v * v, axis=-1, keepdims=True) + norm_eps)


(TEXT, TEXT2, META, RS1, RS1B, RS1X, AG1C, RS2C, RS2Z, TG, TG2, LOSS1, LOSSC, LOSSZ, AG2, AG2X, RS3, RS3X, ARC_I, ARC_O, ARS_I, ARS_O,
 AAG_I, AAG_O, AFC_I, AFC_O, AG1Z, RS1L) = range(28)
FLOW = 16
UP, DOWN = 0, 1
FAR_FIRST = (5, 4, 7, 3, 6, 2, 1)
SLOTS = ((0, UP), (4, UP), (3, UP), (3, DOWN), (2, UP), (2, DOWN), (1, UP), (1, DOWN))


def slot_at(way, far):
    return 0 if far == 0 else 1 if far == 4 else 8 - 2 * far + way


def rows_at(start, count, step):
    return pl.ds(pl.multiple_of(start, step), count)


def kernel(
    x_hbm, t_hbm, wi_hbm, wo_hbm, ib_hbm, tb_hbm, pos_hbm, tab_hbm,
    loss_ref, gt_ref, gi_ref, gwi_ref, gwo_ref,
    x_ref, t_ref, wi_ref, wo_ref, ib_ref, tb_ref, pos_ref, tab_ref,
    xt, hp, act, part, rs1s, rs1r, rs1bs, rs1br, rs1ls, rs1lr, rs1xs, rs1xr, txt, meta, meta_s, meta_r, hot, img, coef, loss_acc, c_send, c_recv, ig, held, rs2s, rs2r, tgs, tgr, tgo, tgs2, tgr2,
    l_tile, l1r, lc_tile, lcr, lz_tile, lzr, gfall, gh, swi, swo, rs3s, rs3r, rs3xs, rs3xr,
    arc_si, arc_so, arc_ri, arc_ro, awi, awo, ars_si, ars_so, ars_ri, ars_ro, fwi, fwo,
    lsem, ssem, rsem, csem, rs1sem, ag1sem, rs2sem, ag2sem, rs3sem, rs1bsem, ag2bsem, aagsem,
):
    dp, mp = lax.axis_index("dp"), lax.axis_index("mp")
    core, y, xl = lax.rem(dp, 2), lax.rem(dp // 2, 4), dp // 8
    xh, z = lax.rem(mp, 2), mp // 2
    x = xh * 2 + xl
    partner = (dp + 1 - 2 * core, mp)

    across = (dp, mp + 1 - 2 * xh)

    def z_peer(j):
        return (dp, lax.rem(z + j, 8) * 2 + xh)

    def plane_dev(x2, y2):
        return ((lax.rem(x2, 2) * 4 + y2) * 2 + core, z * 2 + x2 // 2)

    def ar_peer(j):
        xl2, y2 = lax.rem(xl + lax.rem(j, 2), 2), lax.rem(y + j // 2, 4)
        return ((xl2 * 4 + y2) * 2 + core, mp), y2 * 2 + xl2

    def plane_peer(j):
        return plane_dev(lax.rem(x + lax.rem(j, 4), 4), lax.rem(y + j // 4, 4))

    def copy(src, dst, phase, device, recv=None):
        return pltpu.make_async_remote_copy(
            src_ref=src, dst_ref=dst, send_sem=ssem.at[phase],
            recv_sem=rsem.at[phase] if recv is None else recv, device_id=device, device_id_type=MESH,
        )

    def got(ref, phase):
        copy(ref, ref, phase, partner).wait_recv()

    def sent(ref, phase):
        copy(ref, ref, phase, partner).wait_send()

    def hops(f, way):
        return 4 if f % 2 == way else 3

    def neighbour(way, distance=1):
        return z_peer(distance if way == UP else 8 - distance)

    def toward(way, far):
        return lax.rem(z + (far if way == UP else 8 - far), 8)

    barrier = pltpu.get_barrier_semaphore()

    def greet(j, _):
        pl.semaphore_signal(barrier, inc=1, device_id=plane_peer(j), device_id_type=MESH)
        return 0

    lax.fori_loop(1, 16, greet, 0)

    def greet_z(j, _):
        pl.semaphore_signal(barrier, inc=1, device_id=z_peer(j), device_id_type=MESH)
        return 0

    lax.fori_loop(1, 8, greet_z, 0)
    pl.semaphore_signal(barrier, inc=1, device_id=partner, device_id_type=MESH)

    loads = [
        pltpu.make_async_copy(src, dst, lsem.at[i])
        for i, (src, dst) in enumerate(
            (
                (t_hbm, t_ref), (tb_hbm, tb_ref), (pos_hbm, pos_ref), (ib_hbm, ib_ref), (tab_hbm, tab_ref),
                (wi_hbm, wi_ref), (wo_hbm, wo_ref),
            )
        )
    ]
    for load in loads:
        load.start()
    for far, way in SLOTS:
        for other in (0, 1):
            from_rows = rows_at((toward(way, far) * 2 + (1 - xh if other else xh)) * OWN, OWN, OWN)
            to_rows = pl.ds(slot_at(way, far) * 64 + other * OWN, OWN)
            pltpu.make_async_copy(x_hbm.at[from_rows], x_ref.at[to_rows], lsem.at[7]).start()
    for load in loads[:5]:
        load.wait()

    own_slot = y * 4 + x
    own_text = rows_at(own_slot * OWN, OWN, OWN)
    wide = t_ref[...].astype(F32)
    txt[own_text, :D] = (wide / row_norm(wide)).astype(BF16)
    eye = lax.broadcasted_iota(jnp.int32, (OWN, OWN), 0) == lax.broadcasted_iota(jnp.int32, (OWN, OWN), 1)
    tb_col = jnp.sum(jnp.where(eye, tb_ref[...].astype(F32), 0.0), axis=1, keepdims=True)
    lane = lax.broadcasted_iota(jnp.int32, (OWN, ext), 1)
    level = jnp.where(lane < 24, lax.rem(lane, 8), -1).astype(F32)
    txt[own_text, D:] = jnp.where(level == tb_col, 1.0, 0.0).astype(BF16)

    pl.semaphore_wait(barrier, 23)

    def send_text_y(slot_x, j):
        rows = rows_at((y * 4 + slot_x) * OWN, OWN, OWN)
        copy(txt.at[rows], txt.at[rows], TEXT2, plane_dev(x, lax.rem(y + j, 4))).start()

    def send_own_y(j, _):
        send_text_y(x, j)
        return 0

    lax.fori_loop(1, 4, send_own_y, 0)

    def text_on():
        got(txt.at[pl.ds(0, 3 * OWN)], TEXT)

        def send(i, _):
            send_text_y(lax.rem(x + 1 + i // 3, 4), 1 + lax.rem(i, 3))
            return 0

        lax.fori_loop(0, 9, send, 0)

    def slot_of(f, way, far, flows):
        return pl.ds(((way * flows + f) * 4 + far - 1) * FLOW, FLOW)

    def sem_of(sems, f, way, far, flows):
        return sems.at[(way * flows + f) * 4 + far - 1]

    def last_of(f, way, last):
        return pl.ds((way + 2 * last[3].index(f)) * FLOW, FLOW)

    def reduce_step(far, which, flows, row_of, held, sbuf, rbuf, phase, sems, last):
        for f in which:
            for way in (UP, DOWN):
                if far > hops(f, way):
                    continue
                value = held[pl.ds(row_of(f, slot_at(way, far)), FLOW), :]
                for beyond in {1: (2,), 2: (3, 4)}.get(far, ()):
                    if beyond <= hops(f, way):
                        before = slot_of(f, way, beyond, flows)
                        copy(rbuf.at[before], rbuf.at[before], phase, partner, sem_of(sems, f, way, beyond, flows)).wait_recv()
                        value = value + rbuf[before, :].astype(F32)
                sem = sem_of(sems, f, way, far, flows)
                if f in last[3] and far == 1:
                    sbuf1, rbuf1, phase1, _ = last
                    slot = last_of(f, way, last)
                    sbuf1[slot, :] = value
                    copy(sbuf1.at[slot], rbuf1.at[slot], phase1, neighbour(way), sem).start()
                else:
                    slot = slot_of(f, way, far, flows)
                    sbuf[slot, :] = value.astype(BF16)
                    copy(sbuf.at[slot], rbuf.at[slot], phase, neighbour(way, 2 if far == 4 else 1), sem).start()

    def reduce_end(f, flows, row_of, held, rbuf, phase, sems, last):
        value = held[pl.ds(row_of(f, 0), FLOW), :]
        for way in (UP, DOWN):
            slot = slot_of(f, way, 1, flows)
            if f in last[3]:
                rbuf, phase, slot = last[1], last[2], last_of(f, way, last)
            copy(rbuf.at[slot], rbuf.at[slot], phase, partner, sem_of(sems, f, way, 1, flows)).wait_recv()
            value = value + rbuf[slot, :].astype(F32)
        return value

    def gather_step(far, which, flows, row_of, buf, phase, sems):
        for f in which:
            for way in (UP, DOWN):
                if far > hops(f, way):
                    continue
                rows = pl.ds(row_of(f, slot_at(1 - way, far)), FLOW)
                if far > 0:
                    copy(buf.at[rows], buf.at[rows], phase, partner, sem_of(sems, f, way, far, flows)).wait_recv()
                for distance in {0: (1,), 1: (1,), 2: (1, 2)}.get(far, ()):
                    if far + distance <= hops(f, way):
                        onto = pl.ds(row_of(f, slot_at(1 - way, far + distance)), FLOW)
                        sem = sem_of(sems, f, way, far + distance, flows)
                        copy(buf.at[rows], buf.at[onto], phase, neighbour(way, distance), sem).start()

    def mp_row(f, slot):
        return slot * 64 + (OWN, 0, FLOW, OWN + FLOW)[f]

    def reduce_mp(held, sbuf, rbuf, bs, br, xs, xr, last, phases, sems, bsems):
        ring_phase, b_phase, x_phase = phases

        def send_across(slots):
            for slot in slots:
                rows = pl.ds(slot * FLOW, FLOW)
                bs[rows, :] = held[slot * 64 + 48 : slot * 64 + 64, :].astype(BF16)
                copy(bs.at[rows], br.at[rows], b_phase, across, bsems.at[slot]).start()

        def ring(far):
            reduce_step(far, (0, 1), 3, mp_row, held, sbuf, rbuf, ring_phase, sems, last)

        def met(slots):
            for slot in slots:
                rows = pl.ds(slot * FLOW, FLOW)
                copy(br.at[rows], br.at[rows], b_phase, partner, bsems.at[slot]).wait_recv()
                held[slot * 64 + FLOW : slot * 64 + 2 * FLOW, :] += br[rows, :].astype(F32)

        def cross(far):
            met((1,) if far == 4 else (slot_at(UP, far), slot_at(DOWN, far)))
            reduce_step(far, (2,), 3, mp_row, held, sbuf, rbuf, ring_phase, sems, last)

        def end_across():
            xs[...] = reduce_end(0, 3, mp_row, held, rbuf, ring_phase, sems, last)
            copy(xs, xr, x_phase, across).start()
            met((0,))

        def end():
            near = reduce_end(1, 3, mp_row, held, rbuf, ring_phase, sems, last)
            mixed = reduce_end(2, 3, mp_row, held, rbuf, ring_phase, sems, last)
            got(xr, x_phase)
            return jnp.concatenate([near + xr[...], mixed], axis=0)

        return send_across, ring, cross, end_across, end

    for load in loads[5:]:
        load.wait()

    pltpu.make_async_copy(x_ref, x_ref, lsem.at[7]).wait()

    def forward(g):
        rows = pl.ds(g * 128, 128)
        pre = dot(x_ref[rows, :], wi_ref[...])
        hp[rows, :] = pre
        a = gelu_tanh(pre).astype(BF16)
        act[rows, :] = a
        part[rows, :] = dot(a, wo_ref[...])

    rs1_across, rs1_ring, rs1_cross, rs1_end_across, rs1_end = reduce_mp(
        part, rs1s, rs1r, rs1bs, rs1br, rs1xs, rs1xr, (rs1ls, rs1lr, RS1L, (2,)), (RS1, RS1B, RS1X), rs1sem, rs1bsem
    )
    forward(0)
    rs1_across((1, 0))
    def send_text(j, _):
        device = plane_dev(lax.rem(x + j, 4), y)
        copy(txt.at[own_text], txt.at[own_text], TEXT, device).start()
        return 0

    lax.fori_loop(1, 4, send_text, 0)
    rs1_ring(4)
    forward(1)
    rs1_across((2, 3))
    rs1_ring(3)
    forward(2)
    rs1_across((4, 5))
    rs1_cross(4)
    text_on()
    rs1_ring(2)
    forward(3)
    rs1_across((6, 7))
    rs1_cross(3)
    rs1_ring(1)
    for g in range(4):
        xt[:, g * 128 : g * 128 + 128] = x_ref[g * 128 : g * 128 + 128, :].T
    pos = pos_ref[...]
    pos_hi = pos // 64
    line = lax.broadcasted_iota(jnp.int32, (8, ROWS), 0)
    table_rows = jnp.where(
        line == 0, pos_hi, jnp.where(line == 1, pos - pos_hi * 64, jnp.where(line == 2, ib_ref[...], 0))
    ).astype(F32).astype(BF16)
    took = lax.broadcasted_iota(jnp.int32, (ROWS, ROWS), 0)
    into = lax.broadcasted_iota(jnp.int32, (ROWS, ROWS), 1)
    slot = into // 64
    distance = jnp.where(lax.rem(slot, 2) == 0, 4 - slot // 2, slot // 2 + 4)
    distance = jnp.where(slot == 0, 0, jnp.where(slot == 1, 4, distance))
    right = took == (lax.rem(z + distance, 8) * 2 + xh) * OWN + lax.rem(into, OWN)
    first = lax.rem(into, 64) < OWN
    meta[...] = dot(table_rows, jnp.where(right & first, 1.0, 0.0).astype(BF16))
    meta_s[...] = dot(table_rows, jnp.where(right & jnp.logical_not(first), 1.0, 0.0).astype(BF16))

    copy(meta_s, meta_r, META, partner).start()
    rs1_cross(2)
    rs1_end_across()
    rs1_cross(1)
    features = rs1_end() + x_ref[:OWN, :].astype(F32)
    norm = row_norm(features)
    unit = features / norm

    img[:OWN, :] = unit.astype(BF16)
    def send_img(from_row, to_row, count, sem, distance):
        copy(
            img.at[pl.ds(from_row, count)], img.at[pl.ds(to_row, count)], AG1Z, z_peer(distance % 8), ag1sem.at[sem]
        ).start()

    def got_img(count, sem):
        copy(img.at[pl.ds(0, count)], img.at[pl.ds(0, count)], AG1Z, partner, ag1sem.at[sem]).wait_recv()

    for way, sign in ((UP, 1), (DOWN, -1)):
        send_img(0, slot_at(1 - way, 2) * 64, OWN, way, 2 * sign)
    for way, sign in ((UP, 1), (DOWN, -1)):
        send_img(0, slot_at(1 - way, 1) * 64, OWN, 2 + way, sign)

    def to_partner(slot):
        copy(
            img.at[pl.ds(slot * 64, OWN)], img.at[pl.ds(slot * 64 + OWN, OWN)], AG1C, partner, csem.at[slot // 2 + (4 if slot == 1 else 0)]
        ).start()

    def from_partner(far):
        count = OWN if far in (0, 4) else 2 * OWN
        copy(
            img.at[pl.ds(0, count)], img.at[pl.ds(0, count)], AG1C, partner, csem.at[0 if far == 0 else 4 - far if far < 4 else 4]
        ).wait_recv()

    to_partner(0)

    got(meta_r, META)
    meta[...] += meta_r[...]

    eye8 = lax.broadcasted_iota(jnp.int32, (8, 8), 0) == lax.broadcasted_iota(jnp.int32, (8, 8), 1)

    buckets = meta[2:3, :]
    weights = jnp.zeros((8, ROWS), F32)
    for k in range(8):
        column = jnp.sum(jnp.where(eye8, tab_ref[k : k + 1, :], 0.0), axis=1, keepdims=True)
        weights = weights + jnp.where(buckets == float(k), column, 0.0)
    hi = weights.astype(BF16).astype(F32)
    mid = (weights - hi).astype(BF16).astype(F32)
    low = weights - hi - mid
    hot[...] = jnp.concatenate([hi, mid, low, jnp.zeros((ext - 24, ROWS), F32)], axis=0).astype(BF16)
    meta[0:1, :] = meta[0:1, :] * 64.0 + meta[1:2, :]

    loss_acc[...] = jnp.zeros_like(loss_acc)

    def pairs(g):
        images = pl.ds(g * 128, 128)

        logits = logit_scale * dot_nt(txt[:, :D], img[images, :]) + logit_bias
        weight = dot(txt[:, D:], hot[:, images])
        slot = lax.broadcasted_iota(jnp.int32, (ROWS, 1), 0)
        p = slot // OWN
        px, py = lax.rem(p, 4), p // 4
        index = (((lax.rem(px, 2) * 4 + py) * 2 + core) * 16 + z * 2 + px // 2) * OWN + lax.rem(slot, OWN)
        hit = index.astype(F32) == meta[0:1, images]
        against = jnp.where(hit, -logits, logits)
        grown = jnp.exp(against)
        loss_acc[...] += jnp.sum((weight * jnp.log(1.0 + grown)).reshape(ROWS // 8, 8, 128), axis=0)
        slope = logit_scale * weight * (grown / (1.0 + grown))
        coef[:, images] = jnp.where(hit, -slope, slope).astype(BF16)

    def image_grad(g):
        rows = pl.ds(g * 128, 128)
        ig[rows, :] = dot_tn(coef[:, rows], txt[:, :D])
        to = pl.ds(g * 64, 64)
        for slot in (2 * g, 2 * g + 1):
            c_send[slot * OWN : slot * OWN + OWN, :] = ig[slot * 64 + OWN : slot * 64 + 64, :]
        copy(c_send.at[to], c_recv.at[to], RS2C, partner, csem.at[5 + g]).start()

    def both_cores(g):
        to = pl.ds(g * 64, 64)
        copy(c_send.at[to], c_recv.at[to], RS2C, partner, csem.at[5 + g]).wait_recv()
        for slot in (2 * g, 2 * g + 1):
            rows = pl.ds(slot * OWN, OWN)
            held[rows, :] = ig[slot * 64 : slot * 64 + OWN, :] + c_recv[rows, :]

    for way in (UP, DOWN):
        got_img(OWN, 2 + way)
        to_partner(slot_at(1 - way, 1))
    for way, sign in ((UP, 1), (DOWN, -1)):
        got_img(OWN, way)
        row = slot_at(1 - way, 2) * 64
        send_img(row, slot_at(1 - way, 3) * 64, OWN, 4 + way, sign)
        send_img(row + FLOW * way, 64 + FLOW * way, FLOW, 6 + way, 2 * sign)
    for way in (UP, DOWN):
        to_partner(slot_at(1 - way, 2))
    got(txt.at[pl.ds(0, 3 * 128)], TEXT2)
    from_partner(1)
    pairs(3)
    for way in (UP, DOWN):
        got_img(OWN, 4 + way)
        to_partner(slot_at(1 - way, 3))
    from_partner(2)
    pairs(2)
    image_grad(3)
    for way in (UP, DOWN):
        got_img(FLOW, 6 + way)
    to_partner(1)
    from_partner(3)
    pairs(1)
    image_grad(1)
    from_partner(0)
    from_partner(4)
    pairs(0)

    def send_rs2(value, sem, distance):
        rows = pl.ds(sem * OWN, value.shape[0])
        rs2s[rows, :] = value.astype(BF16)
        copy(rs2s.at[rows], rs2r.at[rows], RS2Z, z_peer(distance % 8), rs2sem.at[sem]).start()

    def got_rs2(sem, count=OWN):
        rows = pl.ds(sem * OWN, count)
        copy(rs2r.at[rows], rs2r.at[rows], RS2Z, partner, rs2sem.at[sem]).wait_recv()
        return rs2r[rows, :].astype(F32)

    def held_at(way, far):
        row = slot_at(way, far) * OWN
        return held[row : row + OWN, :]

    image_grad(0)
    both_cores(1)
    send_rs2(held_at(UP, 3), 2, 1)
    send_rs2(held_at(DOWN, 3), 3, -1)
    both_cores(0)
    far4 = held_at(UP, 4)
    send_rs2(far4[:FLOW], 0, 2)
    send_rs2(far4[FLOW:], 1, -2)
    image_grad(2)
    both_cores(3)
    send_rs2(held_at(UP, 1), 6, 1)
    send_rs2(held_at(DOWN, 1), 7, -1)

    def text_grad(j, _):
        b = lax.rem(y + j, 4)
        rows = rows_at(b * 128, 128, 128)
        tgs[rows, :] = dot(coef[rows, :], img[...]).astype(BF16)
        copy(tgs.at[rows], tgr.at[rows_at((j - 1) * 128, 128, 128)], TG, plane_dev(x, b)).start()
        return 0

    lax.fori_loop(1, 3, text_grad, 0)
    both_cores(2)
    far2 = held_at(UP, 2) + got_rs2(2)
    send_rs2(jnp.concatenate([far2[:FLOW] + got_rs2(0, FLOW), far2[FLOW:]], axis=0), 4, 2)
    far2 = held_at(DOWN, 2) + got_rs2(3)
    send_rs2(jnp.concatenate([far2[:FLOW], far2[FLOW:] + got_rs2(1, FLOW)], axis=0), 5, -2)
    text_grad(3, 0)
    tgo[...] = dot(coef[rows_at(y * 128, 128, 128), :], img[...])

    def text_grad_on():
        got(tgr, TG)
        tgo[...] += tgr[0:128, :].astype(F32) + tgr[128:256, :].astype(F32) + tgr[256:384, :].astype(F32)

        def send(j, _):
            x2 = lax.rem(x + j, 4)
            rows = rows_at(x2 * OWN, OWN, OWN)
            tgs2[rows, :] = tgo[rows, :].astype(BF16)
            copy(tgs2.at[rows], tgr2.at[rows_at((j - 1) * OWN, OWN, OWN)], TG2, plane_dev(x2, y)).start()
            return 0

        lax.fori_loop(1, 4, send, 0)

    l_tile[...] = jnp.zeros((8, 128), F32) + jnp.sum(loss_acc[...])

    def send_loss(j, _):
        copy(l_tile, l1r.at[rows_at((j - 1) * 8, 8, 8)], LOSS1, plane_peer(j)).start()
        return 0

    lax.fori_loop(1, 16, send_loss, 0)

    own_grad = held[0:OWN, :] + got_rs2(6) + got_rs2(7) + got_rs2(4) + got_rs2(5)
    projected = jnp.sum(unit * own_grad, axis=-1, keepdims=True)
    grad_features = (own_grad - unit * projected) / norm
    gfall[:OWN, :] = grad_features.astype(BF16)
    def cross_gf(slot):
        copy(
            gfall.at[pl.ds(slot * 64 + FLOW, FLOW)], gfall.at[pl.ds(slot * 64 + 48, FLOW)], AG2X, across, ag2bsem.at[slot]
        ).start()

    def crossed_gf(slots):
        for slot in slots:
            rows = pl.ds(slot * 64 + 48, FLOW)
            copy(gfall.at[rows], gfall.at[rows], AG2X, partner, ag2bsem.at[slot]).wait_recv()

    def ag2_step(far, which):
        gather_step(far, which, 3, mp_row, gfall, AG2, ag2sem)

    def near_step(far):
        ag2_step(far, (2, 1))
        for slot in (1,) if far == 4 else (slot_at(UP, far), slot_at(DOWN, far)):
            cross_gf(slot)

    other_rows = pl.ds(OWN, FLOW)
    copy(gfall.at[pl.ds(0, FLOW)], gfall.at[other_rows], AG2X, across).start()
    ag2_step(0, (2, 1))
    cross_gf(0)
    near_step(1)
    got(gfall.at[other_rows], AG2X)
    ag2_step(0, (0,))
    near_step(2)

    def backward(g):
        rows = pl.ds(g * 128, 128)
        gh[rows, :] = (dot_nt(gfall[rows, :], wo_ref[...]) * gelu_slope(hp[rows, :])).astype(BF16)

    def to_input(g):
        rows = pl.ds(g * 128, 128)
        part[rows, :] = dot_nt(gh[rows, :], wi_ref[...])

    rs3_last = (None, None, None, ())

    def rs3_ring(far):
        reduce_step(far, (0, 3, 1, 2), 4, mp_row, part, rs3s, rs3r, RS3, rs3sem, rs3_last)

    def rs3_end(flows):
        return jnp.concatenate([reduce_end(f, 4, mp_row, part, rs3r, RS3, rs3sem, rs3_last) for f in flows], axis=0)

    other_cols, own_cols = rows_at((1 - core) * 128, 128, 128), rows_at(core * 128, 128, 128)
    late, early = pl.ds(0, 256), pl.ds(256, 256)

    def w_in_half(cols, out, kind):
        out[...] = (swi[:, cols] + dot(xt[:, late], gh[late, cols])).astype(kind)

    ag2_step(1, (0,))
    crossed_gf((6, 7))
    backward(3)
    near_step(3)
    ag2_step(2, (0,))
    crossed_gf((4, 5))
    backward(2)
    swo[...] = dot_tn(act[early, :], gfall[early, :])
    near_step(4)
    ag2_step(3, (0,))
    swi[...] = dot(xt[:, early], gh[early, :])
    crossed_gf((2, 3))
    backward(1)
    to_input(2)
    to_input(3)
    to_input(1)
    ag2_step(4, (0,))
    crossed_gf((0, 1))
    arc_so[...] = (swo[other_cols, :] + dot_tn(act[late, other_cols], gfall[late, :])).astype(BF16)
    copy(arc_so, arc_ro, ARC_O, partner).start()
    backward(0)
    w_in_half(other_cols, arc_si, BF16)
    copy(arc_si, arc_ri, ARC_I, partner).start()
    awo[...] = swo[own_cols, :] + dot_tn(act[late, own_cols], gfall[late, :])
    got(arc_ro, ARC_O)
    awo[...] += arc_ro[...].astype(F32)
    ars_so[...] = awo[...].astype(BF16)

    def send_ars_out(j, _):
        device, q = ar_peer(j)
        copy(ars_so.at[rows_at(q * 16, 16, 16)], ars_ro.at[rows_at((j - 1) * 16, 16, 16)], ARS_O, device).start()
        return 0

    for peer in FAR_FIRST:
        send_ars_out(peer, 0)
    to_input(0)
    rs3_ring(4)
    rs3_ring(3)
    w_in_half(own_cols, awi, F32)
    got(arc_ri, ARC_I)
    awi[...] += arc_ri[...].astype(F32)
    ars_si[...] = awi[...].astype(BF16)

    def send_ars_in(j, _):
        device, q = ar_peer(j)
        copy(ars_si.at[rows_at(q * 144, 144, 144)], ars_ri.at[rows_at((j - 1) * 144, 144, 144)], ARS_I, device).start()
        return 0

    for peer in FAR_FIRST:
        send_ars_in(peer, 0)
    text_grad_on()
    rs3_ring(2)
    got(l1r, LOSS1)
    loss = l_tile[...]
    for j in range(15):
        loss = loss + l1r[j * 8 : j * 8 + 8, :]
    lc_tile[...] = loss
    copy(lc_tile, lcr, LOSSC, partner).start()

    rs3_ring(1)

    q = y * 2 + xl
    own_in, own_out = rows_at(q * 144, 144, 144), rows_at(q * 16, 16, 16)
    total_in, total_out = awi[own_in, :], awo[own_out, :]
    got(ars_ro, ARS_O)
    for j in range(7):
        total_out = total_out + ars_ro[j * 16 : j * 16 + 16, :].astype(F32)
    fwo[core, own_out, :] = total_out.astype(BF16)

    def send_aag_out(j, _):
        device, _ = ar_peer(j)
        copy(fwo.at[core, own_out], fwo.at[core, own_out], AAG_O, device, aagsem.at[7 + j]).start()
        return 0

    for peer in FAR_FIRST:
        send_aag_out(peer, 0)
    copy(fwo.at[core, own_out], fwo.at[core, own_out], AFC_O, partner).start()
    got(ars_ri, ARS_I)
    for j in range(7):
        total_in = total_in + ars_ri[j * 144 : j * 144 + 144, :].astype(F32)
    fwi[core, own_in, :] = total_in.astype(BF16)

    def send_aag_in(j, _):
        device, _ = ar_peer(j)
        copy(fwi.at[core, own_in], fwi.at[core, own_in], AAG_I, device, aagsem.at[j - 1]).start()
        return 0

    for peer in FAR_FIRST:
        send_aag_in(peer, 0)
    copy(fwi.at[core, own_in], fwi.at[core, own_in], AFC_I, partner).start()
    got(lcr, LOSSC)
    lz_tile[...] = loss + lcr[...]

    def send_loss_z(j, _):
        copy(lz_tile, lzr.at[rows_at((j - 1) * 8, 8, 8)], LOSSZ, z_peer(j)).start()
        return 0

    lax.fori_loop(1, 8, send_loss_z, 0)
    rs3xs[...] = rs3_end((0, 3))
    copy(rs3xs, rs3xr, RS3X, across).start()
    grad_image = rs3_end((1, 2)) + grad_features

    def weights_on(j, _):
        xl2, y2 = lax.rem(xl + lax.rem(j, 2), 2), lax.rem(y + 4 - j // 2, 4)
        q2 = y2 * 2 + xl2
        out, into = rows_at(q2 * 16, 16, 16), rows_at(q2 * 144, 144, 144)
        copy(fwo.at[core, out], fwo.at[core, out], AAG_O, partner, aagsem.at[7 + j]).wait_recv()
        copy(fwo.at[core, out], fwo.at[core, out], AFC_O, partner).start()
        copy(fwi.at[core, into], fwi.at[core, into], AAG_I, partner, aagsem.at[j - 1]).wait_recv()
        copy(fwi.at[core, into], fwi.at[core, into], AFC_I, partner).start()
        return 0

    for peer in FAR_FIRST:
        weights_on(peer, 0)
    got(tgr2, TG2)
    grad_text = tgo[rows_at(x * OWN, OWN, OWN), :]
    for j in range(3):
        grad_text = grad_text + tgr2[j * OWN : j * OWN + OWN, :].astype(F32)
    gt_ref[...] = grad_text
    got(lzr, LOSSZ)
    loss = lz_tile[...]
    for j in range(7):
        loss = loss + lzr[j * 8 : j * 8 + 8, :]
    loss_ref[...] = loss * (1.0 / PAIRS)

    sent(txt.at[pl.ds(0, 3 * OWN)], TEXT)
    sent(txt.at[pl.ds(0, 3 * 128)], TEXT2)
    sent(meta_s, META)
    sent(rs1s.at[pl.ds(0, 19 * FLOW)], RS1)
    sent(rs1bs, RS1B)
    sent(rs1ls, RS1L)
    sent(rs1xs, RS1X)
    sent(img.at[pl.ds(0, 14 * FLOW)], AG1Z)
    sent(img.at[pl.ds(0, 8 * OWN)], AG1C)
    sent(c_send, RS2C)
    sent(rs2s.at[pl.ds(0, 14 * FLOW)], RS2Z)
    sent(tgr, TG)
    sent(l1r, LOSS1)
    sent(lc_tile, LOSSC)
    sent(gfall.at[pl.ds(0, 21 * FLOW)], AG2)
    sent(gfall.at[pl.ds(0, 9 * FLOW)], AG2X)
    sent(arc_si, ARC_I)
    sent(arc_so, ARC_O)
    got(rs3xr, RS3X)
    gi_ref[...] = grad_image + rs3xr[...]
    got(fwo.at[1 - core], AFC_O)
    for half in range(2):
        gwo_ref[half * 128 : half * 128 + 128, :] = fwo[half]
    got(fwi.at[1 - core], AFC_I)
    for half in range(2):
        gwi_ref[:, half * 128 : half * 128 + 128] = fwi[half]

    sent(tgr2, TG2)
    sent(lzr, LOSSZ)
    sent(rs3s.at[pl.ds(0, 28 * FLOW)], RS3)
    sent(rs3xs, RS3X)
    sent(ars_ri, ARS_I)
    sent(ars_ro, ARS_O)
    sent(fwi.at[0, pl.ds(0, 7 * 144)], AAG_I)
    sent(fwo.at[0, pl.ds(0, 7 * 16)], AAG_O)
    sent(fwi.at[0], AFC_I)
    sent(fwo.at[0], AFC_O)


def widen(loss_in, gt_in, gi_in, gwi_in, gwo_in, loss_ref, gt_ref, gi_ref, gwi_ref, gwo_ref):
    loss_ref[0, 0] = jnp.max(loss_in[...])
    gt_ref[...] = gt_in[...]
    gi_ref[...] = gi_in[...]
    gwi_ref[...] = gwi_in[...].astype(F32)
    gwo_ref[...] = gwo_in[...].astype(F32)


def per_device(
    image_feats, text_feats, w_in, w_out, image_bucket, text_bucket, positive, reward_table
):
    vmem = pl.BlockSpec(memory_space=pltpu.VMEM)

    def buf(shape, kind=BF16):
        return pltpu.VMEM(shape, kind)

    scratch = [
        buf((ROWS, D)),
        buf((OWN, D)),
        buf((D, HID)),
        buf((HID, D)),
        buf((1, ROWS), jnp.int32),
        buf((1, OWN), jnp.int32),
        buf((1, ROWS), jnp.int32),
        buf((8, 8), F32),
        buf((D, ROWS)),
        buf((ROWS, HID), F32),
        buf((ROWS, HID)),
        buf((ROWS, D), F32),
        buf((ROWS, D)),
        buf((ROWS, D)),
        buf((8 * FLOW, D)),
        buf((8 * FLOW, D)),
        buf((2 * FLOW, D), F32),
        buf((2 * FLOW, D), F32),
        buf((FLOW, D), F32),
        buf((FLOW, D), F32),
        buf((ROWS, D + ext)),
        buf((8, ROWS), F32),
        buf((8, ROWS), F32),
        buf((8, ROWS), F32),
        buf((ext, ROWS)),
        buf((ROWS, D)),
        buf((ROWS, ROWS)),
        buf((8, 128), F32),
        buf((256, D), F32),
        buf((256, D), F32),
        buf((ROWS, D), F32),
        buf((256, D), F32),
        buf((256, D)),
        buf((256, D)),
        buf((ROWS, D)),
        buf((3 * 128, D)),
        buf((128, D), F32),
        buf((128, D)),
        buf((3 * OWN, D)),
        buf((8, 128), F32),
        buf((15 * 8, 128), F32),
        buf((8, 128), F32),
        buf((8, 128), F32),
        buf((8, 128), F32),
        buf((7 * 8, 128), F32),
        buf((ROWS, D)),
        buf((ROWS, HID)),
        buf((D, HID), F32),
        buf((HID, D), F32),
        buf((ROWS, D)),
        buf((ROWS, D)),
        buf((OWN, D), F32),
        buf((OWN, D), F32),
        buf((D, 128)),
        buf((128, D)),
        buf((D, 128)),
        buf((128, D)),
        buf((D, 128), F32),
        buf((128, D), F32),
        buf((D, 128)),
        buf((128, D)),
        buf((7 * 144, 128)),
        buf((7 * 16, D)),
        buf((2, D, 128)),
        buf((2, 128, D)),
        pltpu.SemaphoreType.DMA((8,)),
        pltpu.SemaphoreType.DMA((28,)),
        pltpu.SemaphoreType.DMA((28,)),
        pltpu.SemaphoreType.DMA((9,)),
        pltpu.SemaphoreType.DMA((24,)),
        pltpu.SemaphoreType.DMA((8,)),
        pltpu.SemaphoreType.DMA((8,)),
        pltpu.SemaphoreType.DMA((24,)),
        pltpu.SemaphoreType.DMA((32,)),
        pltpu.SemaphoreType.DMA((8,)),
        pltpu.SemaphoreType.DMA((8,)),
        pltpu.SemaphoreType.DMA((15,)),
    ]
    partial = pl.pallas_call(
        kernel,
        out_shape=(
            jax.ShapeDtypeStruct((8, 128), F32),
            jax.ShapeDtypeStruct((OWN, D), F32),
            jax.ShapeDtypeStruct((OWN, D), F32),
            jax.ShapeDtypeStruct((D, HID), BF16),
            jax.ShapeDtypeStruct((HID, D), BF16),
        ),
        in_specs=[pl.BlockSpec(memory_space=pltpu.HBM)] * 8,
        out_specs=(vmem,) * 5,
        scratch_shapes=scratch,
        compiler_params=pltpu.CompilerParams(
            collective_id=0, has_side_effects=True, vmem_limit_bytes=VMEM_LIMIT
        ),
        name="pairs_and_block",
    )(
        image_feats, text_feats, w_in, w_out, image_bucket[None, :], text_bucket[None, :], positive[None, :],
        reward_table,
    )
    loss, grad_text, grad_image, grad_w_in, grad_w_out = pl.pallas_call(
        widen,
        out_shape=(
            jax.ShapeDtypeStruct((1, 1), F32),
            jax.ShapeDtypeStruct((OWN, D), F32),
            jax.ShapeDtypeStruct((OWN, D), F32),
            jax.ShapeDtypeStruct((D, HID), F32),
            jax.ShapeDtypeStruct((HID, D), F32),
        ),
        in_specs=[vmem] * 5,
        out_specs=(pl.BlockSpec(memory_space=pltpu.SMEM),) + (vmem,) * 4,
        compiler_params=pltpu.CompilerParams(vmem_limit_bytes=VMEM_LIMIT),
        name="widen",
    )(*partial)
    return (loss.reshape(()), grad_text, grad_image, grad_w_in, grad_w_out)


def solution(mesh):
    return jax.shard_map(
        per_device,
        mesh=mesh,
        in_specs=(
            P("dp", None),
            P(("dp", "mp"), None),
            P(None, "mp"),
            P("mp", None),
            P("dp"),
            P(("dp", "mp")),
            P("dp"),
            P(),
        ),
        out_specs=(P(), P(("dp", "mp"), None), P(("dp", "mp"), None), P(None, "mp"), P("mp", None)),
        check_vma=False,
    )
```
